256 devices in a mesh: item: 8 (over y, x_hi), user: 32 (over x_lo, z, core).
Axes of the slice: x: 4 (x_hi: 2, x_lo: 2; x = x_hi * 2 + x_lo), y: 4, z: 8, core: 2. Of those that a mesh axis runs over, the one named last changes fastest.
Arguments:
- user_vecs: bfloat16 [8192, 128], P('user'), may hold values from -15 to 15
- row_weight: bfloat16 [8192], P('user'), may hold values from 0.25 to 4
- positive: int32 [8192], P('user'), may hold values from 0 to 131071
- item_feats: bfloat16 [131072, 128], P(('item', 'user')), may hold values from -6 to 6
- valid: int32 [131072], P(('item', 'user')), may hold values from 0 to 1, as said below
- w_in: bfloat16 [128, 1024], replicated, may hold values from -0.5 to 0.5
- w_out: bfloat16 [1024, 128], replicated, may hold values from -0.1875 to 0.1875
Outputs:
- grad_user: float32 [8192, 128], P('user')
- grad_item: float32 [131072, 128], P(('item', 'user'))
- grad_w_in: float32 [128, 1024], replicated
- grad_w_out: float32 [1024, 128], replicated
The draws below stay inside these ranges and needn't reach their ends.
Inputs may be any that keep to these rules, and one draw needn't show every extreme that they name: `valid`: each aligned block of 16384 items has its own rate of ones, between a quarter and all.
All inputs are finite; a program needn't handle non-finite values.
Results may differ from the reference program's by a relative error of at most 0.012.
The reference program's roundings to bfloat16 on the way (of `hidden`, `item_vec`, `grad_scores`, `grad_vec` and `grad_pre`) count: a program that leaves them out, or rounds other values in their place, can miss the bound.
Values may be sent and summed in bfloat16 or wider, within the bound.
A program may use at most 128 MiB of HBM per device.

```python
import math
import jax
import jax.numpy as jnp
from jax import lax

EMB = 128
HID = 1024
UROWS = 8192
SHARD_ITEMS = 16384
ITEMS = 131072


def item_base(key, twin_share):
    key = jax.random.fold_in(key, 7)
    base = jax.random.normal(key, (ITEMS, EMB), jnp.float32)
    twin_rows = (jnp.arange(ITEMS, dtype=jnp.int32) % 16 == 1).astype(jnp.float32) * twin_share
    base = base * (1.0 - twin_rows[:, None])
    return jnp.clip(base, -6.0, 6.0)


def draw_item_feats(key, part):
    base = item_base(key, 0.0)
    return base.astype(jnp.bfloat16)


def draw_user_vecs(key, part):
    key = jax.random.fold_in(key, 3)
    users = jnp.clip(0.15 * jax.random.normal(key, (UROWS, EMB), jnp.float32), -1.0, 1.0)
    return users.astype(jnp.bfloat16)


def draw_valid(key, part):
    key = jax.random.fold_in(key, 5)
    shard_count = ITEMS // SHARD_ITEMS
    order = jax.random.permutation(jax.random.fold_in(key, 1), shard_count)
    rates = 25 + 75 * order // max(shard_count - 1, 1)
    shard_of = jnp.arange(ITEMS, dtype=jnp.int32) // SHARD_ITEMS
    rolls = jax.random.randint(key, (ITEMS,), 0, 100)
    return (rolls < rates[shard_of]).astype(jnp.int32)


def set_ends(values, own_key, low, high):
    extent = values.shape
    index_at = [jax.random.randint(jax.random.fold_in(own_key, axis), (), 0, extent[axis]) for axis in range(len(extent))]
    values = values.at[tuple(index_at)].set(low)
    longest = extent.index(max(extent))
    index_at[longest] = (index_at[longest] + 1) % extent[longest]
    return values.at[tuple(index_at)].set(high)


def shard_levels(stream_key, extent, pieces, least, high):
    def one(dim, shards_of):
        heights = jax.random.uniform(jax.random.fold_in(jax.random.fold_in(stream_key, 6), dim), (shards_of,), jnp.float32, least / len(pieces), high / len(pieces))
        return jnp.repeat(jnp.exp(heights), extent[dim] // shards_of).reshape((-1,) + (1,) * (len(extent) - dim - 1))

    loudness = one(*pieces[0])
    for cut in pieces[1:]:
        loudness = loudness * one(*cut)
    return loudness


def scatter_about(rng, extent, spread, reach, kind=jnp.bfloat16):
    return jnp.clip(spread * jax.random.normal(rng, extent, jnp.float32), -reach, reach).astype(kind)


def setup_inputs(seed: int = 0) -> dict:
    splits = jax.random.split(jax.random.key(seed), 8)
    return {
        "user_vecs": draw_user_vecs(jax.random.fold_in(splits[7], 71), 0),
        "row_weight": jnp.clip(jnp.exp(math.log(4.0) - 2.7725887 * jax.random.uniform(splits[1], (UROWS,), jnp.float32) ** shard_levels(splits[1], (UROWS,), ((0, 32),), -0.2, 0.2)), 0.25, 4.0).astype(jnp.bfloat16),
        "positive": set_ends(jax.random.randint(splits[2], (UROWS,), 0, ITEMS), jax.random.fold_in(splits[2], 1), 0, ITEMS - 1).astype(jnp.int32),
        "item_feats": draw_item_feats(jax.random.fold_in(splits[7], 71), 0),
        "valid": draw_valid(jax.random.fold_in(splits[7], 71), 0),
        "w_in": scatter_about(splits[5], (EMB, HID), EMB ** -0.5, 0.5),
        "w_out": scatter_about(splits[6], (HID, EMB), HID ** -0.5, 0.1875),
    }


neg_floor = -1e30


def tower(item_feats, w_in, w_out):
    pre_act = jnp.dot(item_feats, w_in, preferred_element_type=jnp.float32)
    hidden = jax.nn.silu(pre_act).astype(jnp.bfloat16)
    item_vec = (item_feats.astype(jnp.float32) + jnp.dot(hidden, w_out, preferred_element_type=jnp.float32)).astype(jnp.bfloat16)
    return pre_act, hidden, item_vec


def reference(user_vecs, row_weight, positive, item_feats, valid, w_in, w_out):
    pre_act, hidden, item_vec = tower(item_feats, w_in, w_out)
    item_ids = jnp.arange(ITEMS, dtype=jnp.int32)
    valid_mask = valid == 1
    block_size = min(512, UROWS)
    block_count = UROWS // block_size
    user_blocks = user_vecs.reshape(block_count, block_size, EMB)
    weight_blocks = row_weight.reshape(block_count, block_size)
    pos_blocks = positive.reshape(block_count, block_size)

    def step(accum, blk):
        users, weights, pos = blk
        scores = jnp.dot(users, item_vec.T, preferred_element_type=jnp.float32)
        is_positive = item_ids[None, :] == pos[:, None]
        live_mask = valid_mask[None, :] | is_positive
        row_peak = jnp.max(jnp.where(live_mask, scores, neg_floor), axis=1)
        expo = jnp.where(live_mask, jnp.exp(scores - row_peak[:, None]), 0.0)
        row_total = jnp.sum(expo, axis=1)
        grad_scores = (weights.astype(jnp.float32)[:, None] * (expo / row_total[:, None] - is_positive.astype(jnp.float32))).astype(jnp.bfloat16)
        accum = accum + jnp.dot(grad_scores.T, users, preferred_element_type=jnp.float32)
        return accum, jnp.dot(grad_scores, item_vec, preferred_element_type=jnp.float32)

    item_grad, user_grad = lax.scan(step, jnp.zeros((ITEMS, EMB), jnp.float32), (user_blocks, weight_blocks, pos_blocks))
    grad_user = user_grad.reshape(UROWS, EMB)
    grad_vec = item_grad.astype(jnp.bfloat16)
    grad_w_out = jnp.dot(hidden.T, grad_vec, preferred_element_type=jnp.float32)
    back_hidden = jnp.dot(grad_vec, w_out.T, preferred_element_type=jnp.float32)
    sigma = jax.nn.sigmoid(pre_act)
    grad_pre = (back_hidden * (sigma * (1.0 + pre_act * (1.0 - sigma)))).astype(jnp.bfloat16)
    grad_w_in = jnp.dot(item_feats.T, grad_pre, preferred_element_type=jnp.float32)
    grad_item = grad_vec.astype(jnp.float32) + jnp.dot(grad_pre, w_in.T, preferred_element_type=jnp.float32)
    return grad_user, grad_item, grad_w_in, grad_w_out
```

```python
import functools

import jax
import jax.numpy as jnp
from jax import lax
from jax.experimental import pallas as pl
from jax.experimental.pallas import tpu as pltpu
from jax.sharding import PartitionSpec as P

MESH = pl.DeviceIdType.MESH
F32 = jnp.float32
BF16 = jnp.bfloat16
DEAD = -1e30
FLOOR = -1e29


def dot(a, b):
    return jnp.dot(a, b, preferred_element_type=F32)


def dot_t(a, b):
    return lax.dot_general(a, b, (((1,), (1,)), ((), ())), preferred_element_type=F32)


class Dims:
    def __init__(self, phys, ub, ib, emb, hid):
        self.ny, self.nxh, self.nxl, self.nz, self.nc = phys
        self.ub, self.ib, self.emb, self.hid = ub, ib, emb, hid
        self.ng = self.ny * self.nxh
        self.np = self.ng * self.nxl
        self.nq = self.nz * self.nc
        self.nj = self.nxl * self.nc
        self.users = self.nz * ub
        self.items = self.nj * ib
        self.wrows = 2 * emb // self.np
        self.lanes = min(self.nq, hid // 128)
        self.prow = self.wrows // (self.nq // self.lanes)
        self.pcol = hid // self.lanes


def kernel(
    d,
    users_in, weight_in, pos_in, feats, valid_in, w_in, w_out,
    out_user, out_item, out_w_in, out_w_out,
    users, meta, vecs, valid, vcol, vec_t, hidden, slope, expo, grad,
    peak_s, total_s, factor, pos_s, weight_s,
    st_own, st_a, st_own2, st_b,
    gv_send, gv_recv, gv_own, gu_send, gu_recv, gu_sum, gu2_recv, gu_out,
    wg_own, wg_send, wg_recv, p2_own, p2_recv, a2, a1,
    us_s, us_r, me_s, me_r, ve_s, ve_r, va_s, va_r, sa_s, sa_r, sb_s, sb_r,
    gv_s, gv_r, gu_s, gu_r, g2_s, g2_r, g3_s, g3_r,
    w1_s, w1_r, w2_s, w2_r, w3_s, w3_r, w4_s, w4_r,
):
    ub, ib, emb, hid = d.ub, d.ib, d.emb, d.hid
    item = lax.axis_index("item")
    user = lax.axis_index("user")
    core = lax.rem(user, d.nc)
    z = lax.rem(user // d.nc, d.nz)
    xl = user // (d.nc * d.nz)
    plane = item * d.nxl + xl
    column = z * d.nc + core

    def dev(item_, xl_, z_, core_):
        return (item_, (xl_ * d.nz + z_) * d.nc + core_)

    def z_peer(k):
        return lax.rem(z + k, d.nz)

    def plane_peer(k):
        return lax.rem(plane + k, d.np)

    def plane_dev(p):
        return dev(p // d.nxl, lax.rem(p, d.nxl), z, core)

    def column_peer(k):
        return lax.rem(column + k, d.nq)

    def column_dev(q):
        return dev(item, xl, q // d.nc, lax.rem(q, d.nc))

    def group_peer(k):
        return lax.rem(item + k, d.ng)

    def block_dev(j):
        return dev(item, lax.rem(xl + j // d.nc, d.nxl), z, lax.rem(core + j % d.nc, d.nc))

    def remote(src, dst, send, recv, to):
        return pltpu.make_async_remote_copy(
            src_ref=src, dst_ref=dst, send_sem=send, recv_sem=recv, device_id=to, device_id_type=MESH
        )

    def each(n, fn):
        def step(k, carry):
            fn(k)
            return carry

        lax.fori_loop(1, n, step, 0)

    barrier = pltpu.get_barrier_semaphore()

    def greet(to):
        pl.semaphore_signal(barrier, inc=1, device_id=to, device_id_type=MESH)

    each(d.np, lambda k: greet(plane_dev(plane_peer(k))))
    each(d.nq, lambda k: greet(column_dev(column_peer(k))))
    diagonal = [j for j in range(d.nj) if j // d.nc and j % d.nc]
    for j in diagonal:
        greet(block_dev(j))

    users[z] = users_in[...]
    meta[z] = jnp.concatenate([pos_in[...].astype(F32), weight_in[...].astype(F32)], axis=0)
    valid[0] = valid_in[...].astype(F32)
    pl.semaphore_wait(barrier, d.np - 1 + d.nq - 1 + len(diagonal))

    def users_copy(k, slot):
        return remote(users.at[slot], users.at[slot], us_s.at[k], us_r.at[k], dev(item, xl, z_peer(k), core))

    def meta_copy(k, slot):
        return remote(meta.at[slot], meta.at[slot], me_s.at[k], me_r.at[k], dev(item, xl, z_peer(k), core))

    def send_users(k):
        users_copy(k, z).start()
        meta_copy(k, z).start()

    each(d.nz, send_users)

    def vecs_copy(j):
        return remote(vecs.at[0], vecs.at[j], ve_s.at[j], ve_r.at[j], block_dev(j))

    def valid_copy(j):
        return remote(valid.at[0], valid.at[j], va_s.at[j], va_r.at[j], block_dev(j))

    rt = min(128, ib)

    def tower(t, carry):
        rows = pl.ds(pl.multiple_of(t * rt, rt), rt)
        x = feats[rows, :]
        pre = dot(x, w_in[...])
        sigma = jax.nn.sigmoid(pre)
        hid_t = (pre * sigma).astype(BF16)
        hidden[rows, :] = hid_t
        slope[rows, :] = sigma * (1.0 + pre * (1.0 - sigma))
        vecs[0, rows, :] = (x.astype(F32) + dot(hid_t, w_out[...])).astype(BF16)
        return carry

    lax.fori_loop(0, ib // rt, tower, 0)
    for j in range(1, d.nj):
        vecs_copy(j).start()
        valid_copy(j).start()

    def local_pos(pos):
        block = pos // ib
        p_core = lax.rem(block, d.nc)
        p_z = lax.rem(block // d.nc, d.nz)
        p_xl = lax.rem(block // (d.nc * d.nz), d.nxl)
        p_item = block // (d.nc * d.nz * d.nxl)
        j = lax.rem(p_xl + d.nxl - xl, d.nxl) * d.nc + lax.rem(p_core + d.nc - core, d.nc)
        here = (p_item == item) & (p_z == z)
        return jnp.where(here, j * ib + lax.rem(pos, ib), -1)

    def scores(k, carry):
        slot = lax.rem(z + d.nz - k, d.nz)

        @pl.when(k > 0)
        def _():
            users_copy(k, slot).wait_recv()
            meta_copy(k, slot).wait_recv()

        pos = local_pos(meta[slot, 0:1, :].astype(jnp.int32))
        at = pl.multiple_of(slot * ub, ub)
        pos_s[:, pl.ds(at, ub)] = pos
        weight_s[:, pl.ds(at, ub)] = meta[slot, 1:2, :]
        for j in range(d.nj):

            @pl.when(k == 0)
            def _():
                if j > 0:
                    vecs_copy(j).wait_recv()
                    valid_copy(j).wait_recv()
                vcol[j] = jnp.broadcast_to(valid[j], (128, ib)).T

            s = dot_t(vecs[j], users[slot])
            for h in range(ub // 128):
                lanes = pl.ds(pl.multiple_of(at + h * 128, 128), 128)
                row = lax.broadcasted_iota(jnp.int32, (ib, 128), 0) + j * ib
                live = (vcol[j] > 0.5) | (row == pos[:, h * 128 : (h + 1) * 128])
                x = jnp.where(live, s[:, h * 128 : (h + 1) * 128], DEAD)
                peak = jnp.maximum(jnp.max(x, axis=0, keepdims=True), FLOOR)
                e = jnp.exp(x - peak)
                peak_s[j, :, lanes] = peak
                total_s[j, :, lanes] = jnp.sum(e, axis=0, keepdims=True)
                expo[pl.ds(j * ib, ib), lanes] = e
        return carry

    lax.fori_loop(0, d.nz, scores, 0)

    def merge(peaks, totals):
        peak = functools.reduce(jnp.maximum, peaks)
        total = sum(t * jnp.exp(p - peak) for p, t in zip(peaks, totals))
        return peak, total

    peak, total = merge([peak_s[j] for j in range(d.nj)], [total_s[j] for j in range(d.nj)])
    st_own[0:1, :] = peak
    st_own[1:2, :] = total

    def st_a_copy(k):
        return remote(st_own, st_a.at[k], sa_s.at[k], sa_r.at[k], dev(group_peer(k), xl, z, core))

    def st_b_copy(k):
        return remote(st_own2, st_b.at[k], sb_s.at[k], sb_r.at[k], dev(item, xl, z_peer(k), core))

    each(d.ng, lambda k: st_a_copy(k).start())
    for j in range(d.nj):
        vec_t[:, j * ib : (j + 1) * ib] = vecs[j].astype(F32).T.astype(BF16)
    each(d.ng, lambda k: st_a_copy(k).wait_recv())
    peak, total = merge(
        [st_own[0:1, :]] + [st_a[k, 0:1, :] for k in range(1, d.ng)],
        [st_own[1:2, :]] + [st_a[k, 1:2, :] for k in range(1, d.ng)],
    )
    st_own2[0:1, :] = peak
    st_own2[1:2, :] = total
    each(d.nz, lambda k: st_b_copy(k).start())
    each(d.nz, lambda k: st_b_copy(k).wait_recv())
    peak, total = merge(
        [st_own2[0:1, :]] + [st_b[k, 0:1, :] for k in range(1, d.nz)],
        [st_own2[1:2, :]] + [st_b[k, 1:2, :] for k in range(1, d.nz)],
    )
    scale = weight_s[...] / total
    for j in range(d.nj):
        factor[j] = scale * jnp.exp(peak_s[j] - peak)

    def gv_copy(j):
        return remote(gv_send.at[j], gv_recv.at[j], gv_s.at[j], gv_r.at[j], block_dev(j))

    for j in reversed(range(d.nj)):

        def grads(t, carry):
            rows = pl.ds(pl.multiple_of(j * ib + t * rt, rt), rt)
            row = lax.broadcasted_iota(jnp.int32, (rt, d.users), 0) + (j * ib + t * rt)
            hit = jnp.where(row == pos_s[...], weight_s[...], 0.0)
            g = (expo[rows, :] * factor[j] - hit).astype(BF16)
            grad[rows, :] = g
            acc = dot(g, users[...].reshape(d.users, emb))
            here = pl.ds(pl.multiple_of(t * rt, rt), rt)
            if j == 0:
                gv_own[here, :] = acc
            else:
                gv_send[j, here, :] = acc.astype(BF16)
            return carry

        lax.fori_loop(0, ib // rt, grads, 0)
        if j > 0:
            gv_copy(j).start()

    def gu_copy(k):
        return remote(gu_send.at[k], gu_recv.at[k], gu_s.at[k], gu_r.at[k], dev(item, xl, z_peer(k), core))

    def user_terms(slot):
        lanes = pl.ds(pl.multiple_of(slot * ub, ub), ub)
        return dot(vec_t[...], grad[:, lanes]).T

    def send_terms(k):
        gu_send[k] = user_terms(z_peer(k)).astype(BF16)
        gu_copy(k).start()

    each(d.nz, send_terms)
    gu_sum[...] = user_terms(z)

    gv = gv_own[...]
    for j in range(1, d.nj):
        gv_copy(j).wait_recv()
        gv = gv + gv_recv[j].astype(F32)
    gv = gv.astype(BF16)
    gv_own[...] = gv.astype(F32)
    gv_t = gv_own[...].T.astype(BF16)
    wg_own[emb:, :] = dot(gv_t, hidden[...])

    def back(t, carry):
        rows = pl.ds(pl.multiple_of(t * rt, rt), rt)
        g = gv_own[rows, :]
        pre = (dot_t(g.astype(BF16), w_out[...]) * slope[rows, :]).astype(BF16)
        hidden[rows, :] = pre
        out_item[rows, :] = g + dot_t(pre, w_in[...])
        return carry

    lax.fori_loop(0, ib // rt, back, 0)
    wg_own[:emb, :] = dot(feats[...].astype(F32).T.astype(BF16), hidden[...])
    for p in range(d.np):
        wg_send[p] = wg_own[p * d.wrows : (p + 1) * d.wrows, :].astype(BF16)

    def w1_copy(k):
        p = plane_peer(k)
        return remote(wg_send.at[p], wg_recv.at[k], w1_s.at[k], w1_r.at[k], plane_dev(p))

    each(d.np, lambda k: w1_copy(k).start())

    def gu_add(k):
        gu_copy(k).wait_recv()
        gu_sum[...] += gu_recv[k].astype(F32)

    each(d.nz, gu_add)
    us = ub // d.ng

    def g2_copy(k):
        to = group_peer(k)
        rows = pl.ds(pl.multiple_of(to * us, us), us)
        return remote(gu_sum.at[rows, :], gu2_recv.at[k], g2_s.at[k], g2_r.at[k], dev(to, xl, z, core))

    each(d.ng, lambda k: g2_copy(k).start())

    each(d.np, lambda k: w1_copy(k).wait_recv())
    part = wg_own[pl.ds(pl.multiple_of(plane * d.wrows, d.wrows), d.wrows), :]
    for k in range(1, d.np):
        part = part + wg_recv[k].astype(F32)

    def piece(q):
        r, c = (q // d.lanes) * d.prow, (q % d.lanes) * d.pcol
        return slice(r, r + d.prow), slice(c, c + d.pcol)

    for q in range(d.nq):
        r, c = piece(q)
        p2_own[q] = part[r, c]

    def w2_copy(k):
        q = column_peer(k)
        return remote(p2_own.at[q], p2_recv.at[k], w2_s.at[k], w2_r.at[k], column_dev(q))

    each(d.nq, lambda k: w2_copy(k).start())

    def g3_copy(k, slot):
        return remote(gu_out.at[slot], gu_out.at[slot], g3_s.at[k], g3_r.at[k], dev(group_peer(k), xl, z, core))

    each(d.ng, lambda k: g2_copy(k).wait_recv())
    mine = gu_sum[pl.ds(pl.multiple_of(item * us, us), us), :]
    for k in range(1, d.ng):
        mine = mine + gu2_recv[k]
    gu_out[item] = mine
    each(d.ng, lambda k: g3_copy(k, item).start())

    each(d.nq, lambda k: w2_copy(k).wait_recv())
    own = p2_own[column]
    for k in range(1, d.nq):
        own = own + p2_recv[k]
    a2[column] = own

    def w3_copy(k, slot):
        return remote(a2.at[slot], a2.at[slot], w3_s.at[k], w3_r.at[k], column_dev(column_peer(k)))

    each(d.nq, lambda k: w3_copy(k, column).start())

    def back_by(here, k, n):
        return lax.rem(here + n - k, n)

    each(d.nq, lambda k: w3_copy(k, back_by(column, k, d.nq)).wait_recv())
    rows_of = []
    for r in range(d.nq // d.lanes):
        rows_of.append(jnp.concatenate([a2[r * d.lanes + c] for c in range(d.lanes)], axis=1))
    a1[plane] = jnp.concatenate(rows_of, axis=0).astype(BF16)

    def w4_copy(k, slot):
        return remote(a1.at[slot], a1.at[slot], w4_s.at[k], w4_r.at[k], plane_dev(plane_peer(k)))

    each(d.np, lambda k: w4_copy(k, plane).start())

    each(d.ng, lambda k: g3_copy(k, back_by(item, k, d.ng)).wait_recv())
    out_user[...] = gu_out[...].reshape(ub, emb)

    each(d.np, lambda k: w4_copy(k, back_by(plane, k, d.np)).wait_recv())
    half = d.np // 2
    out_w_in[...] = a1[:half].astype(F32).reshape(emb, hid)
    out_w_out[...] = a1[half:].astype(F32).reshape(emb, hid).T

    def sent_z(k):
        users_copy(k, z).wait_send()
        meta_copy(k, z).wait_send()
        st_b_copy(k).wait_send()
        gu_copy(k).wait_send()

    def sent_group(k):
        st_a_copy(k).wait_send()
        g2_copy(k).wait_send()
        g3_copy(k, item).wait_send()

    def sent_plane(k):
        w1_copy(k).wait_send()
        w4_copy(k, plane).wait_send()

    def sent_column(k):
        w2_copy(k).wait_send()
        w3_copy(k, column).wait_send()

    each(d.nz, sent_z)
    each(d.ng, sent_group)
    each(d.np, sent_plane)
    each(d.nq, sent_column)
    for j in range(1, d.nj):
        vecs_copy(j).wait_send()
        valid_copy(j).wait_send()
        gv_copy(j).wait_send()


def body(phys, user_vecs, row_weight, positive, item_feats, valid, w_in, w_out):
    ub, emb = user_vecs.shape
    ib, hid = item_feats.shape[0], w_in.shape[1]
    d = Dims(phys, ub, ib, emb, hid)
    vm = pltpu.VMEM
    us = ub // d.ng
    scratch = [
        vm((d.nz, ub, emb), BF16),
        vm((d.nz, 2, ub), F32),
        vm((d.nj, ib, emb), BF16),
        vm((d.nj, 1, ib), F32),
        vm((d.nj, ib, 128), F32),
        vm((emb, d.items), BF16),
        vm((ib, hid), BF16),
        vm((ib, hid), F32),
        vm((d.items, d.users), F32),
        vm((d.items, d.users), BF16),
        vm((d.nj, 1, d.users), F32),
        vm((d.nj, 1, d.users), F32),
        vm((d.nj, 1, d.users), F32),
        vm((1, d.users), jnp.int32),
        vm((1, d.users), F32),
        vm((2, d.users), F32),
        vm((d.ng, 2, d.users), F32),
        vm((2, d.users), F32),
        vm((d.nz, 2, d.users), F32),
        vm((d.nj, ib, emb), BF16),
        vm((d.nj, ib, emb), BF16),
        vm((ib, emb), F32),
        vm((d.nz, ub, emb), BF16),
        vm((d.nz, ub, emb), BF16),
        vm((ub, emb), F32),
        vm((d.ng, us, emb), F32),
        vm((d.ng, us, emb), F32),
        vm((2 * emb, hid), F32),
        vm((d.np, d.wrows, hid), BF16),
        vm((d.np, d.wrows, hid), BF16),
        vm((d.nq, d.prow, d.pcol), F32),
        vm((d.nq, d.prow, d.pcol), F32),
        vm((d.nq, d.prow, d.pcol), F32),
        vm((d.np, d.wrows, hid), BF16),
    ]
    sems = []
    for n in (d.nz, d.nz, d.nj, d.nj, d.ng, d.nz, d.nj, d.nz, d.ng, d.ng, d.np, d.nq, d.nq, d.np):
        sems += [pltpu.SemaphoreType.DMA((n,)), pltpu.SemaphoreType.DMA((n,))]
    whole = pl.BlockSpec(memory_space=pltpu.VMEM)
    return pl.pallas_call(
        functools.partial(kernel, d),
        out_shape=(
            jax.ShapeDtypeStruct((ub, emb), F32),
            jax.ShapeDtypeStruct((ib, emb), F32),
            jax.ShapeDtypeStruct((emb, hid), F32),
            jax.ShapeDtypeStruct((hid, emb), F32),
        ),
        in_specs=[whole] * 7,
        out_specs=(whole,) * 4,
        scratch_shapes=scratch + sems,
        compiler_params=pltpu.CompilerParams(
            collective_id=0, has_side_effects=True, vmem_limit_bytes=56 * 1024 * 1024
        ),
        cost_estimate=pl.CostEstimate(
            flops=6 * d.users * d.items * emb,
            bytes_accessed=4 * 1024 * 1024,
            transcendentals=d.users * d.items,
        ),
    )(
        user_vecs,
        row_weight.reshape(1, ub),
        positive.reshape(1, ub),
        item_feats,
        valid.reshape(1, ib),
        w_in,
        w_out,
    )


def build(mesh, phys):
    return jax.shard_map(
        functools.partial(body, phys),
        mesh=mesh,
        in_specs=(
            P("user", None),
            P("user"),
            P("user"),
            P(("item", "user"), None),
            P(("item", "user")),
            P(),
            P(),
        ),
        out_specs=(P("user", None), P(("item", "user"), None), P(), P()),
        check_vma=False,
    )


def solution(mesh):
    return build(mesh, (4, 2, 2, 8, 2))
```

```python
import functools

import jax
import jax.numpy as jnp
from jax import lax
from jax.experimental import pallas as pl
from jax.experimental.pallas import tpu as pltpu
from jax.sharding import PartitionSpec as P

MESH = pl.DeviceIdType.MESH
F32 = jnp.float32
BF16 = jnp.bfloat16
DEAD = -1e30
FLOOR = -1e29


def dot(a, b):
    return jnp.dot(a, b, preferred_element_type=F32)


def dot_t(a, b):
    return lax.dot_general(a, b, (((1,), (1,)), ((), ())), preferred_element_type=F32)


class Dims:
    def __init__(self, phys, ub, ib, emb, hid):
        self.ny, self.nxh, self.nxl, self.nz, self.nc = phys
        self.ub, self.ib, self.emb, self.hid = ub, ib, emb, hid
        self.ng = self.ny * self.nxh
        self.np = self.ng * self.nxl
        self.nj = self.nxl * self.nc
        self.users = self.nz * ub
        self.items = self.nj * ib
        self.chunk = min(256, ib)
        self.nk = self.items // self.chunk
        self.srows = max(16, emb // self.np)
        self.scols = emb * hid // self.np // self.srows
        self.cols = hid // self.scols


def kernel(
    d,
    users_in, weight_in, pos_in, feats, valid_in, w_in, w_out,
    out_user, out_item, out_w,
    users, meta, vecs, valid, bias, vec_t, hidden, slope, expo, grad,
    peak_s, total_s, factor, tile_s, weight_s,
    st_own, st_a, st_own2, st_b,
    gv_send, gv_recv, gv_own, gu_send, gu_recv, gu_sum, gu2_recv, gu_out,
    wg_own, wc_send, wc_recv, w1_send, w1_recv, wz, a1,
    us_s, us_r, me_s, me_r, ve_s, ve_r, va_s, va_r, sa_s, sa_r, sb_s, sb_r,
    gv_s, gv_r, gu_s, gu_r, g2_s, g2_r, g3_s, g3_r,
    wc_s, wc_r, w1_s, w1_r, wz_s, wz_r, w4_s, w4_r, w5_s, w5_r,
):
    ub, ib, emb, hid = d.ub, d.ib, d.emb, d.hid
    item = lax.axis_index("item")
    user = lax.axis_index("user")
    core = lax.rem(user, d.nc)
    z = lax.rem(lax.div(user, d.nc), d.nz)
    xl = lax.div(user, d.nc * d.nz)
    plane = item * d.nxl + xl

    def dev(item_, xl_, z_, core_):
        return (item_, (xl_ * d.nz + z_) * d.nc + core_)

    def back_by(here, k, n):
        return lax.rem(here + n - k, n)

    def z_peer(k):
        return lax.rem(z + k, d.nz)

    def z_dev(k):
        return dev(item, xl, z_peer(k), core)

    def group_dev(k):
        return dev(lax.rem(item + k, d.ng), xl, z, core)

    def plane_peer(k):
        return lax.rem(plane + k, d.np)

    def plane_dev(p):
        return dev(lax.div(p, d.nxl), lax.rem(p, d.nxl), z, core)

    sibling = dev(item, xl, z, 1 - core)
    across = dev(item, 1 - xl, z, core)

    def remote(src, dst, send, recv, to):
        return pltpu.make_async_remote_copy(
            src_ref=src, dst_ref=dst, send_sem=send, recv_sem=recv, device_id=to, device_id_type=MESH
        )

    def each(n, fn):
        def step(k, carry):
            fn(k)
            return carry

        lax.fori_loop(1, n, step, 0)

    flights = {}

    def fly(name, n, copy_out, copy_in=None, start=True):
        flights[name] = [n, copy_out, copy_in or copy_out, False]
        if start:
            each(n, lambda k: copy_out(k).start())

    def land(name):
        n, _, copy_in, _ = flights[name]
        each(n, lambda k: copy_in(k).wait_recv())
        flights[name][3] = True

    def finish():
        for name, (n, copy_out, _, landed) in flights.items():
            if not landed:
                land(name)
            each(n, lambda k: copy_out(k).wait_send())

    barrier = pltpu.get_barrier_semaphore()

    def greet(to):
        pl.semaphore_signal(barrier, inc=1, device_id=to, device_id_type=MESH)

    each(d.nz, lambda k: greet(z_dev(k)))
    each(d.np, lambda k: greet(plane_dev(plane_peer(k))))
    greet(sibling)

    users[z] = users_in[...]
    pos = pos_in[...].reshape(1, ub)
    meta[z] = jnp.concatenate([pos.astype(F32), weight_in[...].reshape(1, ub).astype(F32)], axis=0)
    valid[0] = valid_in[...].reshape(1, ib).astype(F32)
    rt = min(128, ib)

    def tower(t, carry):
        rows = pl.ds(pl.multiple_of(t * rt, rt), rt)
        x = feats[rows, :]
        pre = dot(x, w_in[...])
        sigma = jax.nn.sigmoid(pre)
        hid_t = (pre * sigma).astype(BF16)
        hidden[rows, :] = hid_t
        slope[rows, :] = sigma * (1.0 + pre * (1.0 - sigma))
        vecs[0, rows, :] = (x.astype(F32) + dot(hid_t, w_out[...])).astype(BF16)
        return carry

    lax.fori_loop(0, ib // rt, tower, 0)
    pl.semaphore_wait(barrier, d.nz - 1 + d.np - 1 + 1)

    def near(step):
        half = lax.div(step + 1, 2)
        return jnp.where(lax.rem(step, 2) == 1, half, d.nz - half)

    def users_copy(k, slot):
        return remote(users.at[slot], users.at[slot], us_s.at[k], us_r.at[k], z_dev(k))

    def meta_copy(k, slot):
        return remote(meta.at[slot], meta.at[slot], me_s.at[k], me_r.at[k], z_dev(k))

    def vecs_copy(j):
        return remote(vecs.at[j // 3 * 2], vecs.at[j], ve_s.at[j], ve_r.at[j], across if j == 2 else sibling)

    def valid_copy(j):
        return remote(valid.at[j // 3 * 2], valid.at[j], va_s.at[j], va_r.at[j], across if j == 2 else sibling)

    for j in (2, 1):
        vecs_copy(j).start()
        valid_copy(j).start()
    fly("meta", d.nz, lambda k: meta_copy(near(k), z), lambda k: meta_copy(k, back_by(z, k, d.nz)))
    fly("users", d.nz, lambda k: users_copy(near(k), z), lambda k: users_copy(k, back_by(z, k, d.nz)))

    def vec_arrives(j):
        vecs_copy(j).wait_recv()
        valid_copy(j).wait_recv()

    def user_slot(step):
        return lax.rem(z + d.nz - near(step), d.nz)

    def local_tile(pos):
        block = pos // ib
        p_core = block % d.nc
        p_z = block // d.nc % d.nz
        p_xl = block // (d.nc * d.nz) % d.nxl
        p_item = block // (d.nc * d.nz * d.nxl)
        j = (p_xl + d.nxl - xl) % d.nxl * d.nc + (p_core + d.nc - core) % d.nc
        here = (p_item == item) & (p_z == z)
        row = jnp.where(here, j * ib + pos % ib, -1)
        lane = lax.broadcasted_iota(jnp.int32, (8, ub), 0)
        return jnp.where(here & (lane == row % 8), row // 8, -1)

    def set_bias(j):
        bias[j] = (jnp.broadcast_to(valid[j], (128, ib)).T - 1.0) * -DEAD

    def enter(step, slot):
        @pl.when(step > 0)
        def _():
            k = near(step)
            users_copy(k, slot).wait_recv()
            meta_copy(k, slot).wait_recv()

        lanes = pl.ds(pl.multiple_of(slot * ub, ub), ub)
        tile_s[:, lanes] = local_tile(meta[slot, 0:1, :].astype(jnp.int32))
        weight_s[:, lanes] = meta[slot, 1:2, :]

    def score(j, slot):
        at = pl.multiple_of(slot * ub, ub)
        for c in range(ib // d.chunk):
            rows = slice(c * d.chunk, (c + 1) * d.chunk)
            s = dot_t(vecs[j, rows, :], users[slot])
            b = bias[j, rows, :].reshape(d.chunk // 8, 8, 128)
            first = j * ib + c * d.chunk
            tile = lax.broadcasted_iota(jnp.int32, (d.chunk // 8, 8, 128), 0) + first // 8
            for h in range(ub // 128):
                lanes = pl.ds(pl.multiple_of(at + h * 128, 128), 128)
                sh = s[:, h * 128 : (h + 1) * 128].reshape(d.chunk // 8, 8, 128)
                x = jnp.where(tile == tile_s[:, lanes][None], sh, sh + b)
                peak = jnp.maximum(jnp.max(x, axis=0), FLOOR)
                e = jnp.exp(x - peak[None])
                ck = first // d.chunk
                peak_s[ck, :, lanes] = peak
                total_s[ck, :, lanes] = jnp.sum(e, axis=0)
                expo[pl.ds(first, d.chunk), lanes] = e.reshape(d.chunk, 128)

    def score_steps(lo, hi, blocks, arrive):
        def step(i, carry):
            slot = jnp.where(i == 0, z, user_slot(i))
            if arrive:
                enter(i, slot)
            for j in blocks:
                score(j, slot)
            return carry

        lax.fori_loop(lo, hi, step, 0)

    early = min(3, d.nz)
    set_bias(0)
    vec_arrives(1)
    set_bias(1)
    score_steps(0, early, (0, 1), True)
    vec_arrives(2)
    vecs_copy(3).start()
    valid_copy(3).start()
    set_bias(2)
    score_steps(0, early, (2,), False)
    vec_arrives(3)
    set_bias(3)
    fly("vecs", d.nj, None, start=False)
    flights.pop("vecs")
    score_steps(0, early, (3,), False)
    score_steps(early, d.nz, (0, 1, 2, 3), True)
    for name in ("users", "meta"):
        flights[name][3] = True

    def merge(peaks, totals):
        peak = functools.reduce(jnp.maximum, peaks)
        total = sum(t * jnp.exp(p - peak) for p, t in zip(peaks, totals))
        return peak, total

    peak8 = functools.reduce(jnp.maximum, [peak_s[c] for c in range(d.nk)])
    peak = jnp.max(peak8, axis=0, keepdims=True)
    total8 = sum(total_s[c] * jnp.exp(peak_s[c] - peak) for c in range(d.nk))
    st_own[0:1, :] = peak
    st_own[1:2, :] = jnp.sum(total8, axis=0, keepdims=True)

    def st_a_copy(k):
        return remote(st_own, st_a.at[k], sa_s.at[k], sa_r.at[k], group_dev(k))

    def st_b_copy(k):
        return remote(st_own2, st_b.at[k], sb_s.at[k], sb_r.at[k], z_dev(k))

    fly("st_a", d.ng, st_a_copy)
    for j in range(d.nj):
        vec_t[:, j * ib : (j + 1) * ib] = vecs[j].astype(F32).T.astype(BF16)
    land("st_a")
    peak, total = merge(
        [st_own[0:1, :]] + [st_a[k, 0:1, :] for k in range(1, d.ng)],
        [st_own[1:2, :]] + [st_a[k, 1:2, :] for k in range(1, d.ng)],
    )
    st_own2[0:1, :] = peak
    st_own2[1:2, :] = total
    fly("st_b", d.nz, st_b_copy)
    land("st_b")
    peak, total = merge(
        [st_own2[0:1, :]] + [st_b[k, 0:1, :] for k in range(1, d.nz)],
        [st_own2[1:2, :]] + [st_b[k, 1:2, :] for k in range(1, d.nz)],
    )
    scale = weight_s[...] / total
    for c in range(d.nk):
        factor[c] = scale * jnp.exp(peak_s[c] - peak)

    def grads(j):
        acc = jnp.zeros((ib, emb), F32)
        width = min(512, d.users)
        tile = lax.broadcasted_iota(jnp.int32, (ib // 8, 8, width), 0) + j * ib // 8
        per = ib // d.chunk
        for u in range(0, d.users, width):
            lanes = slice(u, u + width)
            e = expo[j * ib : (j + 1) * ib, lanes].reshape(per, d.chunk // 8, 8, width)
            e = (e * factor[j * per : (j + 1) * per, :, lanes][:, None]).reshape(ib // 8, 8, width)
            hit = tile == tile_s[:, lanes][None]
            g = jnp.where(hit, e - weight_s[:, lanes][None], e).reshape(ib, width).astype(BF16)
            grad[j * ib : (j + 1) * ib, lanes] = g
            acc = acc + dot(g, users[...].reshape(d.users, emb)[lanes, :])
        return acc

    def gv_copy(j):
        return remote(gv_send.at[j], gv_recv.at[j], gv_s.at[j], gv_r.at[j], across if j == 2 else sibling)

    gv_send[3] = grads(3).astype(BF16)
    gv_copy(3).start()
    acc = grads(2)
    gv_copy(3).wait_recv()
    gv_send[2] = (acc + gv_recv[3].astype(F32)).astype(BF16)
    gv_copy(2).start()
    gv_send[1] = grads(1).astype(BF16)
    gv_copy(1).start()
    gv_own[...] = grads(0)

    def gu_copy(k):
        return remote(gu_send.at[k], gu_recv.at[k], gu_s.at[k], gu_r.at[k], z_dev(k))

    def user_terms(slot):
        lanes = pl.ds(pl.multiple_of(slot * ub, ub), ub)
        return dot(vec_t[...], grad[:, lanes]).T

    def send_terms(step):
        k = near(d.nz - step)
        gu_send[k] = user_terms(z_peer(k)).astype(BF16)
        gu_copy(k).start()

    fly("gu", d.nz, gu_copy, start=False)
    each(d.nz, send_terms)
    gu_sum[...] = user_terms(z)

    for j in (1, 2):
        gv_copy(j).wait_recv()
    gv = gv_own[...] + gv_recv[1].astype(F32) + gv_recv[2].astype(F32)
    gv = gv.astype(BF16)
    gv_own[...] = gv.astype(F32)
    gv_t = gv_own[...].T.astype(BF16)
    wg_own[1] = dot(gv_t, hidden[...])

    def back(t, carry):
        rows = pl.ds(pl.multiple_of(t * rt, rt), rt)
        g = gv_own[rows, :]
        pre = (dot_t(g.astype(BF16), w_out[...]) * slope[rows, :]).astype(BF16)
        hidden[rows, :] = pre
        out_item[rows, :] = g + dot_t(pre, w_in[...])
        return carry

    lax.fori_loop(0, ib // rt, back, 0)
    wg_own[0] = dot(feats[...].astype(F32).T.astype(BF16), hidden[...])

    wc_send[...] = wg_own[1 - core].astype(BF16)
    wc_copy = remote(wc_send, wc_recv, wc_s, wc_r, sibling)
    wc_copy.start()
    wc_copy.wait_recv()
    wg_own[core] += wc_recv[...].astype(F32)
    sr, sc = d.srows, d.scols
    for p in range(d.np):
        r, c = p // d.cols * sr, p % d.cols * sc
        w1_send[p] = wg_own[core, r : r + sr, c : c + sc].astype(BF16)

    def w1_copy(k):
        p = plane_peer(k)
        return remote(w1_send.at[p], w1_recv.at[k], w1_s.at[k], w1_r.at[k], plane_dev(p))

    fly("w1", d.np, w1_copy)
    land("w1")
    part = w1_send[plane].astype(F32)
    for k in range(1, d.np):
        part = part + w1_recv[k].astype(F32)
    wz[z] = part.astype(BF16)

    def wz_copy(k, slot):
        return remote(wz.at[slot], wz.at[slot], wz_s.at[k], wz_r.at[k], z_dev(k))

    fly("wz", d.nz, lambda k: wz_copy(k, z), lambda k: wz_copy(k, back_by(z, k, d.nz)))

    land("gu")

    def gu_add(k):
        gu_sum[...] += gu_recv[k].astype(F32)

    each(d.nz, gu_add)
    us = ub // d.ng

    def g2_copy(k):
        to = lax.rem(item + k, d.ng)
        rows = pl.ds(pl.multiple_of(to * us, us), us)
        return remote(gu_sum.at[rows, :], gu2_recv.at[k], g2_s.at[k], g2_r.at[k], dev(to, xl, z, core))

    fly("g2", d.ng, g2_copy)
    land("wz")
    whole = sum(wz[k].astype(F32) for k in range(d.nz))
    a1[core, plane] = whole.astype(BF16)

    def w4_copy(k, slot):
        there = a1.at[core, slot]
        return remote(there, there, w4_s.at[k], w4_r.at[k], plane_dev(plane_peer(k)))

    def w5_copy(k, slot, of):
        there = a1.at[of, slot]
        return remote(there, there, w5_s.at[k], w5_r.at[k], sibling)

    fly("w4", d.np, lambda k: w4_copy(k, plane), lambda k: w4_copy(k, back_by(plane, k, d.np)))
    w5_copy(0, plane, core).start()

    land("g2")
    mine = gu_sum[pl.ds(pl.multiple_of(item * us, us), us), :]
    for k in range(1, d.ng):
        mine = mine + gu2_recv[k]
    gu_out[item] = mine

    def g3_copy(k, slot):
        return remote(gu_out.at[slot], gu_out.at[slot], g3_s.at[k], g3_r.at[k], group_dev(k))

    fly("g3", d.ng, lambda k: g3_copy(k, item), lambda k: g3_copy(k, back_by(item, k, d.ng)))

    def hand_on(k):
        slot = back_by(plane, k, d.np)
        w4_copy(k, slot).wait_recv()
        w5_copy(k, slot, core).start()

    each(d.np, hand_on)
    flights["w4"][3] = True
    land("g3")
    out_user[...] = gu_out[...].reshape(ub, emb)
    w5_copy(0, plane, 1 - core).wait_recv()
    each(d.np, lambda k: w5_copy(k, back_by(plane, k, d.np), 1 - core).wait_recv())
    out_w[...] = a1[...]

    finish()
    for j in (1, 2, 3):
        vecs_copy(j).wait_send()
        valid_copy(j).wait_send()
        gv_copy(j).wait_send()
    wc_copy.wait_send()
    w5_copy(0, plane, core).wait_send()
    each(d.np, lambda k: w5_copy(k, back_by(plane, k, d.np), core).wait_send())


def unpack(d, user_ref, item_ref, w_ref, out_user, out_item, out_w_in, out_w_out):
    out_user[...] = user_ref[...]
    out_item[...] = item_ref[...]
    for p in range(d.np):
        r, c = p // d.cols * d.srows, p % d.cols * d.scols
        out_w_in[r : r + d.srows, c : c + d.scols] = w_ref[0, p].astype(F32)
    for c in range(d.cols):
        block = jnp.concatenate([w_ref[1, p].astype(F32) for p in range(c, d.np, d.cols)], axis=0)
        out_w_out[c * d.scols : (c + 1) * d.scols, :] = block.T


def body(phys, user_vecs, row_weight, positive, item_feats, valid, w_in, w_out):
    ub, emb = user_vecs.shape
    ib, hid = item_feats.shape[0], w_in.shape[1]
    d = Dims(phys, ub, ib, emb, hid)
    vm = pltpu.VMEM
    us = ub // d.ng
    scratch = [
        vm((d.nz, ub, emb), BF16),
        vm((d.nz, 2, ub), F32),
        vm((d.nj, ib, emb), BF16),
        vm((d.nj, 1, ib), F32),
        vm((d.nj, ib, 128), F32),
        vm((emb, d.items), BF16),
        vm((ib, hid), BF16),
        vm((ib, hid), F32),
        vm((d.items, d.users), F32),
        vm((d.items, d.users), BF16),
        vm((d.nk, 8, d.users), F32),
        vm((d.nk, 8, d.users), F32),
        vm((d.nk, 8, d.users), F32),
        vm((8, d.users), jnp.int32),
        vm((1, d.users), F32),
        vm((2, d.users), F32),
        vm((d.ng, 2, d.users), F32),
        vm((2, d.users), F32),
        vm((d.nz, 2, d.users), F32),
        vm((d.nj, ib, emb), BF16),
        vm((d.nj, ib, emb), BF16),
        vm((ib, emb), F32),
        vm((d.nz, ub, emb), BF16),
        vm((d.nz, ub, emb), BF16),
        vm((ub, emb), F32),
        vm((d.ng, us, emb), F32),
        vm((d.ng, us, emb), F32),
        vm((2, emb, hid), F32),
        vm((emb, hid), BF16),
        vm((emb, hid), BF16),
        vm((d.np, d.srows, d.scols), BF16),
        vm((d.np, d.srows, d.scols), BF16),
        vm((d.nz, d.srows, d.scols), BF16),
        vm((2, d.np, d.srows, d.scols), BF16),
    ]
    dma = pltpu.SemaphoreType.DMA
    sems = []
    for n in (d.nz, d.nz, d.nj, d.nj, d.ng, d.nz, d.nj, d.nz, d.ng, d.ng, None, d.np, d.nz, d.np, d.np):
        sems += [dma, dma] if n is None else [dma((n,)), dma((n,))]
    whole = pl.BlockSpec(memory_space=pltpu.VMEM)
    parts = pl.pallas_call(
        functools.partial(kernel, d),
        out_shape=(
            jax.ShapeDtypeStruct((ub, emb), F32),
            jax.ShapeDtypeStruct((ib, emb), F32),
            jax.ShapeDtypeStruct((2, d.np, d.srows, d.scols), BF16),
        ),
        in_specs=[whole] * 7,
        out_specs=(whole,) * 3,
        scratch_shapes=scratch + sems,
        compiler_params=pltpu.CompilerParams(
            collective_id=0, has_side_effects=True, vmem_limit_bytes=56 * 1024 * 1024
        ),
        cost_estimate=pl.CostEstimate(
            flops=6 * d.users * d.items * emb,
            bytes_accessed=4 * 1024 * 1024,
            transcendentals=d.users * d.items,
        ),
    )(user_vecs, row_weight, positive, item_feats, valid, w_in, w_out)
    return pl.pallas_call(
        functools.partial(unpack, d),
        out_shape=(
            jax.ShapeDtypeStruct((ub, emb), F32),
            jax.ShapeDtypeStruct((ib, emb), F32),
            jax.ShapeDtypeStruct((emb, hid), F32),
            jax.ShapeDtypeStruct((hid, emb), F32),
        ),
        in_specs=[whole] * 3,
        out_specs=(whole,) * 4,
    )(*parts)


def build(mesh, phys):
    return jax.shard_map(
        functools.partial(body, phys),
        mesh=mesh,
        in_specs=(
            P("user", None),
            P("user"),
            P("user"),
            P(("item", "user"), None),
            P(("item", "user")),
            P(),
            P(),
        ),
        out_specs=(P("user", None), P(("item", "user"), None), P(), P()),
        check_vma=False,
    )


def solution(mesh):
    return build(mesh, (4, 2, 2, 8, 2))
```

```python
import functools

import jax
import jax.numpy as jnp
from jax import lax
from jax.experimental import pallas as pl
from jax.experimental.pallas import tpu as pltpu
from jax.sharding import PartitionSpec as P

MESH = pl.DeviceIdType.MESH
F32 = jnp.float32
BF16 = jnp.bfloat16
DEAD = -1e30
FLOOR = -1e29


def dot(a, b):
    return jnp.dot(a, b, preferred_element_type=F32)


def dot_t(a, b):
    return lax.dot_general(a, b, (((1,), (1,)), ((), ())), preferred_element_type=F32)


class Dims:
    def __init__(self, phys, ub, ib, emb, hid):
        self.ny, self.nxh, self.nxl, self.nz, self.nc = phys
        self.ub, self.ib, self.emb, self.hid = ub, ib, emb, hid
        self.ng = self.ny * self.nxh
        self.np = self.ng * self.nxl
        self.nj = self.nxl * self.nc
        self.users = self.nz * ub
        self.items = self.nj * ib
        self.chunk = min(256, ib)
        self.nk = self.items // self.chunk
        self.srows = 2 * emb // self.np
        self.scols = hid // 2


def kernel(
    d,
    users_in, weight_in, pos_in, feats, valid_in, w_in, w_out,
    out_user, out_item, out_w,
    users, meta, vecs, valid, bias, vec_t, hidden, slope, expo, grad,
    peak_s, total_s, factor, tile_s, weight_s,
    st_own, st_a, st_own2, st_b,
    gv_send, gv_recv, gv_own, gu_send, gu_recv, gu_sum, gu2_recv, gu_out,
    wg_own, wc_send, wc_recv, w1_send, w1_recv, wz, a1,
    us_s, us_r, me_s, me_r, ve_s, ve_r, va_s, va_r, sa_s, sa_r, sb_s, sb_r,
    gv_s, gv_r, gu_s, gu_r, g2_s, g2_r, g3_s, g3_r,
    wc_s, wc_r, w1_s, w1_r, wz_s, wz_r, w4_s, w4_r, w5_s, w5_r,
):
    ub, ib, emb, hid = d.ub, d.ib, d.emb, d.hid
    item = lax.axis_index("item")
    user = lax.axis_index("user")
    core = lax.rem(user, d.nc)
    z = lax.rem(lax.div(user, d.nc), d.nz)
    xl = lax.div(user, d.nc * d.nz)
    plane = item * d.nxl + xl

    def dev(item_, xl_, z_, core_):
        return (item_, (xl_ * d.nz + z_) * d.nc + core_)

    def back_by(here, k, n):
        return lax.rem(here + n - k, n)

    def z_peer(k):
        return lax.rem(z + k, d.nz)

    def z_dev(k):
        return dev(item, xl, z_peer(k), core)

    def group_dev(k):
        return dev(lax.rem(item + k, d.ng), xl, z, core)

    def plane_peer(k):
        return lax.rem(plane + k, d.np)

    def plane_dev(p):
        return dev(lax.div(p, d.nxl), lax.rem(p, d.nxl), z, core)

    sibling = dev(item, xl, z, 1 - core)
    across = dev(item, 1 - xl, z, core)

    def remote(src, dst, send, recv, to):
        return pltpu.make_async_remote_copy(
            src_ref=src, dst_ref=dst, send_sem=send, recv_sem=recv, device_id=to, device_id_type=MESH
        )

    def each(n, fn):
        def step(k, carry):
            fn(k)
            return carry

        lax.fori_loop(1, n, step, 0)

    flights = {}

    def fly(name, n, copy_out, copy_in=None, start=True):
        flights[name] = [n, copy_out, copy_in or copy_out, False]
        if start:
            each(n, lambda k: copy_out(k).start())

    def land(name):
        n, _, copy_in, _ = flights[name]
        each(n, lambda k: copy_in(k).wait_recv())
        flights[name][3] = True

    tails = []
    singles = {}

    def launch(name, make):
        singles[name] = [make, False]
        make().start()

    def arrive(name):
        singles[name][0]().wait_recv()
        singles[name][1] = True

    def finish():
        for wait in tails:
            wait()
        for make, landed in singles.values():
            if not landed:
                make().wait_recv()
            make().wait_send()
        for name, (n, copy_out, _, landed) in flights.items():
            if not landed:
                land(name)
            each(n, lambda k: copy_out(k).wait_send())

    barrier = pltpu.get_barrier_semaphore()

    def greet(to):
        pl.semaphore_signal(barrier, inc=1, device_id=to, device_id_type=MESH)

    each(d.nz, lambda k: greet(z_dev(k)))
    each(d.np, lambda k: greet(plane_dev(plane_peer(k))))
    greet(sibling)

    users[z] = users_in[...]
    pos = pos_in[...].reshape(1, ub)
    meta[z] = jnp.concatenate([pos.astype(F32), weight_in[...].reshape(1, ub).astype(F32)], axis=0)
    valid[0] = valid_in[...].reshape(1, ib).astype(F32)
    rt = min(128, ib)

    def tower(t, carry):
        rows = pl.ds(pl.multiple_of(t * rt, rt), rt)
        x = feats[rows, :]
        pre = dot(x, w_in[...])
        sigma = jax.nn.sigmoid(pre)
        hid_t = (pre * sigma).astype(BF16)
        hidden[rows, :] = hid_t
        slope[rows, :] = sigma * (1.0 + pre * (1.0 - sigma))
        vecs[0, rows, :] = (x.astype(F32) + dot(hid_t, w_out[...])).astype(BF16)
        return carry

    lax.fori_loop(0, ib // rt, tower, 0)
    pl.semaphore_wait(barrier, d.nz - 1 + d.np - 1 + 1)

    def near(step):
        half = lax.div(step + 1, 2)
        return jnp.where(lax.rem(step, 2) == 1, half, d.nz - half)

    far = d.nz // 2

    def users_copies(k, slot, to):
        there = z_dev(to)
        return [
            remote(users.at[slot], users.at[slot], us_s.at[k], us_r.at[k], there),
            remote(meta.at[slot], meta.at[slot], me_s.at[k], me_r.at[k], there),
        ]

    def users_start(k, slot, to):
        for copy in users_copies(k, slot, to):
            copy.start()

    def users_sent():
        for k in range(1, d.nz):
            for copy in users_copies(k, z, 1):
                copy.wait_send()

    def users_arrive(k, slot):
        for copy in users_copies(k, slot, 1):
            copy.wait_recv()

    direct = [k for k in (1, d.nz - 1, 2, d.nz - 2) if 0 < k < d.nz]
    direct = sorted(set(direct), key=direct.index)
    handed = [k for k in range(1, d.nz) if k not in direct]

    def hand_on_users():
        for k in handed:
            if k < far:
                users_start(k, back_by(z, 2, d.nz), 1)
            elif k > far:
                users_start(k, back_by(z, d.nz - 2, d.nz), d.nz - 1)
            else:
                behind = jnp.where(core == 0, 2, d.nz - 2)
                users_start(k, back_by(z, behind, d.nz), behind)

    def vecs_copy(j):
        return remote(vecs.at[j // 3 * 2], vecs.at[j], ve_s.at[j], ve_r.at[j], across if j == 2 else sibling)

    def valid_copy(j):
        return remote(valid.at[j // 3 * 2], valid.at[j], va_s.at[j], va_r.at[j], across if j == 2 else sibling)

    for j in (2, 1):
        launch(f"vecs{j}", functools.partial(vecs_copy, j))
        launch(f"valid{j}", functools.partial(valid_copy, j))
    for k in direct:
        users_start(k, z, k)
    tails.append(users_sent)

    def vec_arrives(j):
        arrive(f"vecs{j}")
        arrive(f"valid{j}")

    def user_slot(step):
        return lax.rem(z + d.nz - near(step), d.nz)

    def local_tile(pos):
        block = pos // ib
        p_core = block % d.nc
        p_z = block // d.nc % d.nz
        p_xl = block // (d.nc * d.nz) % d.nxl
        p_item = block // (d.nc * d.nz * d.nxl)
        j = (p_xl + d.nxl - xl) % d.nxl * d.nc + (p_core + d.nc - core) % d.nc
        here = (p_item == item) & (p_z == z)
        row = jnp.where(here, j * ib + pos % ib, -1)
        lane = lax.broadcasted_iota(jnp.int32, (8, ub), 0)
        return jnp.where(here & (lane == row % 8), row // 8, -1)

    def set_bias(j):
        bias[j] = (jnp.broadcast_to(valid[j], (128, ib)).T - 1.0) * -DEAD

    def enter(step, slot):
        lanes = pl.ds(pl.multiple_of(slot * ub, ub), ub)
        tile_s[:, lanes] = local_tile(meta[slot, 0:1, :].astype(jnp.int32))
        weight_s[:, lanes] = meta[slot, 1:2, :]

    def score(j, slot):
        at = pl.multiple_of(slot * ub, ub)
        tile = lax.broadcasted_iota(jnp.int32, (d.chunk // 8, 8, 128), 0)
        for c in range(ib // d.chunk):
            rows = slice(c * d.chunk, (c + 1) * d.chunk)
            s = dot_t(vecs[j, rows, :], users[slot])
            b = bias[j, rows, :].reshape(d.chunk // 8, 8, 128)
            ck = j * (ib // d.chunk) + c
            first = pl.multiple_of(ck * d.chunk, d.chunk)
            for h in range(ub // 128):
                lanes = pl.ds(pl.multiple_of(at + h * 128, 128), 128)
                sh = s[:, h * 128 : (h + 1) * 128].reshape(d.chunk // 8, 8, 128)
                hit = tile == (tile_s[:, lanes] - ck * (d.chunk // 8))[None]
                x = jnp.where(hit, sh, sh + b)
                peak = jnp.maximum(jnp.max(x, axis=0), FLOOR)
                e = jnp.exp(x - peak[None])
                peak_s[ck, :, lanes] = peak
                total_s[ck, :, lanes] = jnp.sum(e, axis=0)
                expo[pl.ds(first, d.chunk), lanes] = e.reshape(d.chunk, 128)

    first = min(5, d.nz)
    turn = min(3, first)

    def early_steps(i, carry):
        pair = lax.div(i, first)
        step = lax.rem(i, first)
        slot = jnp.where(step == 0, z, user_slot(step))

        @pl.when(i == 0)
        def _():
            vec_arrives(1)
            set_bias(0)
            set_bias(1)

        @pl.when(i == turn)
        def _():
            for k in direct:
                if k not in (1, d.nz - 1):
                    users_arrive(k, back_by(z, k, d.nz))
            hand_on_users()
            vec_arrives(2)
            launch("vecs3", functools.partial(vecs_copy, 3))
            launch("valid3", functools.partial(valid_copy, 3))

        @pl.when(i == first)
        def _():
            vec_arrives(3)
            set_bias(2)
            set_bias(3)

        for k in (1, d.nz - 1)[: d.nz - 1]:

            @pl.when(i == (1 if k == 1 else 2))
            def _():
                users_arrive(k, back_by(z, k, d.nz))

        @pl.when(pair == 0)
        def _():
            enter(step, slot)

        score(pair * 2, slot)
        score(pair * 2 + 1, slot)
        return carry

    lax.fori_loop(0, 2 * first, early_steps, 0)

    def late_steps(step, carry):
        k = near(step)
        slot = user_slot(step)
        users_arrive(k, slot)
        enter(step, slot)
        for j in range(d.nj):
            score(j, slot)
        return carry

    lax.fori_loop(first, d.nz, late_steps, 0)

    def merge(logs):
        peak = functools.reduce(jnp.maximum, logs)
        return peak + jnp.log(sum(jnp.exp(v - peak) for v in logs))

    peak8 = functools.reduce(jnp.maximum, [peak_s[c] for c in range(d.nk)])
    peak = jnp.max(peak8, axis=0, keepdims=True)
    total8 = sum(total_s[c] * jnp.exp(peak_s[c] - peak) for c in range(d.nk))
    st_own[...] = peak + jnp.log(jnp.maximum(jnp.sum(total8, axis=0, keepdims=True), 1e-30))

    def st_a_copy(k):
        return remote(st_own, st_a.at[k], sa_s.at[k], sa_r.at[k], group_dev(k))

    def st_b_copy(k):
        return remote(st_own2, st_b.at[k], sb_s.at[k], sb_r.at[k], z_dev(k))

    fly("st_a", d.ng, st_a_copy)
    for j in range(d.nj):
        vec_t[:, j * ib : (j + 1) * ib] = vecs[j].astype(F32).T.astype(BF16)
    land("st_a")
    st_own2[...] = merge([st_own[...]] + [st_a[k] for k in range(1, d.ng)])
    fly("st_b", d.nz, st_b_copy)
    land("st_b")
    log_total = merge([st_own2[...]] + [st_b[k] for k in range(1, d.nz)])
    for c in range(d.nk):
        factor[c] = weight_s[...] * jnp.exp(peak_s[c] - log_total)

    def gv_copy(j):
        return remote(gv_send.at[j], gv_recv.at[j], gv_s.at[j], gv_r.at[j], across if j == 2 else sibling)

    width = min(512, d.users)
    per = ib // d.chunk

    def grads(t, carry):
        j = jnp.where(t == 0, 3, jnp.where(t == 3, 0, t))
        rows = pl.ds(pl.multiple_of(j * ib, ib), ib)
        acc = jnp.zeros((ib, emb), F32)
        tile = lax.broadcasted_iota(jnp.int32, (ib // 8, 8, width), 0)
        for u in range(0, d.users, width):
            lanes = slice(u, u + width)
            e = expo[rows, lanes].reshape(per, d.chunk // 8, 8, width)
            e = (e * factor[pl.ds(j * per, per), :, lanes][:, None]).reshape(ib // 8, 8, width)
            hit = tile == (tile_s[:, lanes] - j * (ib // 8))[None]
            g = jnp.where(hit, e - weight_s[:, lanes][None], e).reshape(ib, width).astype(BF16)
            grad[rows, lanes] = g
            acc = acc + dot(g, users[...].reshape(d.users, emb)[lanes, :])
        gv_own[...] = acc

        for at, i in ((0, 3), (1, 1)):

            @pl.when(t == at)
            def _():
                gv_send[i] = gv_own[...].astype(BF16)
                launch(f"gv{i}", functools.partial(gv_copy, i))

        @pl.when(t == 2)
        def _():
            arrive("gv3")
            gv_send[2] = (gv_own[...] + gv_recv[3].astype(F32)).astype(BF16)
            launch("gv2", functools.partial(gv_copy, 2))

        return carry

    lax.fori_loop(0, 4, grads, 0)

    us = ub // d.ng

    def gu_copy(k):
        to = lax.rem(item + k, d.ng)
        return remote(gu_send.at[to], gu_recv.at[k], gu_s.at[k], gu_r.at[k], dev(to, xl, z, core))

    def user_terms(i, carry):
        lanes = pl.ds(pl.multiple_of(i * width, width), width)
        terms = dot(vec_t[...], grad[:, lanes]).T.astype(BF16)
        for q in range(width // us):
            at = q % d.ng
            gu_send[at, i * (width // ub) + q // d.ng] = terms[q * us : (q + 1) * us, :]
        return carry

    lax.fori_loop(0, d.users // width, user_terms, 0)
    fly("gu", d.ng, gu_copy)

    arrive("gv1")
    arrive("gv2")
    gv = gv_own[...] + gv_recv[1].astype(F32) + gv_recv[2].astype(F32)
    gv = gv.astype(BF16)
    gv_own[...] = gv.astype(F32)
    gv_t = gv_own[...].T.astype(BF16)
    hc = hid // 2
    mine = pl.ds(pl.multiple_of(core * hc, hc), hc)
    other = pl.ds(pl.multiple_of((1 - core) * hc, hc), hc)

    def wc_copy(m):
        return remote(wc_send.at[m], wc_recv.at[m], wc_s.at[m], wc_r.at[m], sibling)

    wg_own[1] = dot(gv_t, hidden[...])
    wc_send[1] = wg_own[1, :, other].astype(BF16)
    launch("wc1", functools.partial(wc_copy, 1))

    def back(t, carry):
        rows = pl.ds(pl.multiple_of(t * rt, rt), rt)
        g = gv_own[rows, :]
        pre = (dot_t(g.astype(BF16), w_out[...]) * slope[rows, :]).astype(BF16)
        hidden[rows, :] = pre
        out_item[rows, :] = g + dot_t(pre, w_in[...])
        return carry

    lax.fori_loop(0, ib // rt, back, 0)
    wg_own[0] = dot(feats[...].astype(F32).T.astype(BF16), hidden[...])
    wc_send[0] = wg_own[0, :, other].astype(BF16)
    launch("wc0", functools.partial(wc_copy, 0))

    half = d.np // 2
    sr = d.srows

    def w1_copy(k):
        p = plane_peer(k)
        return remote(w1_send.at[p], w1_recv.at[k], w1_s.at[k], w1_r.at[k], plane_dev(p))

    fly("w1", d.np, w1_copy, start=False)
    for m in (1, 0):
        arrive(f"wc{m}")
        total = wg_own[m, :, mine] + wc_recv[m].astype(F32)
        w1_send[m * half : (m + 1) * half] = total.astype(BF16).reshape(half, sr, hc)

        def send(k):
            p = plane_peer(k)

            @pl.when(p < half if m == 0 else p >= half)
            def _():
                w1_copy(k).start()

        each(d.np, send)

    land("gu")
    gu_sum[...] = gu_send[item].astype(F32) + sum(gu_recv[k].astype(F32) for k in range(1, d.ng))

    def g2_copy(k):
        return remote(gu_sum.at[z_peer(k)], gu2_recv.at[k], g2_s.at[k], g2_r.at[k], z_dev(k))

    fly("g2", d.nz, g2_copy)
    land("w1")
    part = w1_send[plane].astype(F32)
    for k in range(1, d.np):
        part = part + w1_recv[k].astype(F32)
    wz[z] = part.astype(BF16)

    def wz_copy(k, slot):
        return remote(wz.at[slot], wz.at[slot], wz_s.at[k], wz_r.at[k], z_dev(k))

    fly("wz", d.nz, lambda k: wz_copy(k, z), lambda k: wz_copy(k, back_by(z, k, d.nz)))

    land("g2")
    mine = gu_sum[z]
    for k in range(1, d.nz):
        mine = mine + gu2_recv[k]
    gu_out[item] = mine

    def g3_copy(k, slot):
        return remote(gu_out.at[slot], gu_out.at[slot], g3_s.at[k], g3_r.at[k], group_dev(k))

    fly("g3", d.ng, lambda k: g3_copy(k, item), lambda k: g3_copy(k, back_by(item, k, d.ng)))

    land("wz")
    whole = sum(wz[k].astype(F32) for k in range(d.nz))
    a1[core, plane] = whole.astype(BF16)

    def w4_copy(k, slot):
        there = a1.at[core, slot]
        return remote(there, there, w4_s.at[k], w4_r.at[k], plane_dev(plane_peer(k)))

    def w5_copy(k, slot, of):
        there = a1.at[of, slot]
        return remote(there, there, w5_s.at[k], w5_r.at[k], sibling)

    fly("w4", d.np, lambda k: w4_copy(k, plane), lambda k: w4_copy(k, back_by(plane, k, d.np)))
    w5_copy(0, plane, core).start()

    def hand_on(k):
        slot = back_by(plane, k, d.np)
        w4_copy(k, slot).wait_recv()
        w5_copy(k, slot, core).start()

    each(d.np, hand_on)
    flights["w4"][3] = True
    land("g3")
    out_user[...] = gu_out[...].reshape(ub, emb)
    w5_copy(0, plane, 1 - core).wait_recv()
    each(d.np, lambda k: w5_copy(k, back_by(plane, k, d.np), 1 - core).wait_recv())
    out_w[...] = a1[...]

    finish()
    w5_copy(0, plane, core).wait_send()
    each(d.np, lambda k: w5_copy(k, back_by(plane, k, d.np), core).wait_send())


def unpack(d, user_ref, item_ref, w_ref, out_user, out_item, out_w_in, out_w_out):
    out_user[...] = user_ref[...]
    out_item[...] = item_ref[...]
    half = d.np // 2
    for c in range(2):
        cols = slice(c * d.scols, (c + 1) * d.scols)
        out_w_in[:, cols] = w_ref[c, :half].astype(F32).reshape(d.emb, d.scols)
        out_w_out[cols, :] = w_ref[c, half:].astype(F32).reshape(d.emb, d.scols).T


def body(phys, user_vecs, row_weight, positive, item_feats, valid, w_in, w_out):
    ub, emb = user_vecs.shape
    ib, hid = item_feats.shape[0], w_in.shape[1]
    d = Dims(phys, ub, ib, emb, hid)
    vm = pltpu.VMEM
    us = ub // d.ng
    scratch = [
        vm((d.nz, ub, emb), BF16),
        vm((d.nz, 2, ub), F32),
        vm((d.nj, ib, emb), BF16),
        vm((d.nj, 1, ib), F32),
        vm((d.nj, ib, 128), F32),
        vm((emb, d.items), BF16),
        vm((ib, hid), BF16),
        vm((ib, hid), F32),
        vm((d.items, d.users), F32),
        vm((d.items, d.users), BF16),
        vm((d.nk, 8, d.users), F32),
        vm((d.nk, 8, d.users), F32),
        vm((d.nk, 8, d.users), F32),
        vm((8, d.users), jnp.int32),
        vm((1, d.users), F32),
        vm((1, d.users), F32),
        vm((d.ng, 1, d.users), F32),
        vm((1, d.users), F32),
        vm((d.nz, 1, d.users), F32),
        vm((d.nj, ib, emb), BF16),
        vm((d.nj, ib, emb), BF16),
        vm((ib, emb), F32),
        vm((d.ng, d.nz, us, emb), BF16),
        vm((d.ng, d.nz, us, emb), BF16),
        vm((d.nz, us, emb), F32),
        vm((d.nz, us, emb), F32),
        vm((d.ng, us, emb), F32),
        vm((2, emb, hid), F32),
        vm((2, emb, hid // 2), BF16),
        vm((2, emb, hid // 2), BF16),
        vm((d.np, d.srows, d.scols), BF16),
        vm((d.np, d.srows, d.scols), BF16),
        vm((d.nz, d.srows, d.scols), BF16),
        vm((2, d.np, d.srows, d.scols), BF16),
    ]
    dma = pltpu.SemaphoreType.DMA
    sems = []
    for n in (d.nz, d.nz, d.nj, d.nj, d.ng, d.nz, d.nj, d.ng, d.nz, d.ng, 2, d.np, d.nz, d.np, d.np):
        sems += [dma((n,)), dma((n,))]
    whole = pl.BlockSpec(memory_space=pltpu.VMEM)
    parts = pl.pallas_call(
        functools.partial(kernel, d),
        out_shape=(
            jax.ShapeDtypeStruct((ub, emb), F32),
            jax.ShapeDtypeStruct((ib, emb), F32),
            jax.ShapeDtypeStruct((2, d.np, d.srows, d.scols), BF16),
        ),
        in_specs=[whole] * 7,
        out_specs=(whole,) * 3,
        scratch_shapes=scratch + sems,
        compiler_params=pltpu.CompilerParams(
            collective_id=0, has_side_effects=True, vmem_limit_bytes=44 * 1024 * 1024
        ),
        cost_estimate=pl.CostEstimate(
            flops=6 * d.users * d.items * emb,
            bytes_accessed=4 * 1024 * 1024,
            transcendentals=d.users * d.items,
        ),
    )(user_vecs, row_weight, positive, item_feats, valid, w_in, w_out)
    return pl.pallas_call(
        functools.partial(unpack, d),
        out_shape=(
            jax.ShapeDtypeStruct((ub, emb), F32),
            jax.ShapeDtypeStruct((ib, emb), F32),
            jax.ShapeDtypeStruct((emb, hid), F32),
            jax.ShapeDtypeStruct((hid, emb), F32),
        ),
        in_specs=[whole] * 3,
        out_specs=(whole,) * 4,
    )(*parts)


def build(mesh, phys):
    return jax.shard_map(
        functools.partial(body, phys),
        mesh=mesh,
        in_specs=(
            P("user", None),
            P("user"),
            P("user"),
            P(("item", "user"), None),
            P(("item", "user")),
            P(),
            P(),
        ),
        out_specs=(P("user", None), P(("item", "user"), None), P(), P()),
        check_vma=False,
    )


def solution(mesh):
    return build(mesh, (4, 2, 2, 8, 2))
```

```python
import functools

import jax
import jax.numpy as jnp
from jax import lax
from jax.experimental import pallas as pl
from jax.experimental.pallas import tpu as pltpu
from jax.sharding import PartitionSpec as P

MESH = pl.DeviceIdType.MESH
F32 = jnp.float32
BF16 = jnp.bfloat16
DEAD = -1e30
FLOOR = -1e29


def dot(a, b):
    return jnp.dot(a, b, preferred_element_type=F32)


def dot_t(a, b):
    return lax.dot_general(a, b, (((1,), (1,)), ((), ())), preferred_element_type=F32)


class Dims:
    def __init__(self, phys, ub, ib, emb, hid):
        self.ny, self.nxh, self.nxl, self.nz, self.nc = phys
        self.ub, self.ib, self.emb, self.hid = ub, ib, emb, hid
        self.ng = self.ny * self.nxh
        self.np = self.ng * self.nxl
        self.nj = self.nxl * self.nc
        self.users = self.nz * ub
        self.items = self.nj * ib
        self.chunk = min(256, ib)
        self.nk = self.items // self.chunk
        self.srows = 2 * emb // self.np
        self.scols = hid // 2


def kernel(
    d,
    users_in, weight_in, pos_in, feats, valid_in, w_in, w_out,
    out_user, out_item, out_w,
    users, meta, vecs, valid, bias, vec_t, hidden, slope, expo, grad,
    peak_s, total_s, factor, tile_s, weight_s,
    st_own, st_a, st_own2, st_b,
    gv_send, gv_recv, gv_own, gu_send, gu_recv, gu_sum, gu2_recv, gu_out,
    wg_own, wc_send, wc_recv, w1_send, w1_recv, wz, a1,
    us_s, us_r, me_s, me_r, ve_s, ve_r, va_s, va_r, sa_s, sa_r, sb_s, sb_r,
    gv_s, gv_r, gu_s, gu_r, g2_s, g2_r, g3_s, g3_r,
    wc_s, wc_r, w1_s, w1_r, wz_s, wz_r, w4_s, w4_r, w5_s, w5_r,
):
    ub, ib, emb, hid = d.ub, d.ib, d.emb, d.hid
    item = lax.axis_index("item")
    user = lax.axis_index("user")
    core = lax.rem(user, d.nc)
    z = lax.rem(lax.div(user, d.nc), d.nz)
    xl = lax.div(user, d.nc * d.nz)
    plane = item * d.nxl + xl

    def dev(item_, xl_, z_, core_):
        return (item_, (xl_ * d.nz + z_) * d.nc + core_)

    def back_by(here, k, n):
        return lax.rem(here + n - k, n)

    def z_peer(k):
        return lax.rem(z + k, d.nz)

    def z_dev(k):
        return dev(item, xl, z_peer(k), core)

    def group_dev(k):
        return dev(lax.rem(item + k, d.ng), xl, z, core)

    def plane_peer(k):
        return lax.rem(plane + k, d.np)

    def plane_dev(p):
        return dev(lax.div(p, d.nxl), lax.rem(p, d.nxl), z, core)

    sibling = dev(item, xl, z, 1 - core)
    across = dev(item, 1 - xl, z, core)

    def remote(src, dst, send, recv, to):
        return pltpu.make_async_remote_copy(
            src_ref=src, dst_ref=dst, send_sem=send, recv_sem=recv, device_id=to, device_id_type=MESH
        )

    def each(n, fn):
        def step(k, carry):
            fn(k)
            return carry

        lax.fori_loop(1, n, step, 0)

    flights = {}

    def fly(name, n, copy_out, copy_in=None, start=True):
        flights[name] = [n, copy_out, copy_in or copy_out, False]
        if start:
            each(n, lambda k: copy_out(k).start())

    def land(name):
        n, _, copy_in, _ = flights[name]
        each(n, lambda k: copy_in(k).wait_recv())
        flights[name][3] = True

    tails = []
    singles = {}

    def launch(name, make):
        singles[name] = [make, False]
        make().start()

    def arrive(name):
        singles[name][0]().wait_recv()
        singles[name][1] = True

    def finish():
        for wait in tails:
            wait()
        for make, landed in singles.values():
            if not landed:
                make().wait_recv()
            make().wait_send()
        for name, (n, copy_out, _, landed) in flights.items():
            if not landed:
                land(name)
            each(n, lambda k: copy_out(k).wait_send())

    barrier = pltpu.get_barrier_semaphore()

    def greet(to):
        pl.semaphore_signal(barrier, inc=1, device_id=to, device_id_type=MESH)

    each(d.nz, lambda k: greet(z_dev(k)))
    each(d.np, lambda k: greet(plane_dev(plane_peer(k))))
    greet(sibling)

    users[z] = users_in[...]
    pos = pos_in[...].reshape(1, ub)
    meta[z] = jnp.concatenate([pos.astype(F32), weight_in[...].reshape(1, ub).astype(F32)], axis=0)
    valid[0] = valid_in[...].reshape(1, ib).astype(F32)
    rt = min(128, ib)

    def tower(t, carry):
        rows = pl.ds(pl.multiple_of(t * rt, rt), rt)
        x = feats[rows, :]
        pre = dot(x, w_in[...])
        sigma = jax.nn.sigmoid(pre)
        hid_t = (pre * sigma).astype(BF16)
        hidden[rows, :] = hid_t
        slope[rows, :] = pre
        vecs[0, rows, :] = (x.astype(F32) + dot(hid_t, w_out[...])).astype(BF16)
        return carry

    lax.fori_loop(0, ib // rt, tower, 0)
    pl.semaphore_wait(barrier, d.nz - 1 + d.np - 1 + 1)

    far = d.nz // 2
    direct = [k for k in (2, d.nz - 2, 1, d.nz - 1) if 0 < k < d.nz]
    direct = sorted(set(direct), key=direct.index)
    handed = [k for k in range(1, d.nz) if k not in direct]
    order = [0] + direct + sorted(handed, key=lambda k: k == far)

    def hops_of(step):
        k = 0
        for i in range(1, d.nz):
            k = jnp.where(step == i, order[i], k)
        return k

    def users_copies(k, slot, to):
        there = z_dev(to)
        return [
            remote(users.at[slot], users.at[slot], us_s.at[k], us_r.at[k], there),
            remote(meta.at[slot], meta.at[slot], me_s.at[k], me_r.at[k], there),
        ]

    def users_start(k, slot, to):
        for copy in users_copies(k, slot, to):
            copy.start()

    def users_sent():
        for k in range(1, d.nz):
            for copy in users_copies(k, z, 1):
                copy.wait_send()

    def users_arrive(k, slot):
        for copy in users_copies(k, slot, 1):
            copy.wait_recv()

    def hand_on_users(k):
        slot = back_by(z, k, d.nz)
        ahead = k == 2
        users_start(3 if ahead else d.nz - 3, slot, 1 if ahead else d.nz - 1)

        @pl.when(core == (0 if ahead else 1))
        def _():
            users_start(far, slot, 2 if ahead else d.nz - 2)

    def vecs_copy(j):
        return remote(vecs.at[j // 3 * 2], vecs.at[j], ve_s.at[j], ve_r.at[j], across if j == 2 else sibling)

    def valid_copy(j):
        return remote(valid.at[j // 3 * 2], valid.at[j], va_s.at[j], va_r.at[j], across if j == 2 else sibling)

    for j in (2, 1):
        launch(f"vecs{j}", functools.partial(vecs_copy, j))
        launch(f"valid{j}", functools.partial(valid_copy, j))
    for k in direct:
        users_start(k, z, k)
    tails.append(users_sent)

    def vec_arrives(j):
        arrive(f"vecs{j}")
        arrive(f"valid{j}")

    def user_slot(step):
        return lax.rem(z + d.nz - hops_of(step), d.nz)

    def local_tile(pos):
        block = pos // ib
        p_core = block % d.nc
        p_z = block // d.nc % d.nz
        p_xl = block // (d.nc * d.nz) % d.nxl
        p_item = block // (d.nc * d.nz * d.nxl)
        j = (p_xl + d.nxl - xl) % d.nxl * d.nc + (p_core + d.nc - core) % d.nc
        here = (p_item == item) & (p_z == z)
        row = jnp.where(here, j * ib + pos % ib, -1)
        lane = lax.broadcasted_iota(jnp.int32, (8, ub), 0)
        return jnp.where(here & (lane == row % 8), row // 8, -1)

    def set_bias(j):
        bias[j] = (jnp.broadcast_to(valid[j], (128, ib)).T - 1.0) * -DEAD

    def enter(step, slot):
        lanes = pl.ds(pl.multiple_of(slot * ub, ub), ub)
        tile_s[:, lanes] = local_tile(meta[slot, 0:1, :].astype(jnp.int32))
        weight_s[:, lanes] = meta[slot, 1:2, :]

    def score(j, slot):
        at = pl.multiple_of(slot * ub, ub)
        tile = lax.broadcasted_iota(jnp.int32, (d.chunk // 8, 8, 128), 0)
        for c in range(ib // d.chunk):
            rows = slice(c * d.chunk, (c + 1) * d.chunk)
            s = dot_t(vecs[j, rows, :], users[slot])
            b = bias[j, rows, :].reshape(d.chunk // 8, 8, 128)
            ck = j * (ib // d.chunk) + c
            first = pl.multiple_of(ck * d.chunk, d.chunk)
            for h in range(ub // 128):
                lanes = pl.ds(pl.multiple_of(at + h * 128, 128), 128)
                sh = s[:, h * 128 : (h + 1) * 128].reshape(d.chunk // 8, 8, 128)
                hit = tile == (tile_s[:, lanes] - ck * (d.chunk // 8))[None]
                x = jnp.where(hit, sh, sh + b)
                peak = jnp.maximum(jnp.max(x, axis=0), FLOOR)
                e = jnp.exp(x - peak[None])
                peak_s[ck, :, lanes] = peak
                total_s[ck, :, lanes] = jnp.sum(e, axis=0)
                expo[pl.ds(first, d.chunk), lanes] = e.reshape(d.chunk, 128)

    first = min(5, d.nz)
    turn = min(3, first)

    def early_steps(i, carry):
        pair = lax.div(i, first)
        step = lax.rem(i, first)
        slot = jnp.where(step == 0, z, user_slot(step))

        @pl.when(i == 0)
        def _():
            vec_arrives(1)
            set_bias(0)
            set_bias(1)

        for at in range(1, first):

            @pl.when(i == at)
            def _():
                k = order[at]
                users_arrive(k, back_by(z, k, d.nz))
                if handed and k in (2, d.nz - 2):
                    hand_on_users(k)

        @pl.when(i == turn)
        def _():
            vec_arrives(2)
            launch("vecs3", functools.partial(vecs_copy, 3))
            launch("valid3", functools.partial(valid_copy, 3))

        @pl.when(i == first)
        def _():
            vec_arrives(3)
            set_bias(2)
            set_bias(3)

        @pl.when(pair == 0)
        def _():
            enter(step, slot)

        score(pair * 2, slot)
        score(pair * 2 + 1, slot)
        return carry

    lax.fori_loop(0, 2 * first, early_steps, 0)

    def late_steps(step, carry):
        slot = user_slot(step)
        users_arrive(hops_of(step), slot)
        enter(step, slot)
        for j in range(d.nj):
            score(j, slot)
        return carry

    lax.fori_loop(first, d.nz, late_steps, 0)

    def merge(logs):
        peak = functools.reduce(jnp.maximum, logs)
        return peak + jnp.log(sum(jnp.exp(v - peak) for v in logs))

    peak8 = functools.reduce(jnp.maximum, [peak_s[c] for c in range(d.nk)])
    peak = jnp.max(peak8, axis=0, keepdims=True)
    total8 = sum(total_s[c] * jnp.exp(peak_s[c] - peak) for c in range(d.nk))
    st_own[...] = peak + jnp.log(jnp.maximum(jnp.sum(total8, axis=0, keepdims=True), 1e-30))

    def st_a_copy(k):
        return remote(st_own, st_a.at[k], sa_s.at[k], sa_r.at[k], group_dev(k))

    def st_b_copy(k):
        return remote(st_own2, st_b.at[k], sb_s.at[k], sb_r.at[k], z_dev(k))

    fly("st_a", d.ng, st_a_copy)
    for j in range(d.nj):
        vec_t[:, j * ib : (j + 1) * ib] = vecs[j].astype(F32).T.astype(BF16)

    def slopes(t, carry):
        rows = pl.ds(pl.multiple_of(t * rt, rt), rt)
        pre = slope[rows, :]
        sigma = jax.nn.sigmoid(pre)
        slope[rows, :] = sigma * (1.0 + pre * (1.0 - sigma))
        return carry

    lax.fori_loop(0, ib // rt, slopes, 0)
    land("st_a")
    st_own2[...] = merge([st_own[...]] + [st_a[k] for k in range(1, d.ng)])
    fly("st_b", d.nz, st_b_copy)
    land("st_b")
    log_total = merge([st_own2[...]] + [st_b[k] for k in range(1, d.nz)])
    for c in range(d.nk):
        factor[c] = weight_s[...] * jnp.exp(peak_s[c] - log_total)

    def gv_copy(j):
        return remote(gv_send.at[j], gv_recv.at[j], gv_s.at[j], gv_r.at[j], across if j == 2 else sibling)

    width = min(512, d.users)
    per = ib // d.chunk

    def grads(t, carry):
        j = jnp.where(t == 0, 3, jnp.where(t == 3, 0, t))
        rows = pl.ds(pl.multiple_of(j * ib, ib), ib)
        acc = jnp.zeros((ib, emb), F32)
        tile = lax.broadcasted_iota(jnp.int32, (ib // 8, 8, width), 0)
        for u in range(0, d.users, width):
            lanes = slice(u, u + width)
            e = expo[rows, lanes].reshape(per, d.chunk // 8, 8, width)
            e = (e * factor[pl.ds(j * per, per), :, lanes][:, None]).reshape(ib // 8, 8, width)
            hit = tile == (tile_s[:, lanes] - j * (ib // 8))[None]
            g = jnp.where(hit, e - weight_s[:, lanes][None], e).reshape(ib, width).astype(BF16)
            grad[rows, lanes] = g
            acc = acc + dot(g, users[...].reshape(d.users, emb)[lanes, :])
        gv_own[...] = acc

        for at, i in ((0, 3), (1, 1)):

            @pl.when(t == at)
            def _():
                gv_send[i] = gv_own[...].astype(BF16)
                launch(f"gv{i}", functools.partial(gv_copy, i))

        @pl.when(t == 2)
        def _():
            arrive("gv3")
            gv_send[2] = (gv_own[...] + gv_recv[3].astype(F32)).astype(BF16)
            launch("gv2", functools.partial(gv_copy, 2))

        return carry

    lax.fori_loop(0, 4, grads, 0)

    us = ub // d.ng

    def gu_copy(k):
        to = lax.rem(item + k, d.ng)
        return remote(gu_send.at[to], gu_recv.at[k], gu_s.at[k], gu_r.at[k], dev(to, xl, z, core))

    def user_terms(i, carry):
        lanes = pl.ds(pl.multiple_of(i * width, width), width)
        terms = dot(vec_t[...], grad[:, lanes]).T.astype(BF16)
        for q in range(width // us):
            at = q % d.ng
            gu_send[at, i * (width // ub) + q // d.ng] = terms[q * us : (q + 1) * us, :]
        return carry

    lax.fori_loop(0, d.users // width, user_terms, 0)
    fly("gu", d.ng, gu_copy)

    arrive("gv1")
    arrive("gv2")
    gv = gv_own[...] + gv_recv[1].astype(F32) + gv_recv[2].astype(F32)
    gv = gv.astype(BF16)
    gv_own[...] = gv.astype(F32)
    gv_t = gv_own[...].T.astype(BF16)
    hc = hid // 2
    mine = pl.ds(pl.multiple_of(core * hc, hc), hc)
    other = pl.ds(pl.multiple_of((1 - core) * hc, hc), hc)

    def wc_copy(m):
        return remote(wc_send.at[m], wc_recv.at[m], wc_s.at[m], wc_r.at[m], sibling)

    wg_own[1] = dot(gv_t, hidden[...])
    wc_send[1] = wg_own[1, :, other].astype(BF16)
    launch("wc1", functools.partial(wc_copy, 1))

    def back(t, carry):
        rows = pl.ds(pl.multiple_of(t * rt, rt), rt)
        g = gv_own[rows, :]
        pre = (dot_t(g.astype(BF16), w_out[...]) * slope[rows, :]).astype(BF16)
        hidden[rows, :] = pre
        out_item[rows, :] = g + dot_t(pre, w_in[...])
        return carry

    lax.fori_loop(0, ib // rt, back, 0)
    wg_own[0] = dot(feats[...].astype(F32).T.astype(BF16), hidden[...])
    wc_send[0] = wg_own[0, :, other].astype(BF16)
    launch("wc0", functools.partial(wc_copy, 0))

    half = d.np // 2
    sr = d.srows

    def w1_copy(k):
        p = plane_peer(k)
        return remote(w1_send.at[p], w1_recv.at[k], w1_s.at[k], w1_r.at[k], plane_dev(p))

    fly("w1", d.np, w1_copy, start=False)
    for m in (1, 0):
        arrive(f"wc{m}")
        total = wg_own[m, :, mine] + wc_recv[m].astype(F32)
        w1_send[m * half : (m + 1) * half] = total.astype(BF16).reshape(half, sr, hc)

        def send(k):
            p = plane_peer(k)

            @pl.when(p < half if m == 0 else p >= half)
            def _():
                w1_copy(k).start()

        each(d.np, send)

    land("gu")
    gu_sum[...] = gu_send[item].astype(F32) + sum(gu_recv[k].astype(F32) for k in range(1, d.ng))

    def g2_copy(k):
        return remote(gu_sum.at[z_peer(k)], gu2_recv.at[k], g2_s.at[k], g2_r.at[k], z_dev(k))

    fly("g2", d.nz, g2_copy)
    land("w1")
    part = w1_send[plane].astype(F32)
    for k in range(1, d.np):
        part = part + w1_recv[k].astype(F32)
    wz[z] = part.astype(BF16)

    def wz_copy(k, slot):
        return remote(wz.at[slot], wz.at[slot], wz_s.at[k], wz_r.at[k], z_dev(k))

    fly("wz", d.nz, lambda k: wz_copy(k, z), lambda k: wz_copy(k, back_by(z, k, d.nz)))

    land("g2")
    mine = gu_sum[z]
    for k in range(1, d.nz):
        mine = mine + gu2_recv[k]
    gu_out[item] = mine

    def g3_copy(k, slot):
        return remote(gu_out.at[slot], gu_out.at[slot], g3_s.at[k], g3_r.at[k], group_dev(k))

    fly("g3", d.ng, lambda k: g3_copy(k, item), lambda k: g3_copy(k, back_by(item, k, d.ng)))

    land("wz")
    whole = sum(wz[k].astype(F32) for k in range(d.nz))
    a1[core, plane] = whole.astype(BF16)

    def w4_copy(k, slot):
        there = a1.at[core, slot]
        return remote(there, there, w4_s.at[k], w4_r.at[k], plane_dev(plane_peer(k)))

    def w5_copy(k, slot, of):
        there = a1.at[of, slot]
        return remote(there, there, w5_s.at[k], w5_r.at[k], sibling)

    fly("w4", d.np, lambda k: w4_copy(k, plane), lambda k: w4_copy(k, back_by(plane, k, d.np)))
    w5_copy(0, plane, core).start()

    def hand_on(k):
        slot = back_by(plane, k, d.np)
        w4_copy(k, slot).wait_recv()
        w5_copy(k, slot, core).start()

    each(d.np, hand_on)
    flights["w4"][3] = True
    land("g3")
    out_user[...] = gu_out[...].reshape(ub, emb)
    w5_copy(0, plane, 1 - core).wait_recv()
    each(d.np, lambda k: w5_copy(k, back_by(plane, k, d.np), 1 - core).wait_recv())
    out_w[...] = a1[...]

    finish()
    w5_copy(0, plane, core).wait_send()
    each(d.np, lambda k: w5_copy(k, back_by(plane, k, d.np), core).wait_send())


def unpack(d, user_ref, item_ref, w_ref, out_user, out_item, out_w_in, out_w_out):
    out_user[...] = user_ref[...]
    out_item[...] = item_ref[...]
    half = d.np // 2
    for c in range(2):
        cols = slice(c * d.scols, (c + 1) * d.scols)
        out_w_in[:, cols] = w_ref[c, :half].astype(F32).reshape(d.emb, d.scols)
        out_w_out[cols, :] = w_ref[c, half:].astype(F32).reshape(d.emb, d.scols).T


def body(phys, user_vecs, row_weight, positive, item_feats, valid, w_in, w_out):
    ub, emb = user_vecs.shape
    ib, hid = item_feats.shape[0], w_in.shape[1]
    d = Dims(phys, ub, ib, emb, hid)
    vm = pltpu.VMEM
    us = ub // d.ng
    scratch = [
        vm((d.nz, ub, emb), BF16),
        vm((d.nz, 2, ub), F32),
        vm((d.nj, ib, emb), BF16),
        vm((d.nj, 1, ib), F32),
        vm((d.nj, ib, 128), F32),
        vm((emb, d.items), BF16),
        vm((ib, hid), BF16),
        vm((ib, hid), F32),
        vm((d.items, d.users), F32),
        vm((d.items, d.users), BF16),
        vm((d.nk, 8, d.users), F32),
        vm((d.nk, 8, d.users), F32),
        vm((d.nk, 8, d.users), F32),
        vm((8, d.users), jnp.int32),
        vm((1, d.users), F32),
        vm((1, d.users), F32),
        vm((d.ng, 1, d.users), F32),
        vm((1, d.users), F32),
        vm((d.nz, 1, d.users), F32),
        vm((d.nj, ib, emb), BF16),
        vm((d.nj, ib, emb), BF16),
        vm((ib, emb), F32),
        vm((d.ng, d.nz, us, emb), BF16),
        vm((d.ng, d.nz, us, emb), BF16),
        vm((d.nz, us, emb), F32),
        vm((d.nz, us, emb), F32),
        vm((d.ng, us, emb), F32),
        vm((2, emb, hid), F32),
        vm((2, emb, hid // 2), BF16),
        vm((2, emb, hid // 2), BF16),
        vm((d.np, d.srows, d.scols), BF16),
        vm((d.np, d.srows, d.scols), BF16),
        vm((d.nz, d.srows, d.scols), BF16),
        vm((2, d.np, d.srows, d.scols), BF16),
    ]
    dma = pltpu.SemaphoreType.DMA
    sems = []
    for n in (d.nz, d.nz, d.nj, d.nj, d.ng, d.nz, d.nj, d.ng, d.nz, d.ng, 2, d.np, d.nz, d.np, d.np):
        sems += [dma((n,)), dma((n,))]
    whole = pl.BlockSpec(memory_space=pltpu.VMEM)
    parts = pl.pallas_call(
        functools.partial(kernel, d),
        out_shape=(
            jax.ShapeDtypeStruct((ub, emb), F32),
            jax.ShapeDtypeStruct((ib, emb), F32),
            jax.ShapeDtypeStruct((2, d.np, d.srows, d.scols), BF16),
        ),
        in_specs=[whole] * 7,
        out_specs=(whole,) * 3,
        scratch_shapes=scratch + sems,
        compiler_params=pltpu.CompilerParams(
            collective_id=0, has_side_effects=True, vmem_limit_bytes=56 * 1024 * 1024
        ),
        cost_estimate=pl.CostEstimate(
            flops=6 * d.users * d.items * emb,
            bytes_accessed=4 * 1024 * 1024,
            transcendentals=d.users * d.items,
        ),
    )(user_vecs, row_weight, positive, item_feats, valid, w_in, w_out)
    return pl.pallas_call(
        functools.partial(unpack, d),
        out_shape=(
            jax.ShapeDtypeStruct((ub, emb), F32),
            jax.ShapeDtypeStruct((ib, emb), F32),
            jax.ShapeDtypeStruct((emb, hid), F32),
            jax.ShapeDtypeStruct((hid, emb), F32),
        ),
        in_specs=[whole] * 3,
        out_specs=(whole,) * 4,
    )(*parts)


def build(mesh, phys):
    return jax.shard_map(
        functools.partial(body, phys),
        mesh=mesh,
        in_specs=(
            P("user", None),
            P("user"),
            P("user"),
            P(("item", "user"), None),
            P(("item", "user")),
            P(),
            P(),
        ),
        out_specs=(P("user", None), P(("item", "user"), None), P(), P()),
        check_vma=False,
    )


def solution(mesh):
    return build(mesh, (4, 2, 2, 8, 2))
```

```python
import functools

import jax
import jax.numpy as jnp
from jax import lax
from jax.experimental import pallas as pl
from jax.experimental.pallas import tpu as pltpu
from jax.sharding import PartitionSpec as P

MESH = pl.DeviceIdType.MESH
F32 = jnp.float32
BF16 = jnp.bfloat16
DEAD = -1e30
FLOOR = -1e29


def dot(a, b):
    return jnp.dot(a, b, preferred_element_type=F32)


def dot_t(a, b):
    return lax.dot_general(a, b, (((1,), (1,)), ((), ())), preferred_element_type=F32)


class Dims:
    def __init__(self, phys, ub, ib, emb, hid):
        self.ny, self.nxh, self.nxl, self.nz, self.nc = phys
        self.ub, self.ib, self.emb, self.hid = ub, ib, emb, hid
        self.ng = self.ny * self.nxh
        self.np = self.ng * self.nxl
        self.nj = self.nxl * self.nc
        self.users = self.nz * ub
        self.items = self.nj * ib
        self.chunk = min(256, ib)
        self.nk = self.items // self.chunk
        self.srows = max(16, emb // self.np)
        self.scols = emb * (hid // 2) // self.np // self.srows


def kernel(
    d,
    users_in, weight_in, pos_in, feats_in, valid_in, w_in_in, w_out_in,
    out_user, out_item, out_w,
    feats, w_in, w_out, users, meta, vecs, valid, bias, vec_t, hidden, slope, expo, grad,
    peak_s, total_s, factor, tile_s, weight_s,
    st_own, st_a, st_own2, st_b,
    gv_send, gv_recv, gv_own, gu_send, gu_recv, gu_sum, gu2_recv, gu_out,
    wg_own, wc_send, wc_recv, w1_send, w1_recv, wz, a1,
    in_s, us_s, us_r, me_s, me_r, ve_s, ve_r, va_s, va_r, sa_s, sa_r, sb_s, sb_r,
    gv_s, gv_r, gu_s, gu_r, g2_s, g2_r, g3_s, g3_r,
    wc_s, wc_r, w1_s, w1_r, wz_s, wz_r, w4_s, w4_r, w5_s, w5_r,
):
    ub, ib, emb, hid = d.ub, d.ib, d.emb, d.hid
    item = lax.axis_index("item")
    user = lax.axis_index("user")
    core = lax.rem(user, d.nc)
    z = lax.rem(lax.div(user, d.nc), d.nz)
    xl = lax.div(user, d.nc * d.nz)
    plane = item * d.nxl + xl

    def dev(item_, xl_, z_, core_):
        return (item_, (xl_ * d.nz + z_) * d.nc + core_)

    def back_by(here, k, n):
        return lax.rem(here + n - k, n)

    def z_peer(k):
        return lax.rem(z + k, d.nz)

    def z_dev(k):
        return dev(item, xl, z_peer(k), core)

    def group_dev(k):
        return dev(lax.rem(item + k, d.ng), xl, z, core)

    def plane_peer(k):
        return lax.rem(plane + k, d.np)

    def plane_dev(p):
        return dev(lax.div(p, d.nxl), lax.rem(p, d.nxl), z, core)

    sibling = dev(item, xl, z, 1 - core)
    across = dev(item, 1 - xl, z, core)

    def remote(src, dst, send, recv, to):
        return pltpu.make_async_remote_copy(
            src_ref=src, dst_ref=dst, send_sem=send, recv_sem=recv, device_id=to, device_id_type=MESH
        )

    def each(n, fn):
        def step(k, carry):
            fn(k)
            return carry

        lax.fori_loop(1, n, step, 0)

    flights = {}

    def fly(name, n, copy_out, copy_in=None, start=True):
        flights[name] = [n, copy_out, copy_in or copy_out, False]
        if start:
            each(n, lambda k: copy_out(k).start())

    def land(name):
        n, _, copy_in, _ = flights[name]
        each(n, lambda k: copy_in(k).wait_recv())
        flights[name][3] = True

    tails = []
    singles = {}

    def launch(name, make):
        singles[name] = [make, False]
        make().start()

    def arrive(name):
        singles[name][0]().wait_recv()
        singles[name][1] = True

    def finish():
        for wait in tails:
            wait()
        for make, landed in singles.values():
            if not landed:
                make().wait_recv()
            make().wait_send()
        for name, (n, copy_out, _, landed) in flights.items():
            if not landed:
                land(name)
            each(n, lambda k: copy_out(k).wait_send())

    inputs = [(feats_in, feats), (w_in_in, w_in), (w_out_in, w_out), (users_in, users.at[z])]
    inputs = [pltpu.make_async_copy(src, dst, in_s.at[i]) for i, (src, dst) in enumerate(inputs)]
    for copy in inputs:
        copy.start()

    barrier = pltpu.get_barrier_semaphore()

    def greet(to):
        pl.semaphore_signal(barrier, inc=1, device_id=to, device_id_type=MESH)

    each(d.nz, lambda k: greet(z_dev(k)))
    each(d.np, lambda k: greet(plane_dev(plane_peer(k))))
    greet(sibling)

    pos = pos_in[...].reshape(1, ub)
    meta[z] = jnp.concatenate([pos.astype(F32), weight_in[...].reshape(1, ub).astype(F32)], axis=0)
    valid[0] = valid_in[...].reshape(1, ib).astype(F32)
    for copy in inputs:
        copy.wait()
    x = feats[...]
    pre = dot(x, w_in[...])
    hid_t = (pre * jax.nn.sigmoid(pre)).astype(BF16)
    hidden[...] = hid_t
    slope[...] = pre
    vecs[0] = (x.astype(F32) + dot(hid_t, w_out[...])).astype(BF16)
    pl.semaphore_wait(barrier, d.nz - 1 + d.np - 1 + 1)

    far = d.nz // 2
    direct = [k for k in (2, d.nz - 2, 1, d.nz - 1) if 0 < k < d.nz]
    direct = sorted(set(direct), key=direct.index)
    handed = [k for k in range(1, d.nz) if k not in direct]
    order = [0] + direct + sorted(handed, key=lambda k: k == far)

    def hops_of(step):
        k = 0
        for i in range(1, d.nz):
            k = jnp.where(step == i, order[i], k)
        return k

    def users_copies(k, slot, to):
        there = z_dev(to)
        return [
            remote(users.at[slot], users.at[slot], us_s.at[k], us_r.at[k], there),
            remote(meta.at[slot], meta.at[slot], me_s.at[k], me_r.at[k], there),
        ]

    def users_start(k, slot, to):
        for copy in users_copies(k, slot, to):
            copy.start()

    def users_sent():
        for k in range(1, d.nz):
            for copy in users_copies(k, z, 1):
                copy.wait_send()

    def users_arrive(k, slot):
        for copy in users_copies(k, slot, 1):
            copy.wait_recv()

    def hand_on_users(k):
        slot = back_by(z, k, d.nz)
        ahead = k == 2
        users_start(3 if ahead else d.nz - 3, slot, 1 if ahead else d.nz - 1)

        @pl.when(core == (0 if ahead else 1))
        def _():
            users_start(far, slot, 2 if ahead else d.nz - 2)

    def vecs_copy(j):
        return remote(vecs.at[j // 3 * 2], vecs.at[j], ve_s.at[j], ve_r.at[j], across if j == 2 else sibling)

    def valid_copy(j):
        return remote(valid.at[j // 3 * 2], valid.at[j], va_s.at[j], va_r.at[j], across if j == 2 else sibling)

    for j in (2, 1):
        launch(f"vecs{j}", functools.partial(vecs_copy, j))
        launch(f"valid{j}", functools.partial(valid_copy, j))
    for k in direct:
        users_start(k, z, k)
    tails.append(users_sent)

    def vec_arrives(j):
        arrive(f"vecs{j}")
        arrive(f"valid{j}")

    def local_tile(pos):
        block = pos // ib
        p_core = block % d.nc
        p_z = block // d.nc % d.nz
        p_xl = block // (d.nc * d.nz) % d.nxl
        p_item = block // (d.nc * d.nz * d.nxl)
        j = (p_xl + d.nxl - xl) % d.nxl * d.nc + (p_core + d.nc - core) % d.nc
        here = (p_item == item) & (p_z == z)
        row = jnp.where(here, j * ib + pos % ib, -1)
        lane = lax.broadcasted_iota(jnp.int32, (8, ub), 0)
        return jnp.where(here & (lane == row % 8), row // 8, -1)

    def set_bias(j):
        bias[j] = (jnp.broadcast_to(valid[j], (128, ib)).T - 1.0) * -DEAD

    def enter(slot):
        lanes = pl.ds(pl.multiple_of(slot * ub, ub), ub)
        tile_s[:, lanes] = local_tile(meta[slot, 0:1, :].astype(jnp.int32))
        weight_s[:, lanes] = meta[slot, 1:2, :]

    def score(j, slot):
        at = pl.multiple_of(slot * ub, ub)
        tile = lax.broadcasted_iota(jnp.int32, (d.chunk // 8, 8, 128), 0)
        for c in range(ib // d.chunk):
            rows = slice(c * d.chunk, (c + 1) * d.chunk)
            s = dot_t(vecs[j, rows, :], users[slot])
            b = bias[j, rows, :].reshape(d.chunk // 8, 8, 128)
            ck = j * (ib // d.chunk) + c
            first = pl.multiple_of(ck * d.chunk, d.chunk)
            for h in range(ub // 128):
                lanes = pl.ds(pl.multiple_of(at + h * 128, 128), 128)
                sh = s[:, h * 128 : (h + 1) * 128].reshape(d.chunk // 8, 8, 128)
                hit = tile == (tile_s[:, lanes] - ck * (d.chunk // 8))[None]
                x = jnp.where(hit, sh, sh + b)
                peak = jnp.maximum(jnp.max(x, axis=0), FLOOR)
                e = jnp.exp(x - peak[None])
                peak_s[ck, :, lanes] = peak
                total_s[ck, :, lanes] = jnp.sum(e, axis=0)
                expo[pl.ds(first, d.chunk), lanes] = e.reshape(d.chunk, 128)

    first = min(5, d.nz)
    groups = [order[1:3], order[3:5]] if d.nz >= 5 else [order[1:first]]
    ng = len(groups)

    def early_steps(i, carry):
        pair = lax.div(i, ng)
        turn = lax.rem(i, ng)

        for at, group in enumerate(groups):

            @pl.when(i == at)
            def _():
                for k in group:
                    slot = back_by(z, k, d.nz)
                    users_arrive(k, slot)
                    if handed and k in (2, d.nz - 2):
                        hand_on_users(k)
                    enter(slot)

        for q in range(len(groups[0])):
            k = functools.reduce(lambda a, g: jnp.where(turn == g, groups[g][q], a), range(1, ng), groups[0][q])
            slot = back_by(z, k, d.nz)
            score(pair * 2, slot)
            score(pair * 2 + 1, slot)
        return carry

    def late_steps(step, carry):
        k = hops_of(step)
        slot = back_by(z, k, d.nz)
        users_arrive(k, slot)
        enter(slot)
        for j in range(d.nj):
            score(j, slot)
        return carry

    enter(z)
    set_bias(0)
    score(0, z)
    vec_arrives(1)
    set_bias(1)
    score(1, z)
    lax.fori_loop(0, ng, early_steps, 0)
    vec_arrives(2)
    launch("vecs3", functools.partial(vecs_copy, 3))
    launch("valid3", functools.partial(valid_copy, 3))
    set_bias(2)
    score(2, z)
    vec_arrives(3)
    set_bias(3)
    score(3, z)
    lax.fori_loop(ng, 2 * ng, early_steps, 0)
    lax.fori_loop(first, d.nz, late_steps, 0)

    def merge(logs):
        peak = functools.reduce(jnp.maximum, logs)
        return peak + jnp.log(sum(jnp.exp(v - peak) for v in logs))

    peak8 = functools.reduce(jnp.maximum, [peak_s[c] for c in range(d.nk)])
    peak = jnp.max(peak8, axis=0, keepdims=True)
    total8 = sum(total_s[c] * jnp.exp(peak_s[c] - peak) for c in range(d.nk))
    st_own[...] = peak + jnp.log(jnp.maximum(jnp.sum(total8, axis=0, keepdims=True), 1e-30))

    def st_a_copy(k):
        return remote(st_own, st_a.at[k], sa_s.at[k], sa_r.at[k], group_dev(k))

    def st_b_copy(k):
        return remote(st_own2, st_b.at[k], sb_s.at[k], sb_r.at[k], z_dev(k))

    fly("st_a", d.ng, st_a_copy)
    for j in range(d.nj):
        vec_t[:, j * ib : (j + 1) * ib] = vecs[j].astype(F32).T.astype(BF16)

    pre = slope[...]
    sigma = jax.nn.sigmoid(pre)
    slope[...] = sigma * (1.0 + pre * (1.0 - sigma))
    land("st_a")
    st_own2[...] = merge([st_own[...]] + [st_a[k] for k in range(1, d.ng)])
    fly("st_b", d.nz, st_b_copy)
    land("st_b")
    log_total = merge([st_own2[...]] + [st_b[k] for k in range(1, d.nz)])
    for c in range(d.nk):
        factor[c] = weight_s[...] * jnp.exp(peak_s[c] - log_total)

    def gv_copy(j):
        return remote(gv_send.at[j], gv_recv.at[j], gv_s.at[j], gv_r.at[j], across if j == 2 else sibling)

    width = min(512, d.users)
    per = ib // d.chunk

    def grads(t, carry):
        j = 3 - t
        rows = pl.ds(pl.multiple_of(j * ib, ib), ib)
        acc = jnp.zeros((ib, emb), F32)
        tile = lax.broadcasted_iota(jnp.int32, (ib // 8, 8, width), 0)
        for u in range(0, d.users, width):
            lanes = slice(u, u + width)
            e = expo[rows, lanes].reshape(per, d.chunk // 8, 8, width)
            e = (e * factor[pl.ds(j * per, per), :, lanes][:, None]).reshape(ib // 8, 8, width)
            hit = tile == (tile_s[:, lanes] - j * (ib // 8))[None]
            g = jnp.where(hit, e - weight_s[:, lanes][None], e).reshape(ib, width).astype(BF16)
            grad[rows, lanes] = g
            acc = acc + dot(g, users[...].reshape(d.users, emb)[lanes, :])
        gv_own[...] = acc

        for at, i in ((0, 3), (2, 1)):

            @pl.when(t == at)
            def _():
                gv_send[i] = gv_own[...].astype(BF16)
                launch(f"gv{i}", functools.partial(gv_copy, i))

        @pl.when(t == 1)
        def _():
            arrive("gv3")
            gv_send[2] = (gv_own[...] + gv_recv[3].astype(F32)).astype(BF16)
            launch("gv2", functools.partial(gv_copy, 2))

        return carry

    lax.fori_loop(0, 4, grads, 0)

    us = ub // d.ng

    def gu_copy(k):
        to = lax.rem(item + k, d.ng)
        return remote(gu_send.at[to], gu_recv.at[k], gu_s.at[k], gu_r.at[k], dev(to, xl, z, core))

    def user_terms(i, carry):
        lanes = pl.ds(pl.multiple_of(i * width, width), width)
        terms = dot(vec_t[...], grad[:, lanes]).T.astype(BF16)
        for q in range(width // us):
            at = q % d.ng
            gu_send[at, i * (width // ub) + q // d.ng] = terms[q * us : (q + 1) * us, :]
        return carry

    lax.fori_loop(0, d.users // width, user_terms, 0)
    fly("gu", d.ng, gu_copy)

    arrive("gv1")
    arrive("gv2")
    gv = gv_own[...] + gv_recv[1].astype(F32) + gv_recv[2].astype(F32)
    gv = gv.astype(BF16)
    gv_own[...] = gv.astype(F32)
    gv_t = gv_own[...].T.astype(BF16)
    hc = hid // 2
    mine = pl.ds(pl.multiple_of(core * hc, hc), hc)
    other = pl.ds(pl.multiple_of((1 - core) * hc, hc), hc)

    def wc_copy(m):
        return remote(wc_send.at[m], wc_recv.at[m], wc_s.at[m], wc_r.at[m], sibling)

    wg_own[1] = dot(gv_t, hidden[...])
    wc_send[1] = wg_own[1, :, other].astype(BF16)
    launch("wc1", functools.partial(wc_copy, 1))

    pre = (dot_t(gv, w_out[...]) * slope[...]).astype(BF16)
    hidden[...] = pre
    wg_own[0] = dot(feats[...].astype(F32).T.astype(BF16), pre)
    wc_send[0] = wg_own[0, :, other].astype(BF16)
    launch("wc0", functools.partial(wc_copy, 0))

    sr, sc = d.srows, d.scols
    cols = hc // sc

    def w1_copy(m, k):
        p = plane_peer(k)
        return remote(w1_send.at[m, p], w1_recv.at[m, k], w1_s.at[m, k], w1_r.at[m, k], plane_dev(p))

    for m in (1, 0):
        arrive(f"wc{m}")
        total = (wg_own[m, :, mine] + wc_recv[m].astype(F32)).astype(BF16)
        for c in range(cols):
            rows = slice(c * d.np // cols, (c + 1) * d.np // cols)
            w1_send[m, rows] = total[:, c * sc : (c + 1) * sc].reshape(d.np // cols, sr, sc)
        fly(f"w1{m}", d.np, functools.partial(w1_copy, m))
    out_item[...] = gv_own[...] + dot_t(hidden[...], w_in[...])

    land("gu")
    gu_sum[...] = gu_send[item].astype(F32) + sum(gu_recv[k].astype(F32) for k in range(1, d.ng))

    def g2_copy(k):
        return remote(gu_sum.at[z_peer(k)], gu2_recv.at[k], g2_s.at[k], g2_r.at[k], z_dev(k))

    fly("g2", d.nz, g2_copy)
    def wz_copy(m, k, slot):
        there = wz.at[m, slot]
        return remote(there, there, wz_s.at[m, k], wz_r.at[m, k], z_dev(k))

    for m in (1, 0):
        land(f"w1{m}")
        part = w1_send[m, plane].astype(F32)
        for k in range(1, d.np):
            part = part + w1_recv[m, k].astype(F32)
        wz[m, z] = part.astype(BF16)
        fly(
            f"wz{m}",
            d.nz,
            lambda k, m=m: wz_copy(m, k, z),
            lambda k, m=m: wz_copy(m, k, back_by(z, k, d.nz)),
        )

    land("g2")
    mine = gu_sum[z]
    for k in range(1, d.nz):
        mine = mine + gu2_recv[k]
    gu_out[item] = mine

    def g3_copy(k, slot):
        return remote(gu_out.at[slot], gu_out.at[slot], g3_s.at[k], g3_r.at[k], group_dev(k))

    fly("g3", d.ng, lambda k: g3_copy(k, item), lambda k: g3_copy(k, back_by(item, k, d.ng)))

    def w4_copy(m, k, slot):
        there = a1.at[core, m, slot]
        return remote(there, there, w4_s.at[m, k], w4_r.at[m, k], plane_dev(plane_peer(k)))

    def w5_copy(m, k, slot, of):
        there = a1.at[of, m, slot]
        return remote(there, there, w5_s.at[m, k], w5_r.at[m, k], sibling)

    for m in (1, 0):
        land(f"wz{m}")
        a1[core, m, plane] = sum(wz[m, k].astype(F32) for k in range(d.nz)).astype(BF16)
        fly(
            f"w4{m}",
            d.np,
            lambda k, m=m: w4_copy(m, k, plane),
            lambda k, m=m: w4_copy(m, k, back_by(plane, k, d.np)),
        )
        w5_copy(m, 0, plane, core).start()

    def hand_on(m, k):
        slot = back_by(plane, k, d.np)
        w4_copy(m, k, slot).wait_recv()
        w5_copy(m, k, slot, core).start()

    for m in (1, 0):
        each(d.np, functools.partial(hand_on, m))
        flights[f"w4{m}"][3] = True
    land("g3")
    out_user[...] = gu_out[...].reshape(ub, emb)
    for m in (1, 0):
        w5_copy(m, 0, plane, 1 - core).wait_recv()
        each(d.np, lambda k: w5_copy(m, k, back_by(plane, k, d.np), 1 - core).wait_recv())
    out_w[...] = a1[...]

    finish()
    for m in (1, 0):
        w5_copy(m, 0, plane, core).wait_send()
        each(d.np, lambda k: w5_copy(m, k, back_by(plane, k, d.np), core).wait_send())


def unpack(d, user_ref, item_ref, w_ref, out_user, out_item, out_w_in, out_w_out):
    out_user[...] = user_ref[...]
    out_item[...] = item_ref[...]
    hc, sc = d.hid // 2, d.scols
    cols = hc // sc
    for half in range(2):
        for c in range(cols):
            parts = slice(c * d.np // cols, (c + 1) * d.np // cols)
            at = slice(half * hc + c * sc, half * hc + (c + 1) * sc)
            out_w_in[:, at] = w_ref[half, 0, parts].astype(F32).reshape(d.emb, sc)
            out_w_out[at, :] = w_ref[half, 1, parts].astype(F32).reshape(d.emb, sc).T


def body(phys, user_vecs, row_weight, positive, item_feats, valid, w_in, w_out):
    ub, emb = user_vecs.shape
    ib, hid = item_feats.shape[0], w_in.shape[1]
    d = Dims(phys, ub, ib, emb, hid)
    vm = pltpu.VMEM
    us = ub // d.ng
    scratch = [
        vm((ib, emb), BF16),
        vm((emb, hid), BF16),
        vm((hid, emb), BF16),
        vm((d.nz, ub, emb), BF16),
        vm((d.nz, 2, ub), F32),
        vm((d.nj, ib, emb), BF16),
        vm((d.nj, 1, ib), F32),
        vm((d.nj, ib, 128), F32),
        vm((emb, d.items), BF16),
        vm((ib, hid), BF16),
        vm((ib, hid), F32),
        vm((d.items, d.users), F32),
        vm((d.items, d.users), BF16),
        vm((d.nk, 8, d.users), F32),
        vm((d.nk, 8, d.users), F32),
        vm((d.nk, 8, d.users), F32),
        vm((8, d.users), jnp.int32),
        vm((1, d.users), F32),
        vm((1, d.users), F32),
        vm((d.ng, 1, d.users), F32),
        vm((1, d.users), F32),
        vm((d.nz, 1, d.users), F32),
        vm((d.nj, ib, emb), BF16),
        vm((d.nj, ib, emb), BF16),
        vm((ib, emb), F32),
        vm((d.ng, d.nz, us, emb), BF16),
        vm((d.ng, d.nz, us, emb), BF16),
        vm((d.nz, us, emb), F32),
        vm((d.nz, us, emb), F32),
        vm((d.ng, us, emb), F32),
        vm((2, emb, hid), F32),
        vm((2, emb, hid // 2), BF16),
        vm((2, emb, hid // 2), BF16),
        vm((2, d.np, d.srows, d.scols), BF16),
        vm((2, d.np, d.srows, d.scols), BF16),
        vm((2, d.nz, d.srows, d.scols), BF16),
        vm((2, 2, d.np, d.srows, d.scols), BF16),
    ]
    dma = pltpu.SemaphoreType.DMA
    sems = [dma((4,))]
    for n in (d.nz, d.nz, d.nj, d.nj, d.ng, d.nz, d.nj, d.ng, d.nz, d.ng, 2):
        sems += [dma((n,)), dma((n,))]
    for n in (d.np, d.nz, d.np, d.np):
        sems += [dma((2, n)), dma((2, n))]
    whole = pl.BlockSpec(memory_space=pltpu.VMEM)
    where = pl.BlockSpec(memory_space=pl.ANY)
    parts = pl.pallas_call(
        functools.partial(kernel, d),
        out_shape=(
            jax.ShapeDtypeStruct((ub, emb), F32),
            jax.ShapeDtypeStruct((ib, emb), F32),
            jax.ShapeDtypeStruct((2, 2, d.np, d.srows, d.scols), BF16),
        ),
        in_specs=[where, whole, whole, where, whole, where, where],
        out_specs=(whole,) * 3,
        scratch_shapes=scratch + sems,
        compiler_params=pltpu.CompilerParams(
            collective_id=0, has_side_effects=True, vmem_limit_bytes=56 * 1024 * 1024
        ),
        cost_estimate=pl.CostEstimate(
            flops=6 * d.users * d.items * emb,
            bytes_accessed=4 * 1024 * 1024,
            transcendentals=d.users * d.items,
        ),
    )(user_vecs, row_weight, positive, item_feats, valid, w_in, w_out)
    return pl.pallas_call(
        functools.partial(unpack, d),
        out_shape=(
            jax.ShapeDtypeStruct((ub, emb), F32),
            jax.ShapeDtypeStruct((ib, emb), F32),
            jax.ShapeDtypeStruct((emb, hid), F32),
            jax.ShapeDtypeStruct((hid, emb), F32),
        ),
        in_specs=[whole] * 3,
        out_specs=(whole,) * 4,
    )(*parts)


def build(mesh, phys):
    return jax.shard_map(
        functools.partial(body, phys),
        mesh=mesh,
        in_specs=(
            P("user", None),
            P("user"),
            P("user"),
            P(("item", "user"), None),
            P(("item", "user")),
            P(),
            P(),
        ),
        out_specs=(P("user", None), P(("item", "user"), None), P(), P()),
        check_vma=False,
    )


def solution(mesh):
    return build(mesh, (4, 2, 2, 8, 2))
```

```python
import functools

import jax
import jax.numpy as jnp
from jax import lax
from jax.experimental import pallas as pl
from jax.experimental.pallas import tpu as pltpu
from jax.sharding import PartitionSpec as P

MESH = pl.DeviceIdType.MESH
F32 = jnp.float32
BF16 = jnp.bfloat16
DEAD = -1e30
FLOOR = -1e29


def dot(a, b):
    return jnp.dot(a, b, preferred_element_type=F32)


def dot_t(a, b):
    return lax.dot_general(a, b, (((1,), (1,)), ((), ())), preferred_element_type=F32)


class Dims:
    def __init__(self, phys, ub, ib, emb, hid):
        self.ny, self.nxh, self.nxl, self.nz, self.nc = phys
        self.ub, self.ib, self.emb, self.hid = ub, ib, emb, hid
        self.ng = self.ny * self.nxh
        self.np = self.ng * self.nxl
        self.nj = self.nxl * self.nc
        self.users = self.nz * ub
        self.items = self.nj * ib
        self.chunk = min(256, ib)
        self.nk = self.items // self.chunk
        self.srows = 2 * emb // self.np
        self.scols = hid // 2
        self.groups = min(4, self.np)


def kernel(
    d,
    users_in, weight_in, pos_in, feats_in, valid_in, w_in_in, w_out_in,
    out_user, out_item, out_w,
    feats, w_in, w_out, weight_v, pos_v, valid_v, item_v, users, meta, vecs, valid, bias, vec_t, hidden, slope, expo, grad,
    peak_s, total_s, factor, tile_s, weight_s,
    st_own, st_a, st_own2, st_b,
    gv_send, gv_recv, gv_own, gu_send, gu_recv, gu_sum, gu2_recv, gu_out,
    wg_own, wc_send, wc_recv, w1_send, w1_recv, wz, a1,
    in_s, out_s, us_s, us_r, me_s, me_r, ve_s, ve_r, va_s, va_r, sa_s, sa_r, sb_s, sb_r,
    gv_s, gv_r, gu_s, gu_r, g2_s, g2_r, g3_s, g3_r,
    wc_s, wc_r, w1_s, w1_r, wz_s, wz_r, w4_s, w4_r, w5_s, w5_r,
):
    ub, ib, emb, hid = d.ub, d.ib, d.emb, d.hid
    item = lax.axis_index("item")
    user = lax.axis_index("user")
    core = lax.rem(user, d.nc)
    z = lax.rem(lax.div(user, d.nc), d.nz)
    xl = lax.div(user, d.nc * d.nz)
    plane = item * d.nxl + xl

    def dev(item_, xl_, z_, core_):
        return (item_, (xl_ * d.nz + z_) * d.nc + core_)

    def back_by(here, k, n):
        return lax.rem(here + n - k, n)

    def z_peer(k):
        return lax.rem(z + k, d.nz)

    def z_dev(k):
        return dev(item, xl, z_peer(k), core)

    def group_dev(k):
        return dev(lax.rem(item + k, d.ng), xl, z, core)

    def plane_peer(k):
        return lax.rem(plane + k, d.np)

    def plane_dev(p):
        return dev(lax.div(p, d.nxl), lax.rem(p, d.nxl), z, core)

    sibling = dev(item, xl, z, 1 - core)
    across = dev(item, 1 - xl, z, core)

    def remote(src, dst, send, recv, to):
        return pltpu.make_async_remote_copy(
            src_ref=src, dst_ref=dst, send_sem=send, recv_sem=recv, device_id=to, device_id_type=MESH
        )

    def each(n, fn):
        def step(k, carry):
            fn(k)
            return carry

        lax.fori_loop(1, n, step, 0)

    flights = {}

    def fly(name, n, copy_out, copy_in=None, start=True):
        flights[name] = [n, copy_out, copy_in or copy_out, False]
        if start:
            each(n, lambda k: copy_out(k).start())

    def land(name):
        n, _, copy_in, _ = flights[name]
        each(n, lambda k: copy_in(k).wait_recv())
        flights[name][3] = True

    def sent(*names):
        for name in names:
            if name in flights:
                n, copy_out, _, landed = flights.pop(name)
                each(n, lambda k: copy_out(k).wait_send())
            else:
                make, landed = singles.pop(name)
                make().wait_send()

    tails = []
    singles = {}

    def launch(name, make):
        singles[name] = [make, False]
        make().start()

    def arrive(name):
        singles[name][0]().wait_recv()
        singles[name][1] = True

    def finish():
        for wait in tails:
            wait()
        for name in list(flights):
            if not flights[name][3]:
                land(name)
            sent(name)
        for name in list(singles):
            if not singles[name][1]:
                arrive(name)
            sent(name)

    inputs = [(feats_in, feats), (w_in_in, w_in), (w_out_in, w_out), (users_in, users.at[z])]
    inputs += [(weight_in, weight_v), (pos_in, pos_v), (valid_in, valid_v)]
    inputs = [pltpu.make_async_copy(src, dst, in_s.at[i]) for i, (src, dst) in enumerate(inputs)]
    for copy in inputs:
        copy.start()

    barrier = pltpu.get_barrier_semaphore()

    def greet(to):
        pl.semaphore_signal(barrier, inc=1, device_id=to, device_id_type=MESH)

    each(d.nz, lambda k: greet(z_dev(k)))
    each(d.np, lambda k: greet(plane_dev(plane_peer(k))))
    greet(sibling)

    for copy in inputs:
        copy.wait()
    pos = pos_v[...].reshape(1, ub)
    meta[z] = jnp.concatenate([pos.astype(F32), weight_v[...].reshape(1, ub).astype(F32)], axis=0)
    valid[0] = valid_v[...].reshape(1, ib).astype(F32)
    x = feats[...]
    pre = dot(x, w_in[...])
    hid_t = (pre * jax.nn.sigmoid(pre)).astype(BF16)
    hidden[...] = hid_t
    slope[...] = pre
    vecs[0] = (x.astype(F32) + dot(hid_t, w_out[...])).astype(BF16)
    pl.semaphore_wait(barrier, d.nz - 1 + d.np - 1 + 1)

    far = d.nz // 2
    direct = [k for k in (2, d.nz - 2, 1, d.nz - 1) if 0 < k < d.nz]
    direct = sorted(set(direct), key=direct.index)
    handed = [k for k in range(1, d.nz) if k not in direct]
    order = [0] + direct + sorted(handed, key=lambda k: k == far)

    def hops_of(step):
        k = 0
        for i in range(1, d.nz):
            k = jnp.where(step == i, order[i], k)
        return k

    def users_copies(k, slot, to):
        there = z_dev(to)
        return [
            remote(users.at[slot], users.at[slot], us_s.at[k], us_r.at[k], there),
            remote(meta.at[slot], meta.at[slot], me_s.at[k], me_r.at[k], there),
        ]

    def users_start(k, slot, to):
        for copy in users_copies(k, slot, to):
            copy.start()

    def users_sent():
        for k in range(1, d.nz):
            for copy in users_copies(k, z, 1):
                copy.wait_send()

    def users_arrive(k, slot):
        for copy in users_copies(k, slot, 1):
            copy.wait_recv()

    def hand_on_users(k):
        slot = back_by(z, k, d.nz)
        ahead = k == 2
        users_start(3 if ahead else d.nz - 3, slot, 1 if ahead else d.nz - 1)

        @pl.when(core == (0 if ahead else 1))
        def _():
            users_start(far, slot, 2 if ahead else d.nz - 2)

    def vecs_copy(j):
        return remote(vecs.at[j // 3 * 2], vecs.at[j], ve_s.at[j], ve_r.at[j], across if j == 2 else sibling)

    def valid_copy(j):
        return remote(valid.at[j // 3 * 2], valid.at[j], va_s.at[j], va_r.at[j], across if j == 2 else sibling)

    for j in (2, 1):
        launch(f"vecs{j}", functools.partial(vecs_copy, j))
        launch(f"valid{j}", functools.partial(valid_copy, j))
    for k in direct:
        users_start(k, z, k)
    tails.append(users_sent)

    def vec_arrives(j):
        arrive(f"vecs{j}")
        arrive(f"valid{j}")

    def local_tile(pos):
        block = pos // ib
        p_core = block % d.nc
        p_z = block // d.nc % d.nz
        p_xl = block // (d.nc * d.nz) % d.nxl
        p_item = block // (d.nc * d.nz * d.nxl)
        j = (p_xl + d.nxl - xl) % d.nxl * d.nc + (p_core + d.nc - core) % d.nc
        here = (p_item == item) & (p_z == z)
        row = jnp.where(here, j * ib + pos % ib, -1)
        lane = lax.broadcasted_iota(jnp.int32, (8, ub), 0)
        return jnp.where(here & (lane == row % 8), row // 8, -1)

    def set_bias(j):
        bias[j] = (jnp.broadcast_to(valid[j], (128, ib)).T - 1.0) * -DEAD

    def enter(slot):
        lanes = pl.ds(pl.multiple_of(slot * ub, ub), ub)
        tile_s[:, lanes] = local_tile(meta[slot, 0:1, :].astype(jnp.int32))
        weight_s[:, lanes] = meta[slot, 1:2, :]

    def score(j, slot):
        at = pl.multiple_of(slot * ub, ub)
        tile = lax.broadcasted_iota(jnp.int32, (d.chunk // 8, 8, 128), 0)
        for c in range(ib // d.chunk):
            rows = slice(c * d.chunk, (c + 1) * d.chunk)
            s = dot_t(vecs[j, rows, :], users[slot])
            b = bias[j, rows, :].reshape(d.chunk // 8, 8, 128)
            ck = j * (ib // d.chunk) + c
            first = pl.multiple_of(ck * d.chunk, d.chunk)
            for h in range(ub // 128):
                lanes = pl.ds(pl.multiple_of(at + h * 128, 128), 128)
                sh = s[:, h * 128 : (h + 1) * 128].reshape(d.chunk // 8, 8, 128)
                hit = tile == (tile_s[:, lanes] - ck * (d.chunk // 8))[None]
                x = jnp.where(hit, sh, sh + b)
                peak = jnp.maximum(jnp.max(x, axis=0), FLOOR)
                e = jnp.exp(x - peak[None])
                peak_s[ck, :, lanes] = peak
                total_s[ck, :, lanes] = jnp.sum(e, axis=0)
                expo[pl.ds(first, d.chunk), lanes] = e.reshape(d.chunk, 128)

    first = min(5, d.nz)
    groups = [order[1:3], order[3:5]] if d.nz >= 5 else [order[1:first]]
    ng = len(groups)

    def early_steps(i, carry):
        pair = lax.div(i, ng)
        turn = lax.rem(i, ng)

        for at, group in enumerate(groups):

            @pl.when(i == at)
            def _():
                for k in group:
                    slot = back_by(z, k, d.nz)
                    users_arrive(k, slot)
                    if handed and k in (2, d.nz - 2):
                        hand_on_users(k)
                    enter(slot)

        for q in range(len(groups[0])):
            k = functools.reduce(lambda a, g: jnp.where(turn == g, groups[g][q], a), range(1, ng), groups[0][q])
            slot = back_by(z, k, d.nz)
            score(pair * 2, slot)
            score(pair * 2 + 1, slot)
        return carry

    def late_steps(step, carry):
        k = hops_of(step)
        slot = back_by(z, k, d.nz)
        users_arrive(k, slot)
        enter(slot)
        for j in range(d.nj):
            score(j, slot)
        return carry

    enter(z)
    set_bias(0)
    score(0, z)
    vec_arrives(1)
    set_bias(1)
    score(1, z)
    lax.fori_loop(0, ng, early_steps, 0)
    vec_arrives(2)
    launch("vecs3", functools.partial(vecs_copy, 3))
    launch("valid3", functools.partial(valid_copy, 3))
    set_bias(2)
    score(2, z)
    vec_arrives(3)
    set_bias(3)
    score(3, z)
    lax.fori_loop(ng, 2 * ng, early_steps, 0)
    lax.fori_loop(first, d.nz, late_steps, 0)

    def merge(logs):
        peak = functools.reduce(jnp.maximum, logs)
        return peak + jnp.log(sum(jnp.exp(v - peak) for v in logs))

    peak8 = functools.reduce(jnp.maximum, [peak_s[c] for c in range(d.nk)])
    peak = jnp.max(peak8, axis=0, keepdims=True)
    total8 = sum(total_s[c] * jnp.exp(peak_s[c] - peak) for c in range(d.nk))
    st_own[...] = peak + jnp.log(jnp.maximum(jnp.sum(total8, axis=0, keepdims=True), 1e-30))

    def st_a_copy(k):
        return remote(st_own, st_a.at[k], sa_s.at[k], sa_r.at[k], group_dev(k))

    def st_b_copy(k):
        return remote(st_own2, st_b.at[k], sb_s.at[k], sb_r.at[k], z_dev(k))

    fly("st_a", d.ng, st_a_copy)
    for j in range(d.nj):
        vec_t[:, j * ib : (j + 1) * ib] = vecs[j].astype(F32).T.astype(BF16)

    pre = slope[...]
    sigma = jax.nn.sigmoid(pre)
    slope[...] = sigma * (1.0 + pre * (1.0 - sigma))
    land("st_a")
    st_own2[...] = merge([st_own[...]] + [st_a[k] for k in range(1, d.ng)])
    fly("st_b", d.nz, st_b_copy)
    land("st_b")
    log_total = merge([st_own2[...]] + [st_b[k] for k in range(1, d.nz)])
    for c in range(d.nk):
        factor[c] = weight_s[...] * jnp.exp(peak_s[c] - log_total)

    def gv_copy(j):
        return remote(gv_send.at[j], gv_recv.at[j], gv_s.at[j], gv_r.at[j], across if j == 2 else sibling)

    width = min(512, d.users)
    per = ib // d.chunk

    def grads(t, carry):
        j = 3 - t
        rows = pl.ds(pl.multiple_of(j * ib, ib), ib)
        acc = jnp.zeros((ib, emb), F32)
        tile = lax.broadcasted_iota(jnp.int32, (ib // 8, 8, width), 0)
        for u in range(0, d.users, width):
            lanes = slice(u, u + width)
            e = expo[rows, lanes].reshape(per, d.chunk // 8, 8, width)
            e = (e * factor[pl.ds(j * per, per), :, lanes][:, None]).reshape(ib // 8, 8, width)
            hit = tile == (tile_s[:, lanes] - j * (ib // 8))[None]
            g = jnp.where(hit, e - weight_s[:, lanes][None], e).reshape(ib, width).astype(BF16)
            grad[rows, lanes] = g
            acc = acc + dot(g, users[...].reshape(d.users, emb)[lanes, :])
        gv_own[...] = acc

        for at, i in ((0, 3), (2, 1)):

            @pl.when(t == at)
            def _():
                gv_send[i] = gv_own[...].astype(BF16)
                launch(f"gv{i}", functools.partial(gv_copy, i))

        @pl.when(t == 1)
        def _():
            arrive("gv3")
            gv_send[2] = (gv_own[...] + gv_recv[3].astype(F32)).astype(BF16)
            launch("gv2", functools.partial(gv_copy, 2))

        return carry

    lax.fori_loop(0, 4, grads, 0)

    us = ub // d.ng
    zs = width // ub
    turns = d.users // width
    offsets = sorted(range(turns), key=lambda o: -min(o, turns - o))

    def gu_copy(k):
        return remote(gu_send.at[z_peer(k)], gu_recv.at[k], gu_s.at[k], gu_r.at[k], z_dev(k))

    def user_terms(i, carry):
        offset = functools.reduce(lambda a, t: jnp.where(i == t, offsets[t], a), range(1, turns), offsets[0])
        q = lax.rem(lax.div(z, zs) + offset, turns)
        lanes = pl.ds(pl.multiple_of(q * width, width), width)
        terms = dot(vec_t[...], grad[:, lanes]).T
        for e in range(zs):
            slot = q * zs + e
            part = terms[e * ub : (e + 1) * ub, :]

            @pl.when(slot == z)
            def _():
                gu_sum[...] = part

            @pl.when(slot != z)
            def _():
                gu_send[slot] = part.astype(BF16)
                gu_copy(back_by(slot, z, d.nz)).start()

        return carry

    fly("gu", d.nz, gu_copy, start=False)
    lax.fori_loop(0, turns, user_terms, 0)

    arrive("gv1")
    arrive("gv2")
    gv = gv_own[...] + gv_recv[1].astype(F32) + gv_recv[2].astype(F32)
    gv = gv.astype(BF16)
    gv_own[...] = gv.astype(F32)
    gv_t = gv_own[...].T.astype(BF16)
    hc = hid // 2
    mine = pl.ds(pl.multiple_of(core * hc, hc), hc)
    other = pl.ds(pl.multiple_of((1 - core) * hc, hc), hc)

    def wc_copy(m):
        return remote(wc_send.at[m], wc_recv.at[m], wc_s.at[m], wc_r.at[m], sibling)

    wg_own[1] = dot(gv_t, hidden[...])
    wc_send[1] = wg_own[1, :, other].astype(BF16)
    launch("wc1", functools.partial(wc_copy, 1))

    pre = (dot_t(gv, w_out[...]) * slope[...]).astype(BF16)
    hidden[...] = pre
    wg_own[0] = dot(feats[...].astype(F32).T.astype(BF16), pre)
    wc_send[0] = wg_own[0, :, other].astype(BF16)
    launch("wc0", functools.partial(wc_copy, 0))

    sr = d.srows
    half = d.np // 2

    def w1_copy(k):
        p = plane_peer(k)
        return remote(w1_send.at[p], w1_recv.at[k], w1_s.at[k], w1_r.at[k], plane_dev(p))

    for m in (1, 0):
        arrive(f"wc{m}")
        total = (wg_own[m, :, mine] + wc_recv[m].astype(F32)).astype(BF16)
        w1_send[m * half : (m + 1) * half] = total.reshape(half, sr, hc)
    fly("w1", d.np, w1_copy)

    def out_copy(i):
        pairs = [(item_v, out_item), (gu_out, out_user), (a1.at[core], out_w.at[core]), (a1.at[1 - core], out_w.at[1 - core])]
        return pltpu.make_async_copy(*pairs[i], out_s.at[i])

    item_v[...] = gv_own[...] + dot_t(hidden[...], w_in[...])
    out_copy(0).start()
    tails.append(lambda: out_copy(0).wait())
    tails.remove(users_sent)
    users_sent()
    sent("vecs1", "vecs2", "vecs3", "valid1", "valid2", "valid3", "st_a", "st_b")
    sent("gv1", "gv2", "gv3", "wc0", "wc1")
    land("w1")
    part = w1_send[plane].astype(F32)
    for k in range(1, d.np):
        part = part + w1_recv[k].astype(F32)
    wz[z] = part.astype(BF16)

    def wz_copy(k, slot):
        return remote(wz.at[slot], wz.at[slot], wz_s.at[k], wz_r.at[k], z_dev(k))

    fly("wz", d.nz, lambda k: wz_copy(k, z), lambda k: wz_copy(k, back_by(z, k, d.nz)))

    land("gu")
    gu_sum[...] += sum(gu_recv[k].astype(F32) for k in range(1, d.nz))

    def rows_of(i):
        return pl.ds(pl.multiple_of(i * us, us), us)

    def g2_copy(k):
        to = lax.rem(item + k, d.ng)
        return remote(gu_sum.at[rows_of(to), :], gu2_recv.at[k], g2_s.at[k], g2_r.at[k], group_dev(k))

    fly("g2", d.ng, g2_copy)
    sent("w1", "gu")
    land("wz")
    a1[core, plane] = sum(wz[k].astype(F32) for k in range(d.nz)).astype(BF16)

    def w4_copy(k, slot):
        there = a1.at[core, slot]
        return remote(there, there, w4_s.at[k], w4_r.at[k], plane_dev(plane_peer(k)))

    fly("w4", d.np, lambda k: w4_copy(k, plane), lambda k: w4_copy(k, back_by(plane, k, d.np)))

    land("g2")
    gu_out[rows_of(item), :] = gu_sum[rows_of(item), :] + sum(gu2_recv[k] for k in range(1, d.ng))

    def g3_copy(k, at):
        there = gu_out.at[rows_of(at), :]
        return remote(there, there, g3_s.at[k], g3_r.at[k], group_dev(k))

    fly("g3", d.ng, lambda k: g3_copy(k, item), lambda k: g3_copy(k, back_by(item, k, d.ng)))
    sent("wz", "g2")

    per_group = d.np // d.groups

    def w5_copy(g, of):
        there = a1.at[of, pl.ds(g * per_group, per_group)]
        return remote(there, there, w5_s.at[g], w5_r.at[g], sibling)

    for g in range(d.groups):
        for slot in range(g * per_group, (g + 1) * per_group):

            @pl.when(slot != plane)
            def _():
                w4_copy(back_by(plane, slot, d.np), slot).wait_recv()

        w5_copy(g, core).start()
    flights["w4"][3] = True
    out_copy(2).start()
    land("g3")
    out_copy(1).start()
    for g in range(d.groups):
        w5_copy(g, 1 - core).wait_recv()
    out_copy(3).start()

    finish()
    for g in range(d.groups):
        w5_copy(g, core).wait_send()
    for i in (1, 2, 3):
        out_copy(i).wait()


def unpack(d, user_ref, item_ref, w_ref, out_user, out_item, out_w_in, out_w_out, w_v, w_in_v, w_out_v, sems):
    half, hc = d.np // 2, d.scols
    copies = [pltpu.make_async_copy(w_ref.at[h, m], w_v.at[h, m], sems.at[2 * h + m]) for h in range(2) for m in range(2)]
    copies += [
        pltpu.make_async_copy(user_ref, out_user, sems.at[4]),
        pltpu.make_async_copy(item_ref, out_item, sems.at[5]),
    ]
    for copy in copies:
        copy.start()
    results = [
        pltpu.make_async_copy(w_in_v, out_w_in, sems.at[6]),
        pltpu.make_async_copy(w_out_v, out_w_out, sems.at[7]),
    ]
    for m in (1, 0):
        for h in range(2):
            copies[2 * h + m].wait()
            block = w_v[h, m].astype(F32).reshape(d.emb, hc)
            at = slice(h * hc, (h + 1) * hc)
            if m == 0:
                w_in_v[:, at] = block
            else:
                w_out_v[at, :] = block.T
        results[m].start()
    for copy in copies[4:] + results:
        copy.wait()


def body(phys, user_vecs, row_weight, positive, item_feats, valid, w_in, w_out):
    ub, emb = user_vecs.shape
    ib, hid = item_feats.shape[0], w_in.shape[1]
    d = Dims(phys, ub, ib, emb, hid)
    vm = pltpu.VMEM
    us = ub // d.ng
    scratch = [
        vm((ib, emb), BF16),
        vm((emb, hid), BF16),
        vm((hid, emb), BF16),
        vm((ub,), BF16),
        vm((ub,), jnp.int32),
        vm((ib,), jnp.int32),
        vm((ib, emb), F32),
        vm((d.nz, ub, emb), BF16),
        vm((d.nz, 2, ub), F32),
        vm((d.nj, ib, emb), BF16),
        vm((d.nj, 1, ib), F32),
        vm((d.nj, ib, 128), F32),
        vm((emb, d.items), BF16),
        vm((ib, hid), BF16),
        vm((ib, hid), F32),
        vm((d.items, d.users), F32),
        vm((d.items, d.users), BF16),
        vm((d.nk, 8, d.users), F32),
        vm((d.nk, 8, d.users), F32),
        vm((d.nk, 8, d.users), F32),
        vm((8, d.users), jnp.int32),
        vm((1, d.users), F32),
        vm((1, d.users), F32),
        vm((d.ng, 1, d.users), F32),
        vm((1, d.users), F32),
        vm((d.nz, 1, d.users), F32),
        vm((d.nj, ib, emb), BF16),
        vm((d.nj, ib, emb), BF16),
        vm((ib, emb), F32),
        vm((d.nz, ub, emb), BF16),
        vm((d.nz, ub, emb), BF16),
        vm((ub, emb), F32),
        vm((d.ng, us, emb), F32),
        vm((ub, emb), F32),
        vm((2, emb, hid), F32),
        vm((2, emb, hid // 2), BF16),
        vm((2, emb, hid // 2), BF16),
        vm((d.np, d.srows, d.scols), BF16),
        vm((d.np, d.srows, d.scols), BF16),
        vm((d.nz, d.srows, d.scols), BF16),
        vm((2, d.np, d.srows, d.scols), BF16),
    ]
    dma = pltpu.SemaphoreType.DMA
    sems = [dma((7,)), dma((4,))]
    for n in (d.nz, d.nz, d.nj, d.nj, d.ng, d.nz, d.nj, d.nz, d.ng, d.ng, 2, d.np, d.nz, d.np, d.groups):
        sems += [dma((n,)), dma((n,))]
    where = pl.BlockSpec(memory_space=pl.ANY)
    parts = pl.pallas_call(
        functools.partial(kernel, d),
        out_shape=(
            jax.ShapeDtypeStruct((ub, emb), F32),
            jax.ShapeDtypeStruct((ib, emb), F32),
            jax.ShapeDtypeStruct((2, d.np, d.srows, d.scols), BF16),
        ),
        in_specs=[where] * 7,
        out_specs=(where,) * 3,
        scratch_shapes=scratch + sems,
        compiler_params=pltpu.CompilerParams(
            collective_id=0, has_side_effects=True, vmem_limit_bytes=56 * 1024 * 1024
        ),
        cost_estimate=pl.CostEstimate(
            flops=6 * d.users * d.items * emb,
            bytes_accessed=4 * 1024 * 1024,
            transcendentals=d.users * d.items,
        ),
    )(user_vecs, row_weight, positive, item_feats, valid, w_in, w_out)
    user, item, weights = parts
    weights = weights.reshape(2, 2, d.np // 2, d.srows, d.scols)
    return pl.pallas_call(
        functools.partial(unpack, d),
        out_shape=(
            jax.ShapeDtypeStruct((ub, emb), F32),
            jax.ShapeDtypeStruct((ib, emb), F32),
            jax.ShapeDtypeStruct((emb, hid), F32),
            jax.ShapeDtypeStruct((hid, emb), F32),
        ),
        in_specs=[where] * 3,
        out_specs=(where,) * 4,
        scratch_shapes=[
            vm(weights.shape, BF16),
            vm((emb, hid), F32),
            vm((hid, emb), F32),
            dma((8,)),
        ],
    )(user, item, weights)


def build(mesh, phys):
    return jax.shard_map(
        functools.partial(body, phys),
        mesh=mesh,
        in_specs=(
            P("user", None),
            P("user"),
            P("user"),
            P(("item", "user"), None),
            P(("item", "user")),
            P(),
            P(),
        ),
        out_specs=(P("user", None), P(("item", "user"), None), P(), P()),
        check_vma=False,
    )


def solution(mesh):
    return build(mesh, (4, 2, 2, 8, 2))
```

```python
import functools

import jax
import jax.numpy as jnp
from jax import lax
from jax.experimental import pallas as pl
from jax.experimental.pallas import tpu as pltpu
from jax.sharding import PartitionSpec as P

MESH = pl.DeviceIdType.MESH
F32 = jnp.float32
BF16 = jnp.bfloat16
DEAD = -1e30
FLOOR = -1e29


def dot(a, b):
    return jnp.dot(a, b, preferred_element_type=F32)


def dot_t(a, b):
    return lax.dot_general(a, b, (((1,), (1,)), ((), ())), preferred_element_type=F32)


class Dims:
    def __init__(self, phys, ub, ib, emb, hid):
        self.ny, self.nxh, self.nxl, self.nz, self.nc = phys
        self.ub, self.ib, self.emb, self.hid = ub, ib, emb, hid
        self.ng = self.ny * self.nxh
        self.np = self.ng * self.nxl
        self.nj = self.nxl * self.nc
        self.users = self.nz * ub
        self.items = self.nj * ib
        self.chunk = min(256, ib)
        self.nk = self.items // self.chunk
        self.srows = 2 * emb // self.np
        self.scols = hid // 2
        self.groups = min(4, self.np)


def kernel(
    d,
    users_in, weight_in, pos_in, feats_in, valid_in, w_in_in, w_out_in,
    out_user, out_item, out_w,
    feats, w_in, w_out, weight_v, pos_v, valid_v, item_v, users, meta, vecs, valid, bias, vec_t, hidden, slope, expo, grad,
    peak_s, total_s, factor, tile_s, weight_s,
    st_own, st_a, st_own2, st_b,
    gv_send, gv_recv, gv_own, gu_send, gu_recv, gu_sum, gu2_recv, gu_out,
    wg_own, wc_send, wc_recv, w1_send, w1_recv, wz, a1,
    in_s, out_s, us_s, us_r, me_s, me_r, ve_s, ve_r, va_s, va_r, sa_s, sa_r, sb_s, sb_r,
    gv_s, gv_r, gu_s, gu_r, g2_s, g2_r, g3_s, g3_r,
    wc_s, wc_r, w1_s, w1_r, wz_s, wz_r, w4_s, w4_r, w5_s, w5_r,
):
    ub, ib, emb, hid = d.ub, d.ib, d.emb, d.hid
    item = lax.axis_index("item")
    user = lax.axis_index("user")
    core = lax.rem(user, d.nc)
    z = lax.rem(lax.div(user, d.nc), d.nz)
    xl = lax.div(user, d.nc * d.nz)
    plane = item * d.nxl + xl

    def dev(item_, xl_, z_, core_):
        return (item_, (xl_ * d.nz + z_) * d.nc + core_)

    def back_by(here, k, n):
        return lax.rem(here + n - k, n)

    def z_peer(k):
        return lax.rem(z + k, d.nz)

    def z_dev(k):
        return dev(item, xl, z_peer(k), core)

    def group_dev(k):
        return dev(lax.rem(item + k, d.ng), xl, z, core)

    def plane_peer(k):
        return lax.rem(plane + k, d.np)

    def plane_dev(p):
        return dev(lax.div(p, d.nxl), lax.rem(p, d.nxl), z, core)

    sibling = dev(item, xl, z, 1 - core)
    across = dev(item, 1 - xl, z, core)

    def remote(src, dst, send, recv, to):
        return pltpu.make_async_remote_copy(
            src_ref=src, dst_ref=dst, send_sem=send, recv_sem=recv, device_id=to, device_id_type=MESH
        )

    def each(n, fn):
        def step(k, carry):
            fn(k)
            return carry

        lax.fori_loop(1, n, step, 0)

    flights = {}

    def fly(name, n, copy_out, copy_in=None, start=True):
        flights[name] = [n, copy_out, copy_in or copy_out, False]
        if start:
            each(n, lambda k: copy_out(k).start())

    def land(name):
        n, _, copy_in, _ = flights[name]
        each(n, lambda k: copy_in(k).wait_recv())
        flights[name][3] = True

    def sent(*names):
        for name in names:
            if name in flights:
                n, copy_out, _, landed = flights.pop(name)
                each(n, lambda k: copy_out(k).wait_send())
            else:
                make, landed = singles.pop(name)
                make().wait_send()

    tails = []
    singles = {}

    def launch(name, make):
        singles[name] = [make, False]
        make().start()

    def arrive(name):
        singles[name][0]().wait_recv()
        singles[name][1] = True

    def finish():
        for wait in tails:
            wait()
        for name in list(flights):
            if not flights[name][3]:
                land(name)
            sent(name)
        for name in list(singles):
            if not singles[name][1]:
                arrive(name)
            sent(name)

    inputs = [(feats_in, feats), (w_in_in, w_in), (w_out_in, w_out), (users_in, users.at[z])]
    inputs += [(weight_in, weight_v), (pos_in, pos_v), (valid_in, valid_v)]
    inputs = [pltpu.make_async_copy(src, dst, in_s.at[i]) for i, (src, dst) in enumerate(inputs)]
    for copy in inputs:
        copy.start()

    barrier = pltpu.get_barrier_semaphore()

    def greet(to):
        pl.semaphore_signal(barrier, inc=1, device_id=to, device_id_type=MESH)

    each(d.nz, lambda k: greet(z_dev(k)))
    each(d.np, lambda k: greet(plane_dev(plane_peer(k))))
    greet(sibling)

    for copy in inputs:
        copy.wait()
    pos = pos_v[...].reshape(1, ub)
    meta[z] = jnp.concatenate([pos.astype(F32), weight_v[...].reshape(1, ub).astype(F32)], axis=0)
    valid[0] = valid_v[...].reshape(1, ib).astype(F32)
    x = feats[...]
    pre = dot(x, w_in[...])
    hid_t = (pre * jax.nn.sigmoid(pre)).astype(BF16)
    hidden[...] = hid_t
    slope[...] = pre
    vecs[0] = (x.astype(F32) + dot(hid_t, w_out[...])).astype(BF16)
    pl.semaphore_wait(barrier, d.nz - 1 + d.np - 1 + 1)

    far = d.nz // 2
    direct = [k for k in (2, d.nz - 2, 1, d.nz - 1) if 0 < k < d.nz]
    direct = sorted(set(direct), key=direct.index)
    handed = [k for k in range(1, d.nz) if k not in direct]
    order = [0] + direct + sorted(handed, key=lambda k: k == far)

    def hops_of(step):
        k = 0
        for i in range(1, d.nz):
            k = jnp.where(step == i, order[i], k)
        return k

    def users_copies(k, slot, to):
        there = z_dev(to)
        return [
            remote(users.at[slot], users.at[slot], us_s.at[k], us_r.at[k], there),
            remote(meta.at[slot], meta.at[slot], me_s.at[k], me_r.at[k], there),
        ]

    def users_start(k, slot, to):
        for copy in users_copies(k, slot, to):
            copy.start()

    def users_sent():
        for k in range(1, d.nz):
            for copy in users_copies(k, z, 1):
                copy.wait_send()

    def users_arrive(k, slot):
        for copy in users_copies(k, slot, 1):
            copy.wait_recv()

    def hand_on_users(k):
        slot = back_by(z, k, d.nz)
        ahead = k == 2
        users_start(3 if ahead else d.nz - 3, slot, 1 if ahead else d.nz - 1)

        @pl.when(core == (0 if ahead else 1))
        def _():
            users_start(far, slot, 2 if ahead else d.nz - 2)

    def vecs_copy(j):
        return remote(vecs.at[j // 3 * 2], vecs.at[j], ve_s.at[j], ve_r.at[j], across if j == 2 else sibling)

    def valid_copy(j):
        return remote(valid.at[j // 3 * 2], valid.at[j], va_s.at[j], va_r.at[j], across if j == 2 else sibling)

    for j in (2, 1):
        launch(f"vecs{j}", functools.partial(vecs_copy, j))
        launch(f"valid{j}", functools.partial(valid_copy, j))
    for k in direct:
        users_start(k, z, k)
    tails.append(users_sent)

    def vec_arrives(j):
        arrive(f"vecs{j}")
        arrive(f"valid{j}")

    def local_tile(pos):
        block = pos // ib
        p_core = block % d.nc
        p_z = block // d.nc % d.nz
        p_xl = block // (d.nc * d.nz) % d.nxl
        p_item = block // (d.nc * d.nz * d.nxl)
        j = (p_xl + d.nxl - xl) % d.nxl * d.nc + (p_core + d.nc - core) % d.nc
        here = (p_item == item) & (p_z == z)
        row = jnp.where(here, j * ib + pos % ib, -1)
        lane = lax.broadcasted_iota(jnp.int32, (8, ub), 0)
        return jnp.where(here & (lane == row % 8), row // 8, -1)

    def set_bias(j):
        bias[j] = (jnp.broadcast_to(valid[j], (128, ib)).T - 1.0) * -DEAD

    def enter(slot):
        lanes = pl.ds(pl.multiple_of(slot * ub, ub), ub)
        tile_s[:, lanes] = local_tile(meta[slot, 0:1, :].astype(jnp.int32))
        weight_s[:, lanes] = meta[slot, 1:2, :]

    def score(j, slot):
        at = pl.multiple_of(slot * ub, ub)
        tile = lax.broadcasted_iota(jnp.int32, (d.chunk // 8, 8, 128), 0)
        for c in range(ib // d.chunk):
            rows = slice(c * d.chunk, (c + 1) * d.chunk)
            s = dot_t(vecs[j, rows, :], users[slot])
            b = bias[j, rows, :].reshape(d.chunk // 8, 8, 128)
            ck = j * (ib // d.chunk) + c
            first = pl.multiple_of(ck * d.chunk, d.chunk)
            for h in range(ub // 128):
                lanes = pl.ds(pl.multiple_of(at + h * 128, 128), 128)
                sh = s[:, h * 128 : (h + 1) * 128].reshape(d.chunk // 8, 8, 128)
                hit = tile == (tile_s[:, lanes] - ck * (d.chunk // 8))[None]
                x = jnp.where(hit, sh, sh + b)
                peak = jnp.maximum(jnp.max(x, axis=0), FLOOR)
                e = jnp.exp(x - peak[None])
                peak_s[ck, :, lanes] = peak
                total_s[ck, :, lanes] = jnp.sum(e, axis=0)
                expo[pl.ds(first, d.chunk), lanes] = e.reshape(d.chunk, 128)

    first = min(5, d.nz)
    groups = [order[1:3], order[3:5]] if d.nz >= 5 else [order[1:first]]
    ng = len(groups)

    def early_steps(i, carry):
        pair = lax.div(i, ng)
        turn = lax.rem(i, ng)

        for at, group in enumerate(groups):

            @pl.when(i == at)
            def _():
                for k in group:
                    slot = back_by(z, k, d.nz)
                    users_arrive(k, slot)
                    if handed and k in (2, d.nz - 2):
                        hand_on_users(k)
                    enter(slot)

        for q in range(len(groups[0])):
            k = functools.reduce(lambda a, g: jnp.where(turn == g, groups[g][q], a), range(1, ng), groups[0][q])
            slot = back_by(z, k, d.nz)
            score(pair * 2, slot)
            score(pair * 2 + 1, slot)
        return carry

    def late_steps(step, carry):
        k = hops_of(step)
        slot = back_by(z, k, d.nz)
        users_arrive(k, slot)
        enter(slot)
        for j in range(d.nj):
            score(j, slot)
        return carry

    enter(z)
    set_bias(0)
    score(0, z)
    vec_arrives(1)
    set_bias(1)
    score(1, z)
    lax.fori_loop(0, ng, early_steps, 0)
    vec_arrives(2)
    launch("vecs3", functools.partial(vecs_copy, 3))
    launch("valid3", functools.partial(valid_copy, 3))
    set_bias(2)
    score(2, z)
    vec_arrives(3)
    set_bias(3)
    score(3, z)
    lax.fori_loop(ng, 2 * ng, early_steps, 0)
    lax.fori_loop(first, d.nz, late_steps, 0)

    def merge(logs):
        peak = functools.reduce(jnp.maximum, logs)
        return peak + jnp.log(sum(jnp.exp(v - peak) for v in logs))

    peak8 = functools.reduce(jnp.maximum, [peak_s[c] for c in range(d.nk)])
    peak = jnp.max(peak8, axis=0, keepdims=True)
    total8 = sum(total_s[c] * jnp.exp(peak_s[c] - peak) for c in range(d.nk))
    st_own[...] = peak + jnp.log(jnp.maximum(jnp.sum(total8, axis=0, keepdims=True), 1e-30))

    def st_a_copy(k):
        return remote(st_own, st_a.at[k], sa_s.at[k], sa_r.at[k], group_dev(k))

    def st_b_copy(k):
        return remote(st_own2, st_b.at[k], sb_s.at[k], sb_r.at[k], z_dev(k))

    fly("st_a", d.ng, st_a_copy)
    for j in range(d.nj):
        vec_t[:, j * ib : (j + 1) * ib] = vecs[j].astype(F32).T.astype(BF16)

    pre = slope[...]
    sigma = jax.nn.sigmoid(pre)
    slope[...] = sigma * (1.0 + pre * (1.0 - sigma))
    land("st_a")
    st_own2[...] = merge([st_own[...]] + [st_a[k] for k in range(1, d.ng)])
    fly("st_b", d.nz, st_b_copy)
    land("st_b")
    log_total = merge([st_own2[...]] + [st_b[k] for k in range(1, d.nz)])
    for c in range(d.nk):
        factor[c] = weight_s[...] * jnp.exp(peak_s[c] - log_total)

    def gv_copy(j):
        return remote(gv_send.at[j], gv_recv.at[j], gv_s.at[j], gv_r.at[j], across if j == 2 else sibling)

    width = min(512, d.users)
    per = ib // d.chunk

    def grads(t, carry):
        j = 3 - t
        rows = pl.ds(pl.multiple_of(j * ib, ib), ib)
        acc = jnp.zeros((ib, emb), F32)
        tile = lax.broadcasted_iota(jnp.int32, (ib // 8, 8, width), 0)
        for u in range(0, d.users, width):
            lanes = slice(u, u + width)
            e = expo[rows, lanes].reshape(per, d.chunk // 8, 8, width)
            e = (e * factor[pl.ds(j * per, per), :, lanes][:, None]).reshape(ib // 8, 8, width)
            hit = tile == (tile_s[:, lanes] - j * (ib // 8))[None]
            g = jnp.where(hit, e - weight_s[:, lanes][None], e).reshape(ib, width).astype(BF16)
            grad[rows, lanes] = g
            acc = acc + dot(g, users[...].reshape(d.users, emb)[lanes, :])
        gv_own[...] = acc

        for at, i in ((0, 3), (2, 1)):

            @pl.when(t == at)
            def _():
                gv_send[i] = gv_own[...].astype(BF16)
                launch(f"gv{i}", functools.partial(gv_copy, i))

        @pl.when(t == 1)
        def _():
            arrive("gv3")
            gv_send[2] = (gv_own[...] + gv_recv[3].astype(F32)).astype(BF16)
            launch("gv2", functools.partial(gv_copy, 2))

        return carry

    lax.fori_loop(0, 4, grads, 0)

    us = ub // d.ng
    zs = width // ub
    turns = d.users // width
    offsets = sorted(range(turns), key=lambda o: -min(o, turns - o))

    def gu_copy(k):
        return remote(gu_send.at[z_peer(k)], gu_recv.at[k], gu_s.at[k], gu_r.at[k], z_dev(k))

    def user_terms(i, carry):
        offset = functools.reduce(lambda a, t: jnp.where(i == t, offsets[t], a), range(1, turns), offsets[0])
        q = lax.rem(lax.div(z, zs) + offset, turns)
        lanes = pl.ds(pl.multiple_of(q * width, width), width)
        terms = dot(vec_t[...], grad[:, lanes]).T
        for e in range(zs):
            slot = q * zs + e
            part = terms[e * ub : (e + 1) * ub, :]

            @pl.when(slot == z)
            def _():
                gu_sum[...] = part

            @pl.when(slot != z)
            def _():
                gu_send[slot] = part.astype(BF16)
                gu_copy(back_by(slot, z, d.nz)).start()

        return carry

    fly("gu", d.nz, gu_copy, start=False)
    lax.fori_loop(0, turns, user_terms, 0)

    arrive("gv1")
    arrive("gv2")
    gv = gv_own[...] + gv_recv[1].astype(F32) + gv_recv[2].astype(F32)
    gv = gv.astype(BF16)
    gv_own[...] = gv.astype(F32)
    gv_t = gv_own[...].T.astype(BF16)
    hc = hid // 2
    mine = pl.ds(pl.multiple_of(core * hc, hc), hc)
    other = pl.ds(pl.multiple_of((1 - core) * hc, hc), hc)

    def wc_copy(m):
        return remote(wc_send.at[m], wc_recv.at[m], wc_s.at[m], wc_r.at[m], sibling)

    wg_own[1] = dot(gv_t, hidden[...])
    wc_send[1] = wg_own[1, :, other].astype(BF16)
    launch("wc1", functools.partial(wc_copy, 1))

    pre = (dot_t(gv, w_out[...]) * slope[...]).astype(BF16)
    hidden[...] = pre
    wg_own[0] = dot(feats[...].astype(F32).T.astype(BF16), pre)
    wc_send[0] = wg_own[0, :, other].astype(BF16)
    launch("wc0", functools.partial(wc_copy, 0))

    sr = d.srows
    half = d.np // 2

    def w1_copy(k):
        p = plane_peer(k)
        return remote(w1_send.at[p], w1_recv.at[k], w1_s.at[k], w1_r.at[k], plane_dev(p))

    for m in (1, 0):
        arrive(f"wc{m}")
        total = (wg_own[m, :, mine] + wc_recv[m].astype(F32)).astype(BF16)
        w1_send[m * half : (m + 1) * half] = total.reshape(half, sr, hc)
    fly("w1", d.np, w1_copy)

    def out_copy(i):
        pairs = [(item_v, out_item), (gu_out, out_user), (a1.at[core], out_w.at[core]), (a1.at[1 - core], out_w.at[1 - core])]
        return pltpu.make_async_copy(*pairs[i], out_s.at[i])

    item_v[...] = gv_own[...] + dot_t(hidden[...], w_in[...])
    out_copy(0).start()
    tails.append(lambda: out_copy(0).wait())
    tails.remove(users_sent)
    users_sent()
    sent("vecs1", "vecs2", "vecs3", "valid1", "valid2", "valid3", "st_a", "st_b")
    sent("gv1", "gv2", "gv3", "wc0", "wc1")
    land("w1")
    part = w1_send[plane].astype(F32)
    for k in range(1, d.np):
        part = part + w1_recv[k].astype(F32)
    wz[z] = part.astype(BF16)

    def wz_copy(k, slot):
        return remote(wz.at[slot], wz.at[slot], wz_s.at[k], wz_r.at[k], z_dev(k))

    fly("wz", d.nz, lambda k: wz_copy(k, z), lambda k: wz_copy(k, back_by(z, k, d.nz)))

    land("gu")
    gu_sum[...] += sum(gu_recv[k].astype(F32) for k in range(1, d.nz))

    def rows_of(i):
        return pl.ds(pl.multiple_of(i * us, us), us)

    def g2_copy(k):
        to = lax.rem(item + k, d.ng)
        return remote(gu_sum.at[rows_of(to), :], gu2_recv.at[k], g2_s.at[k], g2_r.at[k], group_dev(k))

    fly("g2", d.ng, g2_copy)
    sent("w1", "gu")
    land("wz")
    a1[core, plane] = sum(wz[k].astype(F32) for k in range(d.nz)).astype(BF16)

    def w4_copy(k, slot):
        there = a1.at[core, slot]
        return remote(there, there, w4_s.at[k], w4_r.at[k], plane_dev(plane_peer(k)))

    fly("w4", d.np, lambda k: w4_copy(k, plane), lambda k: w4_copy(k, back_by(plane, k, d.np)))

    land("g2")
    gu_out[rows_of(item), :] = gu_sum[rows_of(item), :] + sum(gu2_recv[k] for k in range(1, d.ng))

    def g3_copy(k, at):
        there = gu_out.at[rows_of(at), :]
        return remote(there, there, g3_s.at[k], g3_r.at[k], group_dev(k))

    fly("g3", d.ng, lambda k: g3_copy(k, item), lambda k: g3_copy(k, back_by(item, k, d.ng)))
    sent("wz", "g2")

    per_group = d.np // d.groups

    def w5_copy(g, of):
        there = a1.at[of, pl.ds(g * per_group, per_group)]
        return remote(there, there, w5_s.at[g], w5_r.at[g], sibling)

    for g in range(d.groups):
        for slot in range(g * per_group, (g + 1) * per_group):

            @pl.when(slot != plane)
            def _():
                w4_copy(back_by(plane, slot, d.np), slot).wait_recv()

        w5_copy(g, core).start()
    flights["w4"][3] = True
    out_copy(2).start()
    land("g3")
    out_copy(1).start()
    for g in range(d.groups):
        w5_copy(g, 1 - core).wait_recv()
    out_copy(3).start()

    finish()
    for g in range(d.groups):
        w5_copy(g, core).wait_send()
    for i in (1, 2, 3):
        out_copy(i).wait()


def unpack(d, user_ref, item_ref, w_ref, out_user, out_item, out_w_in, out_w_out, user_v, item_v, w_v, w_in_v, w_out_v, sems):
    half, hc = d.np // 2, d.scols
    loads = [(w_ref.at[h, m], w_v.at[h, m]) for m in (1, 0) for h in range(2)]
    loads += [(item_ref, item_v), (user_ref, user_v)]
    loads = [pltpu.make_async_copy(src, dst, sems.at[i]) for i, (src, dst) in enumerate(loads)]
    for copy in loads:
        copy.start()
    stores = [(w_out_v, out_w_out), (w_in_v, out_w_in), (item_v, out_item), (user_v, out_user)]
    stores = [pltpu.make_async_copy(src, dst, sems.at[6 + i]) for i, (src, dst) in enumerate(stores)]
    for m in (1, 0):
        for h in range(2):
            loads[2 * (1 - m) + h].wait()
            block = w_v[h, m].astype(F32).reshape(d.emb, hc)
            at = slice(h * hc, (h + 1) * hc)
            if m == 0:
                w_in_v[:, at] = block
            else:
                w_out_v[at, :] = block.T
        stores[1 - m].start()
    for i in (4, 5):
        loads[i].wait()
        stores[i - 2].start()
    for copy in stores:
        copy.wait()


def body(phys, user_vecs, row_weight, positive, item_feats, valid, w_in, w_out):
    ub, emb = user_vecs.shape
    ib, hid = item_feats.shape[0], w_in.shape[1]
    d = Dims(phys, ub, ib, emb, hid)
    vm = pltpu.VMEM
    us = ub // d.ng
    scratch = [
        vm((ib, emb), BF16),
        vm((emb, hid), BF16),
        vm((hid, emb), BF16),
        vm((ub,), BF16),
        vm((ub,), jnp.int32),
        vm((ib,), jnp.int32),
        vm((ib, emb), F32),
        vm((d.nz, ub, emb), BF16),
        vm((d.nz, 2, ub), F32),
        vm((d.nj, ib, emb), BF16),
        vm((d.nj, 1, ib), F32),
        vm((d.nj, ib, 128), F32),
        vm((emb, d.items), BF16),
        vm((ib, hid), BF16),
        vm((ib, hid), F32),
        vm((d.items, d.users), F32),
        vm((d.items, d.users), BF16),
        vm((d.nk, 8, d.users), F32),
        vm((d.nk, 8, d.users), F32),
        vm((d.nk, 8, d.users), F32),
        vm((8, d.users), jnp.int32),
        vm((1, d.users), F32),
        vm((1, d.users), F32),
        vm((d.ng, 1, d.users), F32),
        vm((1, d.users), F32),
        vm((d.nz, 1, d.users), F32),
        vm((d.nj, ib, emb), BF16),
        vm((d.nj, ib, emb), BF16),
        vm((ib, emb), F32),
        vm((d.nz, ub, emb), BF16),
        vm((d.nz, ub, emb), BF16),
        vm((ub, emb), F32),
        vm((d.ng, us, emb), F32),
        vm((ub, emb), F32),
        vm((2, emb, hid), F32),
        vm((2, emb, hid // 2), BF16),
        vm((2, emb, hid // 2), BF16),
        vm((d.np, d.srows, d.scols), BF16),
        vm((d.np, d.srows, d.scols), BF16),
        vm((d.nz, d.srows, d.scols), BF16),
        vm((2, d.np, d.srows, d.scols), BF16),
    ]
    dma = pltpu.SemaphoreType.DMA
    sems = [dma((7,)), dma((4,))]
    for n in (d.nz, d.nz, d.nj, d.nj, d.ng, d.nz, d.nj, d.nz, d.ng, d.ng, 2, d.np, d.nz, d.np, d.groups):
        sems += [dma((n,)), dma((n,))]
    where = pl.BlockSpec(memory_space=pl.ANY)
    parts = pl.pallas_call(
        functools.partial(kernel, d),
        out_shape=(
            jax.ShapeDtypeStruct((ub, emb), F32),
            jax.ShapeDtypeStruct((ib, emb), F32),
            jax.ShapeDtypeStruct((2, d.np, d.srows, d.scols), BF16),
        ),
        in_specs=[where] * 7,
        out_specs=(where,) * 3,
        scratch_shapes=scratch + sems,
        compiler_params=pltpu.CompilerParams(
            collective_id=0, has_side_effects=True, vmem_limit_bytes=56 * 1024 * 1024
        ),
        cost_estimate=pl.CostEstimate(
            flops=6 * d.users * d.items * emb,
            bytes_accessed=4 * 1024 * 1024,
            transcendentals=d.users * d.items,
        ),
    )(user_vecs, row_weight, positive, item_feats, valid, w_in, w_out)
    user, item, weights = parts
    weights = weights.reshape(2, 2, d.np // 2, d.srows, d.scols)
    return pl.pallas_call(
        functools.partial(unpack, d),
        out_shape=(
            jax.ShapeDtypeStruct((ub, emb), F32),
            jax.ShapeDtypeStruct((ib, emb), F32),
            jax.ShapeDtypeStruct((emb, hid), F32),
            jax.ShapeDtypeStruct((hid, emb), F32),
        ),
        in_specs=[where] * 3,
        out_specs=(where,) * 4,
        scratch_shapes=[
            vm((ub, emb), F32),
            vm((ib, emb), F32),
            vm(weights.shape, BF16),
            vm((emb, hid), F32),
            vm((hid, emb), F32),
            dma((10,)),
        ],
    )(user, item, weights)


def build(mesh, phys):
    return jax.shard_map(
        functools.partial(body, phys),
        mesh=mesh,
        in_specs=(
            P("user", None),
            P("user"),
            P("user"),
            P(("item", "user"), None),
            P(("item", "user")),
            P(),
            P(),
        ),
        out_specs=(P("user", None), P(("item", "user"), None), P(), P()),
        check_vma=False,
    )


def solution(mesh):
    return build(mesh, (4, 2, 2, 8, 2))
```

```python
import functools

import jax
import jax.numpy as jnp
from jax import lax
from jax.experimental import pallas as pl
from jax.experimental.pallas import tpu as pltpu
from jax.sharding import PartitionSpec as P

MESH = pl.DeviceIdType.MESH
F32 = jnp.float32
BF16 = jnp.bfloat16
DEAD = -1e30
FLOOR = -1e29


def dot(a, b):
    return jnp.dot(a, b, preferred_element_type=F32)


def dot_t(a, b):
    return lax.dot_general(a, b, (((1,), (1,)), ((), ())), preferred_element_type=F32)


class Dims:
    def __init__(self, phys, ub, ib, emb, hid):
        self.ny, self.nxh, self.nxl, self.nz, self.nc = phys
        self.ub, self.ib, self.emb, self.hid = ub, ib, emb, hid
        self.ng = self.ny * self.nxh
        self.np = self.ng * self.nxl
        self.nj = self.nxl * self.nc
        self.users = self.nz * ub
        self.items = self.nj * ib
        self.chunk = min(256, ib)
        self.nk = self.items // self.chunk
        self.srows = 2 * emb // self.np
        self.scols = hid // 2
        self.groups = min(4, self.np)
        self.nfar = max(0, self.nz - 5)


def kernel(
    d,
    users_in, weight_in, pos_in, feats_in, valid_in, w_in_in, w_out_in,
    out_user, out_item, out_w,
    feats, w_in, w_out, weight_v, pos_v, valid_v, item_v, users, meta, vecs, valid, bias, vec_t, hidden, slope, expo, grad,
    peak_s, total_s, factor, tile_s, weight_s,
    st_own, st_a, st_own2, st_b,
    gv_send, gv_recv, gv_own, gu_send, gu_recv, gu_sum, gu2_recv, gu_out, gf_send, gf_recv, gf_sum, gf2_recv,
    wg_own, pre_s, feats_t, wc_send, wc_recv, w1_send, w1_recv, wz, a1,
    in_s, out_s, us_s, us_r, me_s, me_r, ve_s, ve_r, va_s, va_r, sa_s, sa_r, sb_s, sb_r,
    gv_s, gv_r, gu_s, gu_r, g2_s, g2_r, g3_s, g3_r,
    wc_s, wc_r, w1_s, w1_r, wz_s, wz_r, w4_s, w4_r, w5_s, w5_r, gf_s, gf_r, f2_s, f2_r,
):
    ub, ib, emb, hid = d.ub, d.ib, d.emb, d.hid
    item = lax.axis_index("item")
    user = lax.axis_index("user")
    core = lax.rem(user, d.nc)
    z = lax.rem(lax.div(user, d.nc), d.nz)
    xl = lax.div(user, d.nc * d.nz)
    plane = item * d.nxl + xl

    def dev(item_, xl_, z_, core_):
        return (item_, (xl_ * d.nz + z_) * d.nc + core_)

    def back_by(here, k, n):
        return lax.rem(here + n - k, n)

    def z_peer(k):
        return lax.rem(z + k, d.nz)

    def z_dev(k):
        return dev(item, xl, z_peer(k), core)

    def group_dev(k):
        return dev(lax.rem(item + k, d.ng), xl, z, core)

    def plane_peer(k):
        return lax.rem(plane + k, d.np)

    def plane_dev(p):
        return dev(lax.div(p, d.nxl), lax.rem(p, d.nxl), z, core)

    sibling = dev(item, xl, z, 1 - core)
    across = dev(item, 1 - xl, z, core)
    diagonal = dev(item, 1 - xl, z, 1 - core)

    def remote(src, dst, send, recv, to):
        return pltpu.make_async_remote_copy(
            src_ref=src, dst_ref=dst, send_sem=send, recv_sem=recv, device_id=to, device_id_type=MESH
        )

    def each(n, fn):
        def step(k, carry):
            fn(k)
            return carry

        lax.fori_loop(1, n, step, 0)

    flights = {}

    def fly(name, n, copy_out, copy_in=None, start=True):
        flights[name] = [n, copy_out, copy_in or copy_out, False]
        if start:
            each(n, lambda k: copy_out(k).start())

    def land(name):
        n, _, copy_in, _ = flights[name]
        each(n, lambda k: copy_in(k).wait_recv())
        flights[name][3] = True

    def sent(*names):
        for name in names:
            if name in flights:
                n, copy_out, _, landed = flights.pop(name)
                each(n, lambda k: copy_out(k).wait_send())
            else:
                make, landed = singles.pop(name)
                make().wait_send()

    tails = []
    singles = {}

    def launch(name, make):
        singles[name] = [make, False]
        make().start()

    def arrive(name):
        singles[name][0]().wait_recv()
        singles[name][1] = True

    def finish():
        for wait in tails:
            wait()
        for name in list(flights):
            if not flights[name][3]:
                land(name)
            sent(name)
        for name in list(singles):
            if not singles[name][1]:
                arrive(name)
            sent(name)

    barrier = pltpu.get_barrier_semaphore()

    def greet(to):
        pl.semaphore_signal(barrier, inc=1, device_id=to, device_id_type=MESH)

    each(d.nz, lambda k: greet(z_dev(k)))
    each(d.np, lambda k: greet(plane_dev(plane_peer(k))))
    greet(sibling)
    greet(diagonal)

    inputs = [(feats_in, feats), (w_in_in, w_in), (w_out_in, w_out), (users_in, users.at[z])]
    inputs += [(weight_in, weight_v), (pos_in, pos_v), (valid_in, valid_v)]
    inputs = [pltpu.make_async_copy(src, dst, in_s.at[i]) for i, (src, dst) in enumerate(inputs)]
    for copy in inputs:
        copy.start()

    for copy in inputs:
        copy.wait()
    pos = pos_v[...].reshape(1, ub)
    meta[z] = jnp.concatenate([pos.astype(F32), weight_v[...].reshape(1, ub).astype(F32)], axis=0)
    valid[0] = valid_v[...].reshape(1, ib).astype(F32)
    x = feats[...]
    pre = dot(x, w_in[...])
    hid_t = (pre * jax.nn.sigmoid(pre)).astype(BF16)
    hidden[...] = hid_t
    slope[...] = pre
    vecs[0] = (x.astype(F32) + dot(hid_t, w_out[...])).astype(BF16)
    pl.semaphore_wait(barrier, d.nz - 1 + d.np - 1 + 2)

    far = d.nz // 2
    direct = [k for k in (2, d.nz - 2, 1, d.nz - 1) if 0 < k < d.nz]
    direct = sorted(set(direct), key=direct.index)
    handed = [k for k in range(1, d.nz) if k not in direct]
    order = [0] + direct + sorted(handed, key=lambda k: k == far)

    def hops_of(step):
        k = 0
        for i in range(1, d.nz):
            k = jnp.where(step == i, order[i], k)
        return k

    def users_copies(k, slot, to):
        there = z_dev(to)
        return [
            remote(users.at[slot], users.at[slot], us_s.at[k], us_r.at[k], there),
            remote(meta.at[slot], meta.at[slot], me_s.at[k], me_r.at[k], there),
        ]

    def users_start(k, slot, to):
        for copy in users_copies(k, slot, to):
            copy.start()

    def users_sent():
        for k in range(1, d.nz):
            for copy in users_copies(k, z, 1):
                copy.wait_send()

    def users_arrive(k, slot):
        for copy in users_copies(k, slot, 1):
            copy.wait_recv()

    def hand_on_users(k):
        slot = back_by(z, k, d.nz)
        ahead = k == 2
        users_start(3 if ahead else d.nz - 3, slot, 1 if ahead else d.nz - 1)

        @pl.when(core == (0 if ahead else 1))
        def _():
            users_start(far, slot, 2 if ahead else d.nz - 2)

    def vecs_copy(j):
        return remote(vecs.at[j // 3 * 2], vecs.at[j], ve_s.at[j], ve_r.at[j], across if j == 2 else sibling)

    def valid_copy(j):
        return remote(valid.at[j // 3 * 2], valid.at[j], va_s.at[j], va_r.at[j], across if j == 2 else sibling)

    for j in (2, 1):
        launch(f"vecs{j}", functools.partial(vecs_copy, j))
        launch(f"valid{j}", functools.partial(valid_copy, j))
    for k in direct:
        users_start(k, z, k)
    tails.append(users_sent)

    def vec_arrives(j):
        arrive(f"vecs{j}")
        arrive(f"valid{j}")

    def local_tile(pos):
        block = pos // ib
        p_core = block % d.nc
        p_z = block // d.nc % d.nz
        p_xl = block // (d.nc * d.nz) % d.nxl
        p_item = block // (d.nc * d.nz * d.nxl)
        j = (p_xl + d.nxl - xl) % d.nxl * d.nc + (p_core + d.nc - core) % d.nc
        here = (p_item == item) & (p_z == z)
        row = jnp.where(here, j * ib + pos % ib, -1)
        lane = lax.broadcasted_iota(jnp.int32, (8, ub), 0)
        return jnp.where(here & (lane == row % 8), row // 8, -1)

    def set_bias(j):
        bias[j] = (jnp.broadcast_to(valid[j], (128, ib)).T - 1.0) * -DEAD

    def enter(slot):
        lanes = pl.ds(pl.multiple_of(slot * ub, ub), ub)
        tile_s[:, lanes] = local_tile(meta[slot, 0:1, :].astype(jnp.int32))
        weight_s[:, lanes] = meta[slot, 1:2, :]

    def score(j, slot):
        at = pl.multiple_of(slot * ub, ub)
        tile = lax.broadcasted_iota(jnp.int32, (d.chunk // 8, 8, 128), 0)
        for c in range(ib // d.chunk):
            rows = slice(c * d.chunk, (c + 1) * d.chunk)
            s = dot_t(vecs[j, rows, :], users[slot])
            b = bias[j, rows, :].reshape(d.chunk // 8, 8, 128)
            ck = j * (ib // d.chunk) + c
            first = pl.multiple_of(ck * d.chunk, d.chunk)
            for h in range(ub // 128):
                lanes = pl.ds(pl.multiple_of(at + h * 128, 128), 128)
                sh = s[:, h * 128 : (h + 1) * 128].reshape(d.chunk // 8, 8, 128)
                hit = tile == (tile_s[:, lanes] - ck * (d.chunk // 8))[None]
                x = jnp.where(hit, sh, sh + b)
                peak = jnp.maximum(jnp.max(x, axis=0), FLOOR)
                e = jnp.exp(x - peak[None])
                peak_s[ck, :, lanes] = peak
                total_s[ck, :, lanes] = jnp.sum(e, axis=0)
                expo[pl.ds(first, d.chunk), lanes] = e.reshape(d.chunk, 128)

    first = min(5, d.nz)
    groups = [order[1:3], order[3:5]] if d.nz >= 5 else [order[1:first]]
    ng = len(groups)

    def early_steps(i, carry):
        pair = lax.div(i, ng)
        turn = lax.rem(i, ng)

        for at, group in enumerate(groups):

            @pl.when(i == at)
            def _():
                for k in group:
                    slot = back_by(z, k, d.nz)
                    users_arrive(k, slot)
                    if handed and k in (2, d.nz - 2):
                        hand_on_users(k)
                    enter(slot)

        for q in range(len(groups[0])):
            k = functools.reduce(lambda a, g: jnp.where(turn == g, groups[g][q], a), range(1, ng), groups[0][q])
            slot = back_by(z, k, d.nz)
            score(pair * 2, slot)
            score(pair * 2 + 1, slot)
        return carry

    def late_steps(step, carry):
        k = hops_of(step)
        slot = back_by(z, k, d.nz)
        users_arrive(k, slot)
        enter(slot)
        for j in range(d.nj):
            score(j, slot)
        return carry

    enter(z)
    set_bias(0)
    score(0, z)
    vec_arrives(1)
    set_bias(1)
    score(1, z)
    lax.fori_loop(0, ng, early_steps, 0)
    vec_arrives(2)
    launch("vecs3", functools.partial(vecs_copy, 3))
    launch("valid3", functools.partial(valid_copy, 3))
    set_bias(2)
    score(2, z)
    vec_arrives(3)
    set_bias(3)
    score(3, z)
    lax.fori_loop(ng, 2 * ng, early_steps, 0)
    lax.fori_loop(first, d.nz, late_steps, 0)

    def merge(logs):
        peak = functools.reduce(jnp.maximum, logs)
        return peak + jnp.log(sum(jnp.exp(v - peak) for v in logs))

    peak8 = functools.reduce(jnp.maximum, [peak_s[c] for c in range(d.nk)])
    peak = jnp.max(peak8, axis=0, keepdims=True)
    total8 = sum(total_s[c] * jnp.exp(peak_s[c] - peak) for c in range(d.nk))
    st_own[...] = peak + jnp.log(jnp.maximum(jnp.sum(total8, axis=0, keepdims=True), 1e-30))

    def st_a_copy(k):
        return remote(st_own, st_a.at[k], sa_s.at[k], sa_r.at[k], group_dev(k))

    def st_b_copy(k):
        return remote(st_own2, st_b.at[k], sb_s.at[k], sb_r.at[k], z_dev(k))

    fly("st_a", d.ng, st_a_copy)
    for j in range(d.nj):
        vec_t[:, j * ib : (j + 1) * ib] = vecs[j].astype(F32).T.astype(BF16)

    pre = slope[...]
    sigma = jax.nn.sigmoid(pre)
    slope[...] = sigma * (1.0 + pre * (1.0 - sigma))
    feats_t[...] = feats[...].astype(F32).T.astype(BF16)
    land("st_a")
    st_own2[...] = merge([st_own[...]] + [st_a[k] for k in range(1, d.ng)])
    fly("st_b", d.nz, st_b_copy)
    land("st_b")
    log_total = merge([st_own2[...]] + [st_b[k] for k in range(1, d.nz)])
    for c in range(d.nk):
        factor[c] = weight_s[...] * jnp.exp(peak_s[c] - log_total)

    lone = ib // 4

    def gv_copy(name):
        i, rows, slot, to = {
            "gv3": (3, slice(lone, ib), 3, sibling),
            "gv3_lone": (3, slice(0, lone), 0, diagonal),
            "gv2": (2, slice(lone, ib), 2, across),
            "gv2_lone": (2, slice(0, lone), 2, across),
            "gv1": (1, slice(0, ib), 1, sibling),
        }[name]
        n = ("gv1", "gv2", "gv3", "gv2_lone", "gv3_lone").index(name)
        return remote(gv_send.at[i, rows], gv_recv.at[slot, rows], gv_s.at[n], gv_r.at[n], to)

    def gv_launch(name):
        launch(name, functools.partial(gv_copy, name))

    width = min(512, d.users)
    per = ib // d.chunk

    def grads(t, carry):
        j = 3 - t
        rows = pl.ds(pl.multiple_of(j * ib, ib), ib)
        acc = jnp.zeros((ib, emb), F32)
        tile = lax.broadcasted_iota(jnp.int32, (ib // 8, 8, width), 0)
        for u in range(0, d.users, width):
            lanes = slice(u, u + width)
            e = expo[rows, lanes].reshape(per, d.chunk // 8, 8, width)
            e = (e * factor[pl.ds(j * per, per), :, lanes][:, None]).reshape(ib // 8, 8, width)
            hit = tile == (tile_s[:, lanes] - j * (ib // 8))[None]
            g = jnp.where(hit, e - weight_s[:, lanes][None], e).reshape(ib, width).astype(BF16)
            grad[rows, lanes] = g
            acc = acc + dot(g, users[...].reshape(d.users, emb)[lanes, :])
        gv_own[...] = acc

        @pl.when(t == 0)
        def _():
            gv_send[3] = gv_own[...].astype(BF16)
            gv_launch("gv3_lone")
            gv_launch("gv3")

        @pl.when(t == 1)
        def _():
            gv_send[2, :lone] = gv_own[:lone, :].astype(BF16)
            gv_launch("gv2_lone")
            arrive("gv3")
            gv_send[2, lone:] = (gv_own[lone:, :] + gv_recv[3, lone:, :].astype(F32)).astype(BF16)
            gv_launch("gv2")

        @pl.when(t == 2)
        def _():
            gv_send[1] = gv_own[...].astype(BF16)
            gv_launch("gv1")

        return carry

    lax.fori_loop(0, 4, grads, 0)

    us = ub // d.ng
    nfar = d.nfar
    zs = width // ub
    turns = d.users // width
    offsets = sorted(range(turns), key=lambda o: -min(o, turns - o))

    def gu_copy(k):
        return remote(gu_send.at[z_peer(k)], gu_recv.at[k], gu_s.at[k], gu_r.at[k], z_dev(k))

    def user_terms(i, carry):
        offset = functools.reduce(lambda a, t: jnp.where(i == t, offsets[t], a), range(1, turns), offsets[0])
        q = lax.rem(lax.div(z, zs) + offset, turns)
        lanes = pl.ds(pl.multiple_of(q * width, width), width)
        terms = dot(vec_t[...], grad[:, lanes]).T
        for e in range(zs):
            slot = q * zs + e
            part = terms[e * ub : (e + 1) * ub, :]

            @pl.when(slot == z)
            def _():
                gu_sum[...] = part

            k = back_by(slot, z, d.nz)
            is_near = (slot != z) & ((k < 3) | (k > d.nz - 3))

            @pl.when(is_near)
            def _():
                gu_send[slot] = part.astype(BF16)
                gu_copy(k).start()

            if nfar:

                @pl.when((k >= 3) & (k <= d.nz - 3))
                def _():
                    for g in range(d.ng):
                        gf_send[g, k - 3] = part[g * us : (g + 1) * us, :].astype(BF16)

        return carry

    def near_hops(i):
        return jnp.where(i < 3, i, i + nfar)

    def gf_copy(k):
        to = lax.rem(item + k, d.ng)
        return remote(gf_send.at[to], gf_recv.at[k], gf_s.at[k], gf_r.at[k], dev(to, xl, z, core))

    def gf2_copy(i):
        return remote(gf_sum.at[i - 1], gf2_recv.at[i - 1], f2_s.at[i], f2_r.at[i], z_dev(i + 2))

    fly("gu", d.nz - nfar, lambda i: gu_copy(near_hops(i)), start=False)
    lax.fori_loop(0, turns, user_terms, 0)
    if nfar:
        fly("gf", d.ng, gf_copy)

    for name in ("gv1", "gv3_lone", "gv2_lone", "gv2"):
        arrive(name)
    gv = gv_own[...] + gv_recv[1].astype(F32) + gv_recv[2].astype(F32)
    gv_own[...] = gv
    gv_own[:lone, :] += gv_recv[0, :lone, :].astype(F32)
    gv = gv_own[...].astype(BF16)
    gv_own[...] = gv.astype(F32)
    hc = hid // 2
    mine = pl.ds(pl.multiple_of(core * hc, hc), hc)
    other = pl.ds(pl.multiple_of((1 - core) * hc, hc), hc)

    def wc_copy(m):
        return remote(wc_send.at[m], wc_recv.at[m], wc_s.at[m], wc_r.at[m], sibling)

    pre_s[...] = (dot_t(gv, w_out[...]) * slope[...]).astype(BF16)
    wc_send[0] = dot(feats_t[...], pre_s[:, other]).astype(BF16)
    launch("wc0", functools.partial(wc_copy, 0))
    gv_t = gv_own[...].T.astype(BF16)
    wc_send[1] = dot(gv_t, hidden[:, other]).astype(BF16)
    launch("wc1", functools.partial(wc_copy, 1))
    wg_own[0] = dot(feats_t[...], pre_s[:, mine])
    wg_own[1] = dot(gv_t, hidden[:, mine])

    sr = d.srows
    half = d.np // 2

    def w1_copy(k):
        p = plane_peer(k)
        return remote(w1_send.at[p], w1_recv.at[k], w1_s.at[k], w1_r.at[k], plane_dev(p))

    fly("w1", d.np, w1_copy, start=False)
    for m in (0, 1):
        arrive(f"wc{m}")
        total = (wg_own[m] + wc_recv[m].astype(F32)).astype(BF16)
        w1_send[m * half : (m + 1) * half] = total.reshape(half, sr, hc)

        def start(k):
            p = plane_peer(k)

            @pl.when(p < half if m == 0 else p >= half)
            def _():
                w1_copy(k).start()

        each(d.np, start)

    def out_copy(i):
        pairs = [(item_v, out_item), (gu_out, out_user), (a1.at[core], out_w.at[core]), (a1.at[1 - core], out_w.at[1 - core])]
        return pltpu.make_async_copy(*pairs[i], out_s.at[i])

    item_v[...] = gv_own[...] + dot_t(pre_s[...], w_in[...])
    out_copy(0).start()
    tails.append(lambda: out_copy(0).wait())
    tails.remove(users_sent)
    users_sent()
    sent("vecs1", "vecs2", "vecs3", "valid1", "valid2", "valid3", "st_a", "st_b")
    sent("gv1", "gv2", "gv3", "gv2_lone", "gv3_lone", "wc0", "wc1")
    if nfar:
        land("gf")
        gf_sum[...] = gf_send[item].astype(F32) + sum(gf_recv[k].astype(F32) for k in range(1, d.ng))
        fly("gf2", nfar + 1, gf2_copy)
    land("w1")
    part = w1_send[plane].astype(F32)
    for k in range(1, d.np):
        part = part + w1_recv[k].astype(F32)
    wz[z] = part.astype(BF16)

    def wz_copy(k, slot):
        return remote(wz.at[slot], wz.at[slot], wz_s.at[k], wz_r.at[k], z_dev(k))

    fly("wz", d.nz, lambda k: wz_copy(k, z), lambda k: wz_copy(k, back_by(z, k, d.nz)))

    land("gu")
    gu_sum[...] += sum(gu_recv[k].astype(F32) for k in range(1, d.nz) if k < 3 or k > d.nz - 3)

    def rows_of(i):
        return pl.ds(pl.multiple_of(i * us, us), us)

    def g2_copy(k):
        to = lax.rem(item + k, d.ng)
        return remote(gu_sum.at[rows_of(to), :], gu2_recv.at[k], g2_s.at[k], g2_r.at[k], group_dev(k))

    fly("g2", d.ng, g2_copy)
    sent("w1", "gu")
    land("wz")
    a1[core, plane] = sum(wz[k].astype(F32) for k in range(d.nz)).astype(BF16)

    def w4_copy(k, slot):
        there = a1.at[core, slot]
        return remote(there, there, w4_s.at[k], w4_r.at[k], plane_dev(plane_peer(k)))

    fly("w4", d.np, lambda k: w4_copy(k, plane), lambda k: w4_copy(k, back_by(plane, k, d.np)))

    land("g2")
    total = gu_sum[rows_of(item), :] + sum(gu2_recv[k] for k in range(1, d.ng))
    if nfar:
        land("gf2")
        total = total + sum(gf2_recv[i] for i in range(nfar))
        sent("gf", "gf2")
    gu_out[rows_of(item), :] = total

    def g3_copy(k, at):
        there = gu_out.at[rows_of(at), :]
        return remote(there, there, g3_s.at[k], g3_r.at[k], group_dev(k))

    fly("g3", d.ng, lambda k: g3_copy(k, item), lambda k: g3_copy(k, back_by(item, k, d.ng)))
    sent("wz", "g2")

    per_group = d.np // d.groups

    def w5_copy(g, of):
        there = a1.at[of, pl.ds(g * per_group, per_group)]
        return remote(there, there, w5_s.at[g], w5_r.at[g], sibling)

    for g in range(d.groups):
        for slot in range(g * per_group, (g + 1) * per_group):

            @pl.when(slot != plane)
            def _():
                w4_copy(back_by(plane, slot, d.np), slot).wait_recv()

        w5_copy(g, core).start()
    flights["w4"][3] = True
    out_copy(2).start()
    land("g3")
    out_copy(1).start()
    for g in range(d.groups):
        w5_copy(g, 1 - core).wait_recv()
    out_copy(3).start()

    finish()
    for g in range(d.groups):
        w5_copy(g, core).wait_send()
    for i in (1, 2, 3):
        out_copy(i).wait()


def unpack(d, user_ref, item_ref, w_ref, out_user, out_item, out_w_in, out_w_out, user_v, item_v, w_v, w_in_v, w_out_v, sems):
    half, hc = d.np // 2, d.scols
    loads = [(w_ref.at[h, m], w_v.at[h, m]) for m in (1, 0) for h in range(2)]
    loads += [(item_ref, item_v), (user_ref, user_v)]
    loads = [pltpu.make_async_copy(src, dst, sems.at[i]) for i, (src, dst) in enumerate(loads)]
    for copy in loads:
        copy.start()
    stores = [(w_out_v, out_w_out), (w_in_v, out_w_in), (item_v, out_item), (user_v, out_user)]
    stores = [pltpu.make_async_copy(src, dst, sems.at[6 + i]) for i, (src, dst) in enumerate(stores)]
    for m in (1, 0):
        for h in range(2):
            loads[2 * (1 - m) + h].wait()
            block = w_v[h, m].astype(F32).reshape(d.emb, hc)
            at = slice(h * hc, (h + 1) * hc)
            if m == 0:
                w_in_v[:, at] = block
            else:
                w_out_v[at, :] = block.T
        stores[1 - m].start()
    for i in (4, 5):
        loads[i].wait()
        stores[i - 2].start()
    for copy in stores:
        copy.wait()


def body(phys, user_vecs, row_weight, positive, item_feats, valid, w_in, w_out):
    ub, emb = user_vecs.shape
    ib, hid = item_feats.shape[0], w_in.shape[1]
    d = Dims(phys, ub, ib, emb, hid)
    vm = pltpu.VMEM
    us = ub // d.ng
    scratch = [
        vm((ib, emb), BF16),
        vm((emb, hid), BF16),
        vm((hid, emb), BF16),
        vm((ub,), BF16),
        vm((ub,), jnp.int32),
        vm((ib,), jnp.int32),
        vm((ib, emb), F32),
        vm((d.nz, ub, emb), BF16),
        vm((d.nz, 2, ub), F32),
        vm((d.nj, ib, emb), BF16),
        vm((d.nj, 1, ib), F32),
        vm((d.nj, ib, 128), F32),
        vm((emb, d.items), BF16),
        vm((ib, hid), BF16),
        vm((ib, hid), F32),
        vm((d.items, d.users), F32),
        vm((d.items, d.users), BF16),
        vm((d.nk, 8, d.users), F32),
        vm((d.nk, 8, d.users), F32),
        vm((d.nk, 8, d.users), F32),
        vm((8, d.users), jnp.int32),
        vm((1, d.users), F32),
        vm((1, d.users), F32),
        vm((d.ng, 1, d.users), F32),
        vm((1, d.users), F32),
        vm((d.nz, 1, d.users), F32),
        vm((d.nj, ib, emb), BF16),
        vm((d.nj, ib, emb), BF16),
        vm((ib, emb), F32),
        vm((d.nz, ub, emb), BF16),
        vm((d.nz, ub, emb), BF16),
        vm((ub, emb), F32),
        vm((d.ng, us, emb), F32),
        vm((ub, emb), F32),
        vm((d.ng, max(1, d.nfar), us, emb), BF16),
        vm((d.ng, max(1, d.nfar), us, emb), BF16),
        vm((max(1, d.nfar), us, emb), F32),
        vm((max(1, d.nfar), us, emb), F32),
        vm((2, emb, hid // 2), F32),
        vm((ib, hid), BF16),
        vm((emb, ib), BF16),
        vm((2, emb, hid // 2), BF16),
        vm((2, emb, hid // 2), BF16),
        vm((d.np, d.srows, d.scols), BF16),
        vm((d.np, d.srows, d.scols), BF16),
        vm((d.nz, d.srows, d.scols), BF16),
        vm((2, d.np, d.srows, d.scols), BF16),
    ]
    dma = pltpu.SemaphoreType.DMA
    sems = [dma((7,)), dma((4,))]
    for n in (d.nz, d.nz, d.nj, d.nj, d.ng, d.nz, 5, d.nz, d.ng, d.ng, 2, d.np, d.nz, d.np, d.groups, d.ng, d.nz):
        sems += [dma((n,)), dma((n,))]
    where = pl.BlockSpec(memory_space=pl.ANY)
    parts = pl.pallas_call(
        functools.partial(kernel, d),
        out_shape=(
            jax.ShapeDtypeStruct((ub, emb), F32),
            jax.ShapeDtypeStruct((ib, emb), F32),
            jax.ShapeDtypeStruct((2, d.np, d.srows, d.scols), BF16),
        ),
        in_specs=[where] * 7,
        out_specs=(where,) * 3,
        scratch_shapes=scratch + sems,
        compiler_params=pltpu.CompilerParams(
            collective_id=0, has_side_effects=True, vmem_limit_bytes=56 * 1024 * 1024
        ),
        cost_estimate=pl.CostEstimate(
            flops=6 * d.users * d.items * emb,
            bytes_accessed=4 * 1024 * 1024,
            transcendentals=d.users * d.items,
        ),
    )(user_vecs, row_weight, positive, item_feats, valid, w_in, w_out)
    user, item, weights = parts
    weights = weights.reshape(2, 2, d.np // 2, d.srows, d.scols)
    return pl.pallas_call(
        functools.partial(unpack, d),
        out_shape=(
            jax.ShapeDtypeStruct((ub, emb), F32),
            jax.ShapeDtypeStruct((ib, emb), F32),
            jax.ShapeDtypeStruct((emb, hid), F32),
            jax.ShapeDtypeStruct((hid, emb), F32),
        ),
        in_specs=[where] * 3,
        out_specs=(where,) * 4,
        scratch_shapes=[
            vm((ub, emb), F32),
            vm((ib, emb), F32),
            vm(weights.shape, BF16),
            vm((emb, hid), F32),
            vm((hid, emb), F32),
            dma((10,)),
        ],
    )(user, item, weights)


def build(mesh, phys):
    return jax.shard_map(
        functools.partial(body, phys),
        mesh=mesh,
        in_specs=(
            P("user", None),
            P("user"),
            P("user"),
            P(("item", "user"), None),
            P(("item", "user")),
            P(),
            P(),
        ),
        out_specs=(P("user", None), P(("item", "user"), None), P(), P()),
        check_vma=False,
    )


def solution(mesh):
    return build(mesh, (4, 2, 2, 8, 2))
```

```python
import functools

import jax
import jax.numpy as jnp
from jax import lax
from jax.experimental import pallas as pl
from jax.experimental.pallas import tpu as pltpu
from jax.sharding import PartitionSpec as P

MESH = pl.DeviceIdType.MESH
F32 = jnp.float32
BF16 = jnp.bfloat16
DEAD = -1e30
FLOOR = -1e29


def dot(a, b):
    return jnp.dot(a, b, preferred_element_type=F32)


def dot_t(a, b):
    return lax.dot_general(a, b, (((1,), (1,)), ((), ())), preferred_element_type=F32)


class Dims:
    def __init__(self, phys, ub, ib, emb, hid):
        self.ny, self.nxh, self.nxl, self.nz, self.nc = phys
        self.ub, self.ib, self.emb, self.hid = ub, ib, emb, hid
        self.ng = self.ny * self.nxh
        self.np = self.ng * self.nxl
        self.nj = self.nxl * self.nc
        self.users = self.nz * ub
        self.items = self.nj * ib
        self.chunk = min(256, ib)
        self.nk = self.items // self.chunk
        self.srows = 2 * emb // self.np
        self.scols = hid // 2
        self.groups = min(4, self.np)
        self.nfar = max(0, self.nz - 5)


def kernel(
    d,
    users_in, weight_in, pos_in, feats_in, valid_in, w_in_in, w_out_in,
    out_user, out_item, out_w,
    feats, w_in, w_out, weight_v, pos_v, valid_v, item_v, users, meta, vecs, valid, bias, vec_t, hidden, slope, expo, grad,
    peak_s, total_s, factor, tile_s, weight_s,
    st_own, st_a, st_own2, st_b,
    gv_send, gv_recv, gv_own, gu_send, gu_recv, gu_sum, gu2_recv, gu_out, gf_send, gf_recv, gf_sum, gf2_recv,
    wg_own, pre_s, feats_t, wc_send, wc_recv, w1_send, w1_recv, wz, a1,
    in_s, out_s, us_s, us_r, me_s, me_r, ve_s, ve_r, va_s, va_r, sa_s, sa_r, sb_s, sb_r,
    gv_s, gv_r, gu_s, gu_r, g2_s, g2_r, g3_s, g3_r,
    wc_s, wc_r, w1_s, w1_r, wz_s, wz_r, w4_s, w4_r, w5_s, w5_r, gf_s, gf_r, f2_s, f2_r,
):
    ub, ib, emb, hid = d.ub, d.ib, d.emb, d.hid
    item = lax.axis_index("item")
    user = lax.axis_index("user")
    core = lax.rem(user, d.nc)
    z = lax.rem(lax.div(user, d.nc), d.nz)
    xl = lax.div(user, d.nc * d.nz)
    plane = item * d.nxl + xl

    def dev(item_, xl_, z_, core_):
        return (item_, (xl_ * d.nz + z_) * d.nc + core_)

    def back_by(here, k, n):
        return lax.rem(here + n - k, n)

    def z_peer(k):
        return lax.rem(z + k, d.nz)

    def z_dev(k):
        return dev(item, xl, z_peer(k), core)

    def group_dev(k):
        return dev(lax.rem(item + k, d.ng), xl, z, core)

    def plane_peer(k):
        return lax.rem(plane + k, d.np)

    def plane_dev(p):
        return dev(lax.div(p, d.nxl), lax.rem(p, d.nxl), z, core)

    sibling = dev(item, xl, z, 1 - core)
    across = dev(item, 1 - xl, z, core)
    diagonal = dev(item, 1 - xl, z, 1 - core)

    def remote(src, dst, send, recv, to):
        return pltpu.make_async_remote_copy(
            src_ref=src, dst_ref=dst, send_sem=send, recv_sem=recv, device_id=to, device_id_type=MESH
        )

    def each(n, fn):
        def step(k, carry):
            fn(k)
            return carry

        lax.fori_loop(1, n, step, 0)

    flights = {}

    def fly(name, n, copy_out, copy_in=None, start=True):
        flights[name] = [n, copy_out, copy_in or copy_out, False]
        if start:
            each(n, lambda k: copy_out(k).start())

    def land(name):
        n, _, copy_in, _ = flights[name]
        each(n, lambda k: copy_in(k).wait_recv())
        flights[name][3] = True

    def sent(*names):
        for name in names:
            if name in flights:
                n, copy_out, _, landed = flights.pop(name)
                each(n, lambda k: copy_out(k).wait_send())
            else:
                make, landed = singles.pop(name)
                make().wait_send()

    tails = []
    singles = {}

    def launch(name, make):
        singles[name] = [make, False]
        make().start()

    def arrive(name):
        singles[name][0]().wait_recv()
        singles[name][1] = True

    def finish():
        for wait in tails:
            wait()
        for name in list(flights):
            if not flights[name][3]:
                land(name)
            sent(name)
        for name in list(singles):
            if not singles[name][1]:
                arrive(name)
            sent(name)

    barrier = pltpu.get_barrier_semaphore()

    def greet(to):
        pl.semaphore_signal(barrier, inc=1, device_id=to, device_id_type=MESH)

    each(d.nz, lambda k: greet(z_dev(k)))
    each(d.np, lambda k: greet(plane_dev(plane_peer(k))))
    greet(sibling)
    greet(diagonal)

    inputs = [(feats_in, feats), (w_in_in, w_in), (w_out_in, w_out), (users_in, users.at[z])]
    inputs += [(weight_in, weight_v), (pos_in, pos_v), (valid_in, valid_v)]
    inputs = [pltpu.make_async_copy(src, dst, in_s.at[i]) for i, (src, dst) in enumerate(inputs)]
    for copy in inputs:
        copy.start()

    for copy in inputs:
        copy.wait()
    pos = pos_v[...].reshape(1, ub)
    meta[z] = jnp.concatenate([pos.astype(F32), weight_v[...].reshape(1, ub).astype(F32)], axis=0)
    valid[0] = valid_v[...].reshape(1, ib).astype(F32)
    x = feats[...]
    pre = dot(x, w_in[...])
    hid_t = (pre * jax.nn.sigmoid(pre)).astype(BF16)
    hidden[...] = hid_t
    slope[...] = pre
    vecs[0] = (x.astype(F32) + dot(hid_t, w_out[...])).astype(BF16)
    pl.semaphore_wait(barrier, d.nz - 1 + d.np - 1 + 2)

    far = d.nz // 2
    direct = [k for k in (2, d.nz - 2, 1, d.nz - 1) if 0 < k < d.nz]
    direct = sorted(set(direct), key=direct.index)
    handed = [k for k in range(1, d.nz) if k not in direct]
    order = [0] + direct + sorted(handed, key=lambda k: k == far)

    def hops_of(step):
        k = 0
        for i in range(1, d.nz):
            k = jnp.where(step == i, order[i], k)
        return k

    def users_copies(k, slot, to):
        there = z_dev(to)
        return [
            remote(users.at[slot], users.at[slot], us_s.at[k], us_r.at[k], there),
            remote(meta.at[slot], meta.at[slot], me_s.at[k], me_r.at[k], there),
        ]

    def users_start(k, slot, to):
        for copy in users_copies(k, slot, to):
            copy.start()

    def users_sent():
        for k in range(1, d.nz):
            for copy in users_copies(k, z, 1):
                copy.wait_send()

    def users_arrive(k, slot):
        for copy in users_copies(k, slot, 1):
            copy.wait_recv()

    def hand_on_users(k):
        slot = back_by(z, k, d.nz)
        ahead = k == 2
        users_start(3 if ahead else d.nz - 3, slot, 1 if ahead else d.nz - 1)

        @pl.when(core == (0 if ahead else 1))
        def _():
            users_start(far, slot, 2 if ahead else d.nz - 2)

    def vecs_copy(j):
        return remote(vecs.at[j // 3 * 2], vecs.at[j], ve_s.at[j], ve_r.at[j], across if j == 2 else sibling)

    def valid_copy(j):
        return remote(valid.at[j // 3 * 2], valid.at[j], va_s.at[j], va_r.at[j], across if j == 2 else sibling)

    for j in (2, 1):
        launch(f"vecs{j}", functools.partial(vecs_copy, j))
        launch(f"valid{j}", functools.partial(valid_copy, j))
    for k in direct:
        users_start(k, z, k)
    tails.append(users_sent)

    def vec_arrives(j):
        arrive(f"vecs{j}")
        arrive(f"valid{j}")

    def local_tile(pos):
        block = pos // ib
        p_core = block % d.nc
        p_z = block // d.nc % d.nz
        p_xl = block // (d.nc * d.nz) % d.nxl
        p_item = block // (d.nc * d.nz * d.nxl)
        j = (p_xl + d.nxl - xl) % d.nxl * d.nc + (p_core + d.nc - core) % d.nc
        here = (p_item == item) & (p_z == z)
        row = jnp.where(here, j * ib + pos % ib, -1)
        lane = lax.broadcasted_iota(jnp.int32, (8, ub), 0)
        return jnp.where(here & (lane == row % 8), row // 8, -1)

    def set_bias(j):
        bias[j] = (jnp.broadcast_to(valid[j], (128, ib)).T - 1.0) * -DEAD

    def enter(slot):
        lanes = pl.ds(pl.multiple_of(slot * ub, ub), ub)
        tile_s[:, lanes] = local_tile(meta[slot, 0:1, :].astype(jnp.int32))
        weight_s[:, lanes] = meta[slot, 1:2, :]

    def score(j, slot):
        at = pl.multiple_of(slot * ub, ub)
        tile = lax.broadcasted_iota(jnp.int32, (d.chunk // 8, 8, 128), 0)
        for c in range(ib // d.chunk):
            rows = slice(c * d.chunk, (c + 1) * d.chunk)
            s = dot_t(vecs[j, rows, :], users[slot])
            b = bias[j, rows, :].reshape(d.chunk // 8, 8, 128)
            ck = j * (ib // d.chunk) + c
            first = pl.multiple_of(ck * d.chunk, d.chunk)
            for h in range(ub // 128):
                lanes = pl.ds(pl.multiple_of(at + h * 128, 128), 128)
                sh = s[:, h * 128 : (h + 1) * 128].reshape(d.chunk // 8, 8, 128)
                hit = tile == (tile_s[:, lanes] - ck * (d.chunk // 8))[None]
                x = jnp.where(hit, sh, sh + b)
                peak = jnp.maximum(jnp.max(x, axis=0), FLOOR)
                e = jnp.exp(x - peak[None])
                peak_s[ck, :, lanes] = peak
                total_s[ck, :, lanes] = jnp.sum(e, axis=0)
                expo[pl.ds(first, d.chunk), lanes] = e.reshape(d.chunk, 128)

    first = min(5, d.nz)
    groups = [order[1:3], order[3:5]] if d.nz >= 5 else [order[1:first]]
    ng = len(groups)

    def early_steps(i, carry):
        pair = lax.div(i, ng)
        turn = lax.rem(i, ng)

        for at, group in enumerate(groups):

            @pl.when(i == at)
            def _():
                for k in group:
                    slot = back_by(z, k, d.nz)
                    users_arrive(k, slot)
                    if handed and k in (2, d.nz - 2):
                        hand_on_users(k)
                    enter(slot)

        @pl.when(i == ng - 1)
        def _():
            vec_arrives(2)
            launch("vecs3", functools.partial(vecs_copy, 3))
            launch("valid3", functools.partial(valid_copy, 3))

        for q in range(len(groups[0])):
            k = functools.reduce(lambda a, g: jnp.where(turn == g, groups[g][q], a), range(1, ng), groups[0][q])
            slot = back_by(z, k, d.nz)
            score(pair * 2, slot)
            score(pair * 2 + 1, slot)
        return carry

    def late_steps(step, carry):
        k = hops_of(step)
        slot = back_by(z, k, d.nz)
        users_arrive(k, slot)
        enter(slot)
        for j in range(d.nj):
            score(j, slot)
        return carry

    enter(z)
    set_bias(0)
    score(0, z)
    vec_arrives(1)
    set_bias(1)
    score(1, z)
    lax.fori_loop(0, ng, early_steps, 0)
    set_bias(2)
    score(2, z)
    vec_arrives(3)
    set_bias(3)
    score(3, z)
    lax.fori_loop(ng, 2 * ng, early_steps, 0)
    lax.fori_loop(first, d.nz, late_steps, 0)

    def merge(logs):
        peak = functools.reduce(jnp.maximum, logs)
        return peak + jnp.log(sum(jnp.exp(v - peak) for v in logs))

    peak8 = functools.reduce(jnp.maximum, [peak_s[c] for c in range(d.nk)])
    peak = jnp.max(peak8, axis=0, keepdims=True)
    total8 = sum(total_s[c] * jnp.exp(peak_s[c] - peak) for c in range(d.nk))
    st_own[...] = peak + jnp.log(jnp.maximum(jnp.sum(total8, axis=0, keepdims=True), 1e-30))

    def st_a_copy(k):
        return remote(st_own, st_a.at[k], sa_s.at[k], sa_r.at[k], group_dev(k))

    def st_b_copy(k):
        return remote(st_own2, st_b.at[k], sb_s.at[k], sb_r.at[k], z_dev(k))

    fly("st_a", d.ng, st_a_copy)
    for j in range(d.nj):
        vec_t[:, j * ib : (j + 1) * ib] = vecs[j].astype(F32).T.astype(BF16)

    pre = slope[...]
    sigma = jax.nn.sigmoid(pre)
    slope[...] = sigma * (1.0 + pre * (1.0 - sigma))
    feats_t[...] = feats[...].astype(F32).T.astype(BF16)
    land("st_a")
    st_own2[...] = merge([st_own[...]] + [st_a[k] for k in range(1, d.ng)])
    fly("st_b", d.nz, st_b_copy)
    land("st_b")
    log_total = merge([st_own2[...]] + [st_b[k] for k in range(1, d.nz)])
    for c in range(d.nk):
        factor[c] = weight_s[...] * jnp.exp(peak_s[c] - log_total)

    lone = ib // 4

    def gv_copy(name):
        i, rows, slot, to = {
            "gv3": (3, slice(lone, ib), 3, sibling),
            "gv3_lone": (3, slice(0, lone), 0, diagonal),
            "gv2": (2, slice(lone, ib), 2, across),
            "gv2_lone": (2, slice(0, lone), 2, across),
            "gv1": (1, slice(0, ib), 1, sibling),
        }[name]
        n = ("gv1", "gv2", "gv3", "gv2_lone", "gv3_lone").index(name)
        return remote(gv_send.at[i, rows], gv_recv.at[slot, rows], gv_s.at[n], gv_r.at[n], to)

    def gv_launch(name):
        launch(name, functools.partial(gv_copy, name))

    width = min(512, d.users)
    per = ib // d.chunk

    def grads(t, carry):
        j = 3 - t
        rows = pl.ds(pl.multiple_of(j * ib, ib), ib)
        acc = jnp.zeros((ib, emb), F32)
        tile = lax.broadcasted_iota(jnp.int32, (ib // 8, 8, width), 0)
        for u in range(0, d.users, width):
            lanes = slice(u, u + width)
            e = expo[rows, lanes].reshape(per, d.chunk // 8, 8, width)
            e = (e * factor[pl.ds(j * per, per), :, lanes][:, None]).reshape(ib // 8, 8, width)
            hit = tile == (tile_s[:, lanes] - j * (ib // 8))[None]
            g = jnp.where(hit, e - weight_s[:, lanes][None], e).reshape(ib, width).astype(BF16)
            grad[rows, lanes] = g
            acc = acc + dot(g, users[...].reshape(d.users, emb)[lanes, :])
        gv_own[...] = acc

        @pl.when(t == 0)
        def _():
            gv_send[3] = gv_own[...].astype(BF16)
            gv_launch("gv3_lone")
            gv_launch("gv3")

        @pl.when(t == 1)
        def _():
            gv_send[2, :lone] = gv_own[:lone, :].astype(BF16)
            gv_launch("gv2_lone")
            arrive("gv3")
            gv_send[2, lone:] = (gv_own[lone:, :] + gv_recv[3, lone:, :].astype(F32)).astype(BF16)
            gv_launch("gv2")

        @pl.when(t == 2)
        def _():
            gv_send[1] = gv_own[...].astype(BF16)
            gv_launch("gv1")

        return carry

    lax.fori_loop(0, 4, grads, 0)

    us = ub // d.ng
    nfar = d.nfar
    zs = width // ub
    turns = d.users // width
    offsets = sorted(range(turns), key=lambda o: -min(o, turns - o))

    def gu_copy(k):
        return remote(gu_send.at[z_peer(k)], gu_recv.at[k], gu_s.at[k], gu_r.at[k], z_dev(k))

    def user_terms(i, carry):
        offset = functools.reduce(lambda a, t: jnp.where(i == t, offsets[t], a), range(1, turns), offsets[0])
        q = lax.rem(lax.div(z, zs) + offset, turns)
        lanes = pl.ds(pl.multiple_of(q * width, width), width)
        terms = dot(vec_t[...], grad[:, lanes]).T
        for e in range(zs):
            slot = q * zs + e
            part = terms[e * ub : (e + 1) * ub, :]

            @pl.when(slot == z)
            def _():
                gu_sum[...] = part

            k = back_by(slot, z, d.nz)
            is_near = (slot != z) & ((k < 3) | (k > d.nz - 3))

            @pl.when(is_near)
            def _():
                gu_send[slot] = part.astype(BF16)
                gu_copy(k).start()

            if nfar:

                @pl.when((k >= 3) & (k <= d.nz - 3))
                def _():
                    for g in range(d.ng):
                        gf_send[g, k - 3] = part[g * us : (g + 1) * us, :].astype(BF16)

        return carry

    def near_hops(i):
        return jnp.where(i < 3, i, i + nfar)

    def gf_copy(k):
        to = lax.rem(item + k, d.ng)
        return remote(gf_send.at[to], gf_recv.at[k], gf_s.at[k], gf_r.at[k], dev(to, xl, z, core))

    def gf2_copy(i):
        return remote(gf_sum.at[i - 1], gf2_recv.at[i - 1], f2_s.at[i], f2_r.at[i], z_dev(i + 2))

    fly("gu", d.nz - nfar, lambda i: gu_copy(near_hops(i)), start=False)
    lax.fori_loop(0, turns, user_terms, 0)
    if nfar:
        fly("gf", d.ng, gf_copy)

    for name in ("gv1", "gv3_lone", "gv2_lone", "gv2"):
        arrive(name)
    gv = gv_own[...] + gv_recv[1].astype(F32) + gv_recv[2].astype(F32)
    gv_own[...] = gv
    gv_own[:lone, :] += gv_recv[0, :lone, :].astype(F32)
    gv = gv_own[...].astype(BF16)
    gv_own[...] = gv.astype(F32)
    hc = hid // 2
    mine = pl.ds(pl.multiple_of(core * hc, hc), hc)
    other = pl.ds(pl.multiple_of((1 - core) * hc, hc), hc)

    def wc_copy(m):
        return remote(wc_send.at[m], wc_recv.at[m], wc_s.at[m], wc_r.at[m], sibling)

    pre_s[...] = (dot_t(gv, w_out[...]) * slope[...]).astype(BF16)
    wc_send[0] = dot(feats_t[...], pre_s[:, other]).astype(BF16)
    launch("wc0", functools.partial(wc_copy, 0))
    gv_t = gv_own[...].T.astype(BF16)
    wc_send[1] = dot(gv_t, hidden[:, other]).astype(BF16)
    launch("wc1", functools.partial(wc_copy, 1))
    wg_own[0] = dot(feats_t[...], pre_s[:, mine])
    wg_own[1] = dot(gv_t, hidden[:, mine])

    sr = d.srows
    half = d.np // 2

    def w1_copy(k):
        p = plane_peer(k)
        return remote(w1_send.at[p], w1_recv.at[k], w1_s.at[k], w1_r.at[k], plane_dev(p))

    fly("w1", d.np, w1_copy, start=False)
    for m in (0, 1):
        arrive(f"wc{m}")
        total = (wg_own[m] + wc_recv[m].astype(F32)).astype(BF16)
        w1_send[m * half : (m + 1) * half] = total.reshape(half, sr, hc)

        def start(k):
            p = plane_peer(k)

            @pl.when(p < half if m == 0 else p >= half)
            def _():
                w1_copy(k).start()

        each(d.np, start)

    def out_copy(i):
        pairs = [(item_v, out_item), (gu_out, out_user), (a1.at[core], out_w.at[core]), (a1.at[1 - core], out_w.at[1 - core])]
        return pltpu.make_async_copy(*pairs[i], out_s.at[i])

    item_v[...] = gv_own[...] + dot_t(pre_s[...], w_in[...])
    out_copy(0).start()
    tails.append(lambda: out_copy(0).wait())
    tails.remove(users_sent)
    users_sent()
    sent("vecs1", "vecs2", "vecs3", "valid1", "valid2", "valid3", "st_a", "st_b")
    sent("gv1", "gv2", "gv3", "gv2_lone", "gv3_lone", "wc0", "wc1")
    if nfar:
        land("gf")
        gf_sum[...] = gf_send[item].astype(F32) + sum(gf_recv[k].astype(F32) for k in range(1, d.ng))
        fly("gf2", nfar + 1, gf2_copy)
    land("w1")
    part = w1_send[plane].astype(F32)
    for k in range(1, d.np):
        part = part + w1_recv[k].astype(F32)
    wz[z] = part.astype(BF16)

    def wz_copy(k, slot):
        return remote(wz.at[slot], wz.at[slot], wz_s.at[k], wz_r.at[k], z_dev(k))

    fly("wz", d.nz, lambda k: wz_copy(k, z), lambda k: wz_copy(k, back_by(z, k, d.nz)))

    land("gu")
    gu_sum[...] += sum(gu_recv[k].astype(F32) for k in range(1, d.nz) if k < 3 or k > d.nz - 3)

    def rows_of(i):
        return pl.ds(pl.multiple_of(i * us, us), us)

    def g2_copy(k):
        to = lax.rem(item + k, d.ng)
        return remote(gu_sum.at[rows_of(to), :], gu2_recv.at[k], g2_s.at[k], g2_r.at[k], group_dev(k))

    fly("g2", d.ng, g2_copy)
    sent("w1", "gu")
    land("wz")
    a1[core, plane] = sum(wz[k].astype(F32) for k in range(d.nz)).astype(BF16)

    def w4_copy(k, slot):
        there = a1.at[core, slot]
        return remote(there, there, w4_s.at[k], w4_r.at[k], plane_dev(plane_peer(k)))

    fly("w4", d.np, lambda k: w4_copy(k, plane), lambda k: w4_copy(k, back_by(plane, k, d.np)))

    land("g2")
    total = gu_sum[rows_of(item), :] + sum(gu2_recv[k] for k in range(1, d.ng))
    if nfar:
        land("gf2")
        total = total + sum(gf2_recv[i] for i in range(nfar))
        sent("gf", "gf2")
    gu_out[rows_of(item), :] = total

    def g3_copy(k, at):
        there = gu_out.at[rows_of(at), :]
        return remote(there, there, g3_s.at[k], g3_r.at[k], group_dev(k))

    fly("g3", d.ng, lambda k: g3_copy(k, item), lambda k: g3_copy(k, back_by(item, k, d.ng)))
    sent("wz", "g2")

    per_group = d.np // d.groups

    def w5_copy(g, of):
        there = a1.at[of, pl.ds(g * per_group, per_group)]
        return remote(there, there, w5_s.at[g], w5_r.at[g], sibling)

    for g in range(d.groups):
        for slot in range(g * per_group, (g + 1) * per_group):

            @pl.when(slot != plane)
            def _():
                w4_copy(back_by(plane, slot, d.np), slot).wait_recv()

        w5_copy(g, core).start()
    flights["w4"][3] = True
    out_copy(2).start()
    land("g3")
    out_copy(1).start()
    for g in range(d.groups):
        w5_copy(g, 1 - core).wait_recv()
    out_copy(3).start()

    finish()
    for g in range(d.groups):
        w5_copy(g, core).wait_send()
    for i in (1, 2, 3):
        out_copy(i).wait()


def unpack(d, user_ref, item_ref, w_ref, out_user, out_item, out_w_in, out_w_out, user_v, item_v, w_v, w_in_v, w_out_v, sems):
    half, hc = d.np // 2, d.scols
    loads = [(w_ref.at[h, m], w_v.at[h, m]) for m in (1, 0) for h in range(2)]
    loads += [(item_ref, item_v), (user_ref, user_v)]
    loads = [pltpu.make_async_copy(src, dst, sems.at[i]) for i, (src, dst) in enumerate(loads)]
    for copy in loads:
        copy.start()
    stores = [(w_out_v, out_w_out), (w_in_v, out_w_in), (item_v, out_item), (user_v, out_user)]
    stores = [pltpu.make_async_copy(src, dst, sems.at[6 + i]) for i, (src, dst) in enumerate(stores)]
    for m in (1, 0):
        for h in range(2):
            loads[2 * (1 - m) + h].wait()
            block = w_v[h, m].astype(F32).reshape(d.emb, hc)
            at = slice(h * hc, (h + 1) * hc)
            if m == 0:
                w_in_v[:, at] = block
            else:
                w_out_v[at, :] = block.T
        stores[1 - m].start()
    for i in (4, 5):
        loads[i].wait()
        stores[i - 2].start()
    for copy in stores:
        copy.wait()


def body(phys, user_vecs, row_weight, positive, item_feats, valid, w_in, w_out):
    ub, emb = user_vecs.shape
    ib, hid = item_feats.shape[0], w_in.shape[1]
    d = Dims(phys, ub, ib, emb, hid)
    vm = pltpu.VMEM
    us = ub // d.ng
    scratch = [
        vm((ib, emb), BF16),
        vm((emb, hid), BF16),
        vm((hid, emb), BF16),
        vm((ub,), BF16),
        vm((ub,), jnp.int32),
        vm((ib,), jnp.int32),
        vm((ib, emb), F32),
        vm((d.nz, ub, emb), BF16),
        vm((d.nz, 2, ub), F32),
        vm((d.nj, ib, emb), BF16),
        vm((d.nj, 1, ib), F32),
        vm((d.nj, ib, 128), F32),
        vm((emb, d.items), BF16),
        vm((ib, hid), BF16),
        vm((ib, hid), F32),
        vm((d.items, d.users), F32),
        vm((d.items, d.users), BF16),
        vm((d.nk, 8, d.users), F32),
        vm((d.nk, 8, d.users), F32),
        vm((d.nk, 8, d.users), F32),
        vm((8, d.users), jnp.int32),
        vm((1, d.users), F32),
        vm((1, d.users), F32),
        vm((d.ng, 1, d.users), F32),
        vm((1, d.users), F32),
        vm((d.nz, 1, d.users), F32),
        vm((d.nj, ib, emb), BF16),
        vm((d.nj, ib, emb), BF16),
        vm((ib, emb), F32),
        vm((d.nz, ub, emb), BF16),
        vm((d.nz, ub, emb), BF16),
        vm((ub, emb), F32),
        vm((d.ng, us, emb), F32),
        vm((ub, emb), F32),
        vm((d.ng, max(1, d.nfar), us, emb), BF16),
        vm((d.ng, max(1, d.nfar), us, emb), BF16),
        vm((max(1, d.nfar), us, emb), F32),
        vm((max(1, d.nfar), us, emb), F32),
        vm((2, emb, hid // 2), F32),
        vm((ib, hid), BF16),
        vm((emb, ib), BF16),
        vm((2, emb, hid // 2), BF16),
        vm((2, emb, hid // 2), BF16),
        vm((d.np, d.srows, d.scols), BF16),
        vm((d.np, d.srows, d.scols), BF16),
        vm((d.nz, d.srows, d.scols), BF16),
        vm((2, d.np, d.srows, d.scols), BF16),
    ]
    dma = pltpu.SemaphoreType.DMA
    sems = [dma((7,)), dma((4,))]
    for n in (d.nz, d.nz, d.nj, d.nj, d.ng, d.nz, 5, d.nz, d.ng, d.ng, 2, d.np, d.nz, d.np, d.groups, d.ng, d.nz):
        sems += [dma((n,)), dma((n,))]
    where = pl.BlockSpec(memory_space=pl.ANY)
    parts = pl.pallas_call(
        functools.partial(kernel, d),
        out_shape=(
            jax.ShapeDtypeStruct((ub, emb), F32),
            jax.ShapeDtypeStruct((ib, emb), F32),
            jax.ShapeDtypeStruct((2, d.np, d.srows, d.scols), BF16),
        ),
        in_specs=[where] * 7,
        out_specs=(where,) * 3,
        scratch_shapes=scratch + sems,
        compiler_params=pltpu.CompilerParams(
            collective_id=0, has_side_effects=True, vmem_limit_bytes=56 * 1024 * 1024
        ),
        cost_estimate=pl.CostEstimate(
            flops=6 * d.users * d.items * emb,
            bytes_accessed=4 * 1024 * 1024,
            transcendentals=d.users * d.items,
        ),
    )(user_vecs, row_weight, positive, item_feats, valid, w_in, w_out)
    user, item, weights = parts
    weights = weights.reshape(2, 2, d.np // 2, d.srows, d.scols)
    return pl.pallas_call(
        functools.partial(unpack, d),
        out_shape=(
            jax.ShapeDtypeStruct((ub, emb), F32),
            jax.ShapeDtypeStruct((ib, emb), F32),
            jax.ShapeDtypeStruct((emb, hid), F32),
            jax.ShapeDtypeStruct((hid, emb), F32),
        ),
        in_specs=[where] * 3,
        out_specs=(where,) * 4,
        scratch_shapes=[
            vm((ub, emb), F32),
            vm((ib, emb), F32),
            vm(weights.shape, BF16),
            vm((emb, hid), F32),
            vm((hid, emb), F32),
            dma((10,)),
        ],
    )(user, item, weights)


def build(mesh, phys):
    return jax.shard_map(
        functools.partial(body, phys),
        mesh=mesh,
        in_specs=(
            P("user", None),
            P("user"),
            P("user"),
            P(("item", "user"), None),
            P(("item", "user")),
            P(),
            P(),
        ),
        out_specs=(P("user", None), P(("item", "user"), None), P(), P()),
        check_vma=False,
    )


def solution(mesh):
    return build(mesh, (4, 2, 2, 8, 2))
```

```python
import functools

import jax
import jax.numpy as jnp
from jax import lax
from jax.experimental import pallas as pl
from jax.experimental.pallas import tpu as pltpu
from jax.sharding import PartitionSpec as P

MESH = pl.DeviceIdType.MESH
F32 = jnp.float32
BF16 = jnp.bfloat16
DEAD = -1e30
FLOOR = -1e29


def dot(a, b):
    return jnp.dot(a, b, preferred_element_type=F32)


def dot_t(a, b):
    return lax.dot_general(a, b, (((1,), (1,)), ((), ())), preferred_element_type=F32)


class Dims:
    def __init__(self, phys, ub, ib, emb, hid):
        self.ny, self.nxh, self.nxl, self.nz, self.nc = phys
        self.ub, self.ib, self.emb, self.hid = ub, ib, emb, hid
        self.ng = self.ny * self.nxh
        self.np = self.ng * self.nxl
        self.nj = self.nxl * self.nc
        self.users = self.nz * ub
        self.items = self.nj * ib
        self.chunk = min(256, ib)
        self.nk = self.items // self.chunk
        self.srows = 2 * emb // self.np
        self.scols = hid // 2
        self.groups = min(4, self.np)
        self.nfar = max(0, self.nz - 5)


def kernel(
    d,
    users_in, weight_in, pos_in, feats_in, valid_in, w_in_in, w_out_in,
    out_user, out_item, out_w,
    feats, w_in, w_out, weight_v, pos_v, valid_v, item_v, users, meta, vecs, valid, bias, vec_t, hidden, slope, expo, grad,
    peak_s, total_s, factor, tile_s, weight_s,
    st_own, st_a, st_own2, st_b,
    gv_send, gv_recv, gv_own, gu_send, gu_recv, gu_sum, gu2_recv, gu_out, gf_send, gf_recv, gf_sum, gf2_recv,
    wg_own, pre_s, feats_t, wc_send, wc_recv, w1_send, w1_recv, wz, a1,
    in_s, out_s, us_s, us_r, me_s, me_r, ve_s, ve_r, va_s, va_r, sa_s, sa_r, sb_s, sb_r,
    gv_s, gv_r, gu_s, gu_r, g2_s, g2_r, g3_s, g3_r,
    wc_s, wc_r, w1_s, w1_r, wz_s, wz_r, w4_s, w4_r, w5_s, w5_r, gf_s, gf_r, f2_s, f2_r,
):
    ub, ib, emb, hid = d.ub, d.ib, d.emb, d.hid
    item = lax.axis_index("item")
    user = lax.axis_index("user")
    core = lax.rem(user, d.nc)
    z = lax.rem(lax.div(user, d.nc), d.nz)
    xl = lax.div(user, d.nc * d.nz)
    plane = item * d.nxl + xl

    def dev(item_, xl_, z_, core_):
        return (item_, (xl_ * d.nz + z_) * d.nc + core_)

    def back_by(here, k, n):
        return lax.rem(here + n - k, n)

    def z_peer(k):
        return lax.rem(z + k, d.nz)

    def z_dev(k):
        return dev(item, xl, z_peer(k), core)

    def group_dev(k):
        return dev(lax.rem(item + k, d.ng), xl, z, core)

    def plane_peer(k):
        return lax.rem(plane + k, d.np)

    def plane_dev(p):
        return dev(lax.div(p, d.nxl), lax.rem(p, d.nxl), z, core)

    sibling = dev(item, xl, z, 1 - core)
    across = dev(item, 1 - xl, z, core)
    diagonal = dev(item, 1 - xl, z, 1 - core)

    def remote(src, dst, send, recv, to):
        return pltpu.make_async_remote_copy(
            src_ref=src, dst_ref=dst, send_sem=send, recv_sem=recv, device_id=to, device_id_type=MESH
        )

    def each(n, fn):
        def step(k, carry):
            fn(k)
            return carry

        lax.fori_loop(1, n, step, 0)

    flights = {}

    def fly(name, n, copy_out, copy_in=None, start=True):
        flights[name] = [n, copy_out, copy_in or copy_out, False]
        if start:
            each(n, lambda k: copy_out(k).start())

    def land(name):
        n, _, copy_in, _ = flights[name]
        each(n, lambda k: copy_in(k).wait_recv())
        flights[name][3] = True

    def sent(*names):
        for name in names:
            if name in flights:
                n, copy_out, _, landed = flights.pop(name)
                each(n, lambda k: copy_out(k).wait_send())
            else:
                make, landed = singles.pop(name)
                make().wait_send()

    tails = []
    singles = {}

    def launch(name, make):
        singles[name] = [make, False]
        make().start()

    def arrive(name):
        singles[name][0]().wait_recv()
        singles[name][1] = True

    def finish():
        for wait in tails:
            wait()
        for name in list(flights):
            if not flights[name][3]:
                land(name)
            sent(name)
        for name in list(singles):
            if not singles[name][1]:
                arrive(name)
            sent(name)

    barrier = pltpu.get_barrier_semaphore()

    def greet(to):
        pl.semaphore_signal(barrier, inc=1, device_id=to, device_id_type=MESH)

    each(d.nz, lambda k: greet(z_dev(k)))
    each(d.np, lambda k: greet(plane_dev(plane_peer(k))))
    greet(sibling)
    greet(diagonal)

    inputs = [(feats_in, feats), (w_in_in, w_in), (w_out_in, w_out), (users_in, users.at[z])]
    inputs += [(weight_in, weight_v), (pos_in, pos_v), (valid_in, valid_v)]
    inputs = [pltpu.make_async_copy(src, dst, in_s.at[i]) for i, (src, dst) in enumerate(inputs)]
    for copy in inputs:
        copy.start()

    for copy in inputs:
        copy.wait()
    pos = pos_v[...].reshape(1, ub)
    meta[z] = jnp.concatenate([pos.astype(F32), weight_v[...].reshape(1, ub).astype(F32)], axis=0)
    valid[0] = valid_v[...].reshape(1, ib).astype(F32)
    x = feats[...]
    pre = dot(x, w_in[...])
    hid_t = (pre * jax.nn.sigmoid(pre)).astype(BF16)
    hidden[...] = hid_t
    slope[...] = pre
    vecs[0] = (x.astype(F32) + dot(hid_t, w_out[...])).astype(BF16)
    pl.semaphore_wait(barrier, d.nz - 1 + d.np - 1 + 2)

    far = d.nz // 2
    direct = [k for k in (2, d.nz - 2, 1, d.nz - 1) if 0 < k < d.nz]
    direct = sorted(set(direct), key=direct.index)
    handed = [k for k in range(1, d.nz) if k not in direct]
    order = [0] + direct + sorted(handed, key=lambda k: k == far)

    def hops_of(step):
        k = 0
        for i in range(1, d.nz):
            k = jnp.where(step == i, order[i], k)
        return k

    def users_copies(k, slot, to):
        there = z_dev(to)
        return [
            remote(users.at[slot], users.at[slot], us_s.at[k], us_r.at[k], there),
            remote(meta.at[slot], meta.at[slot], me_s.at[k], me_r.at[k], there),
        ]

    def users_start(k, slot, to):
        for copy in users_copies(k, slot, to):
            copy.start()

    def users_sent():
        for k in range(1, d.nz):
            for copy in users_copies(k, z, 1):
                copy.wait_send()

    def users_arrive(k, slot):
        for copy in users_copies(k, slot, 1):
            copy.wait_recv()

    def hand_on_users(k):
        slot = back_by(z, k, d.nz)
        ahead = k == 2
        users_start(3 if ahead else d.nz - 3, slot, 1 if ahead else d.nz - 1)

        @pl.when(core == (0 if ahead else 1))
        def _():
            users_start(far, slot, 2 if ahead else d.nz - 2)

    def vecs_copy(j):
        return remote(vecs.at[j // 3 * 2], vecs.at[j], ve_s.at[j], ve_r.at[j], across if j == 2 else sibling)

    def valid_copy(j):
        return remote(valid.at[j // 3 * 2], valid.at[j], va_s.at[j], va_r.at[j], across if j == 2 else sibling)

    for j in (2, 1):
        launch(f"vecs{j}", functools.partial(vecs_copy, j))
        launch(f"valid{j}", functools.partial(valid_copy, j))
    for k in direct:
        users_start(k, z, k)
    tails.append(users_sent)

    def vec_arrives(j):
        arrive(f"vecs{j}")
        arrive(f"valid{j}")

    def local_tile(pos):
        block = pos // ib
        p_core = block % d.nc
        p_z = block // d.nc % d.nz
        p_xl = block // (d.nc * d.nz) % d.nxl
        p_item = block // (d.nc * d.nz * d.nxl)
        j = (p_xl + d.nxl - xl) % d.nxl * d.nc + (p_core + d.nc - core) % d.nc
        here = (p_item == item) & (p_z == z)
        row = jnp.where(here, j * ib + pos % ib, -1)
        lane = lax.broadcasted_iota(jnp.int32, (8, ub), 0)
        return jnp.where(here & (lane == row % 8), row // 8, -1)

    def set_bias(j):
        bias[j] = (jnp.broadcast_to(valid[j], (128, ib)).T - 1.0) * -DEAD

    def enter(slot):
        lanes = pl.ds(pl.multiple_of(slot * ub, ub), ub)
        tile_s[:, lanes] = local_tile(meta[slot, 0:1, :].astype(jnp.int32))
        weight_s[:, lanes] = meta[slot, 1:2, :]

    def score(j, slot):
        at = pl.multiple_of(slot * ub, ub)
        tile = lax.broadcasted_iota(jnp.int32, (d.chunk // 8, 8, 128), 0)
        for c in range(ib // d.chunk):
            rows = slice(c * d.chunk, (c + 1) * d.chunk)
            s = dot_t(vecs[j, rows, :], users[slot])
            b = bias[j, rows, :].reshape(d.chunk // 8, 8, 128)
            ck = j * (ib // d.chunk) + c
            first = pl.multiple_of(ck * d.chunk, d.chunk)
            for h in range(ub // 128):
                lanes = pl.ds(pl.multiple_of(at + h * 128, 128), 128)
                sh = s[:, h * 128 : (h + 1) * 128].reshape(d.chunk // 8, 8, 128)
                hit = tile == (tile_s[:, lanes] - ck * (d.chunk // 8))[None]
                x = jnp.where(hit, sh, sh + b)
                peak = jnp.maximum(jnp.max(x, axis=0), FLOOR)
                e = jnp.exp(x - peak[None])
                peak_s[ck, :, lanes] = peak
                total_s[ck, :, lanes] = jnp.sum(e, axis=0)
                expo[pl.ds(first, d.chunk), lanes] = e.reshape(d.chunk, 128)

    first = min(5, d.nz)
    groups = [order[1:3], order[3:5]] if d.nz >= 5 else [order[1:first]]
    ng = len(groups)

    def early_steps(i, carry):
        pair = lax.div(i, ng)
        turn = lax.rem(i, ng)

        for at, group in enumerate(groups):

            @pl.when(i == at)
            def _():
                for k in group:
                    slot = back_by(z, k, d.nz)
                    users_arrive(k, slot)
                    if handed and k in (2, d.nz - 2):
                        hand_on_users(k)
                    enter(slot)

        @pl.when(i == ng - 1)
        def _():
            vec_arrives(2)
            launch("vecs3", functools.partial(vecs_copy, 3))
            launch("valid3", functools.partial(valid_copy, 3))

        for q in range(len(groups[0])):
            k = functools.reduce(lambda a, g: jnp.where(turn == g, groups[g][q], a), range(1, ng), groups[0][q])
            slot = back_by(z, k, d.nz)
            score(pair * 2, slot)
            score(pair * 2 + 1, slot)
        return carry

    def late_steps(step, carry):
        k = hops_of(step)
        slot = back_by(z, k, d.nz)
        users_arrive(k, slot)
        enter(slot)
        for j in range(d.nj):
            score(j, slot)
        return carry

    enter(z)
    set_bias(0)
    score(0, z)
    vec_arrives(1)
    set_bias(1)
    score(1, z)
    lax.fori_loop(0, ng, early_steps, 0)
    set_bias(2)
    score(2, z)
    vec_arrives(3)
    set_bias(3)
    score(3, z)
    lax.fori_loop(ng, 2 * ng, early_steps, 0)
    lax.fori_loop(first, d.nz, late_steps, 0)

    def merge(logs):
        peak = functools.reduce(jnp.maximum, logs)
        return peak + jnp.log(sum(jnp.exp(v - peak) for v in logs))

    peak8 = functools.reduce(jnp.maximum, [peak_s[c] for c in range(d.nk)])
    peak = jnp.max(peak8, axis=0, keepdims=True)
    total8 = sum(total_s[c] * jnp.exp(peak_s[c] - peak) for c in range(d.nk))
    st_own[...] = peak + jnp.log(jnp.maximum(jnp.sum(total8, axis=0, keepdims=True), 1e-30))

    def st_a_copy(k):
        return remote(st_own, st_a.at[k], sa_s.at[k], sa_r.at[k], group_dev(k))

    def st_b_copy(k):
        return remote(st_own2, st_b.at[k], sb_s.at[k], sb_r.at[k], z_dev(k))

    fly("st_a", d.ng, st_a_copy)
    for j in range(d.nj):
        vec_t[:, j * ib : (j + 1) * ib] = vecs[j].astype(F32).T.astype(BF16)

    pre = slope[...]
    sigma = jax.nn.sigmoid(pre)
    slope[...] = sigma * (1.0 + pre * (1.0 - sigma))
    feats_t[...] = feats[...].astype(F32).T.astype(BF16)
    land("st_a")
    st_own2[...] = merge([st_own[...]] + [st_a[k] for k in range(1, d.ng)])
    fly("st_b", d.nz, st_b_copy)
    land("st_b")
    log_total = merge([st_own2[...]] + [st_b[k] for k in range(1, d.nz)])
    for c in range(d.nk):
        factor[c] = weight_s[...] * jnp.exp(peak_s[c] - log_total)

    lone = ib // 4

    def gv_copy(name):
        i, rows, slot, to = {
            "gv3": (3, slice(lone, ib), 3, sibling),
            "gv3_lone": (3, slice(0, lone), 0, diagonal),
            "gv2": (2, slice(lone, ib), 2, across),
            "gv2_lone": (2, slice(0, lone), 2, across),
            "gv1": (1, slice(0, ib), 1, sibling),
        }[name]
        n = ("gv1", "gv2", "gv3", "gv2_lone", "gv3_lone").index(name)
        return remote(gv_send.at[i, rows], gv_recv.at[slot, rows], gv_s.at[n], gv_r.at[n], to)

    def gv_launch(name):
        launch(name, functools.partial(gv_copy, name))

    width = min(512, d.users)
    per = ib // d.chunk

    def grads(t, carry):
        j = 3 - t
        rows = pl.ds(pl.multiple_of(j * ib, ib), ib)
        acc = jnp.zeros((ib, emb), F32)
        tile = lax.broadcasted_iota(jnp.int32, (ib // 8, 8, width), 0)
        for u in range(0, d.users, width):
            lanes = slice(u, u + width)
            e = expo[rows, lanes].reshape(per, d.chunk // 8, 8, width)
            e = (e * factor[pl.ds(j * per, per), :, lanes][:, None]).reshape(ib // 8, 8, width)
            hit = tile == (tile_s[:, lanes] - j * (ib // 8))[None]
            g = jnp.where(hit, e - weight_s[:, lanes][None], e).reshape(ib, width).astype(BF16)
            grad[rows, lanes] = g
            acc = acc + dot(g, users[...].reshape(d.users, emb)[lanes, :])
        gv_own[...] = acc

        @pl.when(t == 0)
        def _():
            gv_send[3] = gv_own[...].astype(BF16)
            gv_launch("gv3_lone")
            gv_launch("gv3")

        @pl.when(t == 1)
        def _():
            gv_send[2, :lone] = gv_own[:lone, :].astype(BF16)
            gv_launch("gv2_lone")
            arrive("gv3")
            gv_send[2, lone:] = (gv_own[lone:, :] + gv_recv[3, lone:, :].astype(F32)).astype(BF16)
            gv_launch("gv2")

        @pl.when(t == 2)
        def _():
            gv_send[1] = gv_own[...].astype(BF16)
            gv_launch("gv1")

        return carry

    lax.fori_loop(0, 4, grads, 0)

    us = ub // d.ng
    nfar = d.nfar
    zs = width // ub
    turns = d.users // width
    offsets = sorted(range(turns), key=lambda o: -min(o, turns - o))

    def gu_copy(k):
        return remote(gu_send.at[z_peer(k)], gu_recv.at[k], gu_s.at[k], gu_r.at[k], z_dev(k))

    def user_terms(i, carry):
        offset = functools.reduce(lambda a, t: jnp.where(i == t, offsets[t], a), range(1, turns), offsets[0])
        q = lax.rem(lax.div(z, zs) + offset, turns)
        lanes = pl.ds(pl.multiple_of(q * width, width), width)
        terms = dot(vec_t[...], grad[:, lanes]).T
        for e in range(zs):
            slot = q * zs + e
            part = terms[e * ub : (e + 1) * ub, :]

            @pl.when(slot == z)
            def _():
                gu_sum[...] = part

            k = back_by(slot, z, d.nz)
            is_near = (slot != z) & ((k < 3) | (k > d.nz - 3))

            @pl.when(is_near)
            def _():
                gu_send[slot] = part.astype(BF16)
                gu_copy(k).start()

            if nfar:

                @pl.when((k >= 3) & (k <= d.nz - 3))
                def _():
                    for g in range(d.ng):
                        gf_send[g, k - 3] = part[g * us : (g + 1) * us, :].astype(BF16)

        return carry

    def near_hops(i):
        return jnp.where(i < 3, i, i + nfar)

    def gf_copy(k):
        to = lax.rem(item + k, d.ng)
        return remote(gf_send.at[to], gf_recv.at[k], gf_s.at[k], gf_r.at[k], dev(to, xl, z, core))

    def gf2_copy(i):
        return remote(gf_sum.at[i - 1], gf2_recv.at[i - 1], f2_s.at[i], f2_r.at[i], z_dev(i + 2))

    fly("gu", d.nz - nfar, lambda i: gu_copy(near_hops(i)), start=False)
    lax.fori_loop(0, turns, user_terms, 0)
    if nfar:
        fly("gf", d.ng, gf_copy)

    for name in ("gv1", "gv3_lone", "gv2_lone", "gv2"):
        arrive(name)
    gv = gv_own[...] + gv_recv[1].astype(F32) + gv_recv[2].astype(F32)
    gv_own[...] = gv
    gv_own[:lone, :] += gv_recv[0, :lone, :].astype(F32)
    gv = gv_own[...].astype(BF16)
    gv_own[...] = gv.astype(F32)
    hc = hid // 2
    mine = pl.ds(pl.multiple_of(core * hc, hc), hc)
    other = pl.ds(pl.multiple_of((1 - core) * hc, hc), hc)

    def wc_copy(m):
        return remote(wc_send.at[m], wc_recv.at[m], wc_s.at[m], wc_r.at[m], sibling)

    pre_s[...] = (dot_t(gv, w_out[...]) * slope[...]).astype(BF16)
    wc_send[0] = dot(feats_t[...], pre_s[:, other]).astype(BF16)
    launch("wc0", functools.partial(wc_copy, 0))
    gv_t = gv_own[...].T.astype(BF16)
    wc_send[1] = dot(gv_t, hidden[:, other]).astype(BF16)
    launch("wc1", functools.partial(wc_copy, 1))
    wg_own[0] = dot(feats_t[...], pre_s[:, mine])
    wg_own[1] = dot(gv_t, hidden[:, mine])

    sr = d.srows
    half = d.np // 2

    def w1_copy(k):
        p = plane_peer(k)
        return remote(w1_send.at[p], w1_recv.at[k], w1_s.at[k], w1_r.at[k], plane_dev(p))

    fly("w1", d.np, w1_copy, start=False)
    for m in (0, 1):
        arrive(f"wc{m}")
        total = (wg_own[m] + wc_recv[m].astype(F32)).astype(BF16)
        w1_send[m * half : (m + 1) * half] = total.reshape(half, sr, hc)

        def start(k):
            p = plane_peer(k)

            @pl.when(p < half if m == 0 else p >= half)
            def _():
                w1_copy(k).start()

        each(d.np, start)

    def out_copy(i):
        pairs = [(item_v, out_item), (gu_out, out_user), (a1, out_w.at[core])]
        return pltpu.make_async_copy(*pairs[i], out_s.at[i])

    item_v[...] = gv_own[...] + dot_t(pre_s[...], w_in[...])
    out_copy(0).start()
    tails.append(lambda: out_copy(0).wait())
    tails.remove(users_sent)
    users_sent()
    sent("vecs1", "vecs2", "vecs3", "valid1", "valid2", "valid3", "st_a", "st_b")
    sent("gv1", "gv2", "gv3", "gv2_lone", "gv3_lone", "wc0", "wc1")
    if nfar:
        land("gf")
        gf_sum[...] = gf_send[item].astype(F32) + sum(gf_recv[k].astype(F32) for k in range(1, d.ng))
        fly("gf2", nfar + 1, gf2_copy)
    land("w1")
    part = w1_send[plane].astype(F32)
    for k in range(1, d.np):
        part = part + w1_recv[k].astype(F32)
    wz[z] = part.astype(BF16)

    def wz_copy(k, slot):
        return remote(wz.at[slot], wz.at[slot], wz_s.at[k], wz_r.at[k], z_dev(k))

    fly("wz", d.nz, lambda k: wz_copy(k, z), lambda k: wz_copy(k, back_by(z, k, d.nz)))

    land("gu")
    gu_sum[...] += sum(gu_recv[k].astype(F32) for k in range(1, d.nz) if k < 3 or k > d.nz - 3)

    def rows_of(i):
        return pl.ds(pl.multiple_of(i * us, us), us)

    def g2_copy(k):
        to = lax.rem(item + k, d.ng)
        return remote(gu_sum.at[rows_of(to), :], gu2_recv.at[k], g2_s.at[k], g2_r.at[k], group_dev(k))

    fly("g2", d.ng, g2_copy)
    sent("w1", "gu")
    land("wz")
    a1[plane] = sum(wz[k].astype(F32) for k in range(d.nz)).astype(BF16)

    def w4_copy(k, slot):
        there = a1.at[slot]
        return remote(there, there, w4_s.at[k], w4_r.at[k], plane_dev(plane_peer(k)))

    fly("w4", d.np, lambda k: w4_copy(k, plane), lambda k: w4_copy(k, back_by(plane, k, d.np)))

    land("g2")
    total = gu_sum[rows_of(item), :] + sum(gu2_recv[k] for k in range(1, d.ng))
    if nfar:
        land("gf2")
        total = total + sum(gf2_recv[i] for i in range(nfar))
        sent("gf", "gf2")
    gu_out[rows_of(item), :] = total

    def g3_copy(k, at):
        there = gu_out.at[rows_of(at), :]
        return remote(there, there, g3_s.at[k], g3_r.at[k], group_dev(k))

    fly("g3", d.ng, lambda k: g3_copy(k, item), lambda k: g3_copy(k, back_by(item, k, d.ng)))
    sent("wz", "g2")

    per_group = d.np // d.groups

    def w5_copy(g, of):
        slots = pl.ds(g * per_group, per_group)
        return remote(a1.at[slots], out_w.at[of, slots], w5_s.at[g], w5_r.at[g], sibling)

    for g in range(d.groups):
        for slot in range(g * per_group, (g + 1) * per_group):

            @pl.when(slot != plane)
            def _():
                w4_copy(back_by(plane, slot, d.np), slot).wait_recv()

        w5_copy(g, core).start()
    flights["w4"][3] = True
    out_copy(2).start()
    land("g3")
    out_copy(1).start()
    for g in range(d.groups):
        w5_copy(g, 1 - core).wait_recv()

    finish()
    for g in range(d.groups):
        w5_copy(g, core).wait_send()
    for i in (1, 2):
        out_copy(i).wait()


def unpack(d, user_ref, item_ref, w_ref, out_user, out_item, out_w_in, out_w_out, user_v, item_v, w_v, w_in_v, w_out_v, sems):
    half, hc = d.np // 2, d.scols
    loads = [(w_ref.at[h, m], w_v.at[h, m]) for m in (1, 0) for h in range(2)]
    loads += [(item_ref, item_v), (user_ref, user_v)]
    loads = [pltpu.make_async_copy(src, dst, sems.at[i]) for i, (src, dst) in enumerate(loads)]
    for copy in loads:
        copy.start()
    stores = [(w_out_v, out_w_out), (w_in_v, out_w_in), (item_v, out_item), (user_v, out_user)]
    stores = [pltpu.make_async_copy(src, dst, sems.at[6 + i]) for i, (src, dst) in enumerate(stores)]
    for m in (1, 0):
        for h in range(2):
            loads[2 * (1 - m) + h].wait()
            block = w_v[h, m].astype(F32).reshape(d.emb, hc)
            at = slice(h * hc, (h + 1) * hc)
            if m == 0:
                w_in_v[:, at] = block
            else:
                w_out_v[at, :] = block.T
        stores[1 - m].start()
    for i in (4, 5):
        loads[i].wait()
        stores[i - 2].start()
    for copy in stores:
        copy.wait()


def body(phys, user_vecs, row_weight, positive, item_feats, valid, w_in, w_out):
    ub, emb = user_vecs.shape
    ib, hid = item_feats.shape[0], w_in.shape[1]
    d = Dims(phys, ub, ib, emb, hid)
    vm = pltpu.VMEM
    us = ub // d.ng
    scratch = [
        vm((ib, emb), BF16),
        vm((emb, hid), BF16),
        vm((hid, emb), BF16),
        vm((ub,), BF16),
        vm((ub,), jnp.int32),
        vm((ib,), jnp.int32),
        vm((ib, emb), F32),
        vm((d.nz, ub, emb), BF16),
        vm((d.nz, 2, ub), F32),
        vm((d.nj, ib, emb), BF16),
        vm((d.nj, 1, ib), F32),
        vm((d.nj, ib, 128), F32),
        vm((emb, d.items), BF16),
        vm((ib, hid), BF16),
        vm((ib, hid), F32),
        vm((d.items, d.users), F32),
        vm((d.items, d.users), BF16),
        vm((d.nk, 8, d.users), F32),
        vm((d.nk, 8, d.users), F32),
        vm((d.nk, 8, d.users), F32),
        vm((8, d.users), jnp.int32),
        vm((1, d.users), F32),
        vm((1, d.users), F32),
        vm((d.ng, 1, d.users), F32),
        vm((1, d.users), F32),
        vm((d.nz, 1, d.users), F32),
        vm((d.nj, ib, emb), BF16),
        vm((d.nj, ib, emb), BF16),
        vm((ib, emb), F32),
        vm((d.nz, ub, emb), BF16),
        vm((d.nz, ub, emb), BF16),
        vm((ub, emb), F32),
        vm((d.ng, us, emb), F32),
        vm((ub, emb), F32),
        vm((d.ng, max(1, d.nfar), us, emb), BF16),
        vm((d.ng, max(1, d.nfar), us, emb), BF16),
        vm((max(1, d.nfar), us, emb), F32),
        vm((max(1, d.nfar), us, emb), F32),
        vm((2, emb, hid // 2), F32),
        vm((ib, hid), BF16),
        vm((emb, ib), BF16),
        vm((2, emb, hid // 2), BF16),
        vm((2, emb, hid // 2), BF16),
        vm((d.np, d.srows, d.scols), BF16),
        vm((d.np, d.srows, d.scols), BF16),
        vm((d.nz, d.srows, d.scols), BF16),
        vm((d.np, d.srows, d.scols), BF16),
    ]
    dma = pltpu.SemaphoreType.DMA
    sems = [dma((7,)), dma((4,))]
    for n in (d.nz, d.nz, d.nj, d.nj, d.ng, d.nz, 5, d.nz, d.ng, d.ng, 2, d.np, d.nz, d.np, d.groups, d.ng, d.nz):
        sems += [dma((n,)), dma((n,))]
    where = pl.BlockSpec(memory_space=pl.ANY)
    parts = pl.pallas_call(
        functools.partial(kernel, d),
        out_shape=(
            jax.ShapeDtypeStruct((ub, emb), F32),
            jax.ShapeDtypeStruct((ib, emb), F32),
            jax.ShapeDtypeStruct((2, d.np, d.srows, d.scols), BF16),
        ),
        in_specs=[where] * 7,
        out_specs=(where,) * 3,
        scratch_shapes=scratch + sems,
        compiler_params=pltpu.CompilerParams(
            collective_id=0, has_side_effects=True, vmem_limit_bytes=56 * 1024 * 1024
        ),
        cost_estimate=pl.CostEstimate(
            flops=6 * d.users * d.items * emb,
            bytes_accessed=4 * 1024 * 1024,
            transcendentals=d.users * d.items,
        ),
    )(user_vecs, row_weight, positive, item_feats, valid, w_in, w_out)
    user, item, weights = parts
    weights = weights.reshape(2, 2, d.np // 2, d.srows, d.scols)
    return pl.pallas_call(
        functools.partial(unpack, d),
        out_shape=(
            jax.ShapeDtypeStruct((ub, emb), F32),
            jax.ShapeDtypeStruct((ib, emb), F32),
            jax.ShapeDtypeStruct((emb, hid), F32),
            jax.ShapeDtypeStruct((hid, emb), F32),
        ),
        in_specs=[where] * 3,
        out_specs=(where,) * 4,
        scratch_shapes=[
            vm((ub, emb), F32),
            vm((ib, emb), F32),
            vm(weights.shape, BF16),
            vm((emb, hid), F32),
            vm((hid, emb), F32),
            dma((10,)),
        ],
    )(user, item, weights)


def build(mesh, phys):
    return jax.shard_map(
        functools.partial(body, phys),
        mesh=mesh,
        in_specs=(
            P("user", None),
            P("user"),
            P("user"),
            P(("item", "user"), None),
            P(("item", "user")),
            P(),
            P(),
        ),
        out_specs=(P("user", None), P(("item", "user"), None), P(), P()),
        check_vma=False,
    )


def solution(mesh):
    return build(mesh, (4, 2, 2, 8, 2))
```
